256 devices in a mesh: prow: 16 (over y, x), pcol: 16 (over z, core).
Axes of the slice: x: 4, y: 4, z: 8, core: 2. Of those that a mesh axis runs over, the one named last changes fastest.
Arguments:
- ginv_anc: float32 [8192, 8192], P('prow', 'pcol'), as said below
- factor_one: float32 [8192, 2048], P('prow', 'pcol'), may hold values from -0.0625 to 0.0625
- pattern_one: int32 [64, 16], replicated, may hold values from 0 to 1
- dinv_one: float32 [2048, 128], replicated
- factor_two: float32 [8192, 2048], P('prow', 'pcol'), may hold values from -0.0625 to 0.0625
- factor_parent: float32 [128, 2048], P(None, 'pcol'), may hold values from -0.5 to 0.5
- pattern_two: int32 [64, 16], replicated, may hold values from 0 to 1, as said below
- parent: int32 [16], replicated, may hold values from 0 to 15, as said below
- dinv_two: float32 [2048, 128], P('prow')
Outputs:
- anc_one: float32 [2048, 8192], P('prow', 'pcol')
- diag_one: float32 [2048, 128], P('prow')
- anc_two: float32 [2048, 8192], P('prow', 'pcol')
- cross: float32 [2048, 128], P('prow')
- diag_two: float32 [2048, 128], P('prow')
The draws below stay inside these ranges and needn't reach their ends.
Inputs may be any that keep to these rules, and one draw needn't show every extreme that they name: ginv_anc is symmetric. Each upper supernode is the parent of exactly one lower supernode. pattern_two[i, m] <= pattern_one[i, parent[m]].
All inputs are finite; a program needn't handle non-finite values.
Results may differ from the reference program's by a relative error of at most 0.000086.
Values sent between devices are 32-bit elements; how exact they have to be, the bound alone decides.
No kernel may reach another device: no remote copies, remote signals or barrier semaphores. Data moves between devices by JAX's collectives and lax.ppermute only.
A program may use at most 128 MiB of HBM per device.

```python
import math
import jax
import jax.numpy as jnp
from jax import lax

B = 128
NA = 8192
NAB = 64
NK = 16
NM = 16
NKB = 2048
NMB = 2048


def structure(key):
    first, second, third, fourth = jax.random.split(jax.random.fold_in(key, 7), 4)
    pattern_one = jax.random.randint(first, (NAB, NK), 0, 2).astype(jnp.int32)
    order = jax.random.permutation(second, NM).astype(jnp.int32)
    chosen = jax.random.randint(fourth, (), 0, NM).astype(jnp.int32)
    target = (chosen + NM // 2) % NM
    places = jnp.arange(NM, dtype=jnp.int32)
    holder = jnp.sum(places * (order == target).astype(jnp.int32)).astype(jnp.int32)
    previous = jnp.sum(order * (places == chosen).astype(jnp.int32)).astype(jnp.int32)
    parent = jnp.where(places == chosen, target, jnp.where(places == holder, previous, order)).astype(jnp.int32)
    keeper = jax.random.randint(third, (NAB, NM), 0, 4)
    pattern_two = (pattern_one[:, parent] * (keeper > 0).astype(jnp.int32)).astype(jnp.int32)
    return (pattern_one, parent, pattern_two)


def sym_blocks(key, count):
    first, second = jax.random.split(key)
    values = jax.random.normal(first, (count, B, B), jnp.float32) * (0.3 / math.sqrt(B))
    values = values + jnp.swapaxes(values, 1, 2)
    diagonal = jax.random.uniform(second, (count, B), jnp.float32, 1.0, 2.0)
    values = values + diagonal[:, :, None] * jnp.eye(B, dtype=jnp.float32)[None]
    return values.reshape(count * B, B)


def draw_ginv_anc(key, part):
    first, second = jax.random.split(jax.random.fold_in(key, 11), 2)
    values = jax.random.normal(first, (NA, NA), jnp.float32) * (0.5 / math.sqrt(NA))
    values = values + values.T
    diagonal = jax.random.uniform(second, (NA,), jnp.float32, 1.0, 2.0)
    return values + diagonal[:, None] * jnp.eye(NA, dtype=jnp.float32)


def draw_pattern_one(key, part):
    return structure(key)[0]


def draw_parent(key, part):
    return structure(key)[1]


def draw_pattern_two(key, part):
    return structure(key)[2]


def draw_dinv_one(key, part):
    return sym_blocks(jax.random.fold_in(key, 13), NK)


def draw_dinv_two(key, part):
    return sym_blocks(jax.random.fold_in(key, 17), NM)


def block_levels(stream_key, shape, pieces, smallest, top_value):
    def one(axis_at, parts):
        draws = jax.random.uniform(jax.random.fold_in(jax.random.fold_in(stream_key, 6), axis_at), (parts,), jnp.float32, smallest / len(pieces), top_value / len(pieces))
        return jnp.repeat(jnp.exp(draws), shape[axis_at] // parts).reshape((-1,) + (1,) * (len(shape) - axis_at - 1))

    gain = one(*pieces[0])
    for cut in pieces[1:]:
        gain = gain * one(*cut)
    return gain


def centred(own_key, shape, scale, most, cuts=(), kind=jnp.bfloat16):
    entries = jax.random.normal(own_key, shape, jnp.float32) * scale
    if len(cuts) > 0:
        entries = block_levels(own_key, shape, cuts, -0.22, 0.18) * entries
    return jnp.clip(entries, min=-most, max=most).astype(kind)


def setup_inputs(seed: int = 0) -> dict:
    key_list = jax.random.split(jax.random.key(seed), 10)
    ginv_anc = draw_ginv_anc(jax.random.fold_in(key_list[9], 71), 0)
    factor_one = centred(key_list[1], (NA, NKB), NA ** -0.5, 0.0625, ((0, 16), (1, 16)), jnp.float32)
    pattern_one = draw_pattern_one(jax.random.fold_in(key_list[9], 71), 0)
    dinv_one = draw_dinv_one(jax.random.fold_in(key_list[9], 71), 0)
    factor_two = centred(key_list[4], (NA, NMB), NA ** -0.5, 0.0625, ((0, 16), (1, 16)), jnp.float32)
    factor_parent = centred(key_list[5], (B, NMB), B ** -0.5, 0.5, ((1, 16),), jnp.float32)
    pattern_two = draw_pattern_two(jax.random.fold_in(key_list[9], 71), 0)
    parent = draw_parent(jax.random.fold_in(key_list[9], 71), 0)
    dinv_two = draw_dinv_two(jax.random.fold_in(key_list[9], 71), 0)
    return {"ginv_anc": ginv_anc, "factor_one": factor_one, "pattern_one": pattern_one, "dinv_one": dinv_one, "factor_two": factor_two, "factor_parent": factor_parent, "pattern_two": pattern_two, "parent": parent, "dinv_two": dinv_two}


precise = lax.Precision.HIGHEST


def expand(pattern):
    return jnp.repeat(jnp.repeat(pattern.astype(jnp.float32), B, axis=0), B, axis=1)


def reference(ginv_anc, factor_one, pattern_one, dinv_one, factor_two, factor_parent, pattern_two, parent, dinv_two):
    lower_one = factor_one * expand(pattern_one)
    anc_one = -jnp.dot(lower_one.T, ginv_anc, precision=precise, preferred_element_type=jnp.float32)
    diag_one = dinv_one - jnp.einsum("kba,akc->kbc", anc_one.reshape(NK, B, NA), lower_one.reshape(NA, NK, B), precision=precise).reshape(NKB, B)
    lower_two = factor_two * expand(pattern_two)
    par_block = factor_parent.reshape(B, NM, B)
    anc_sel = anc_one.reshape(NK, B, NA)[parent]
    diag_sel = diag_one.reshape(NK, B, B)[parent]
    direct = jnp.dot(lower_two.T, ginv_anc, precision=precise, preferred_element_type=jnp.float32)
    anc_two = -(direct + jnp.einsum("kmj,mka->mja", par_block, anc_sel, precision=precise).reshape(NMB, NA))
    lower_three = lower_two.reshape(NA, NM, B)
    cross = -(jnp.einsum("amj,mka->mjk", lower_three, anc_sel, precision=precise) + jnp.einsum("kmj,mkc->mjc", par_block, diag_sel, precision=precise))
    inner = jnp.einsum("mja,amc->mjc", anc_two.reshape(NM, B, NA), lower_three, precision=precise)
    diag_two = dinv_two - (inner + jnp.einsum("mjk,kmc->mjc", cross, par_block, precision=precise)).reshape(NMB, B)
    return anc_one, diag_one, anc_two, cross.reshape(NMB, B), diag_two
```

```python
import functools

import jax
import jax.numpy as jnp
from jax import lax
from jax.experimental import pallas as pl
from jax.experimental.pallas import tpu as pltpu
from jax.sharding import PartitionSpec as P

ROWS = 16
COLS = 16
B = 128
KA = 512
PACK = 288
MASKS = ((1, 3, 4, 12), (3, 1, 12, 4), (4, 12, 1, 3), (12, 4, 3, 1))
precise = lax.Precision.HIGHEST


def slot_mask(variant, slot):
    mask = 0
    for bit in range(4):
        if (slot >> (3 - bit)) & 1:
            mask ^= MASKS[variant][bit]
    return mask


def split(value):
    high = value.astype(jnp.bfloat16)
    low = (value - high.astype(jnp.float32)).astype(jnp.bfloat16)
    return high, low


def dot_split(left, right, dims):
    out = None
    for a, b in ((left[0], right[0]), (left[0], right[1]), (left[1], right[0])):
        term = lax.dot_general(a, b, (dims, ((), ())), preferred_element_type=jnp.float32)
        out = term if out is None else out + term
    return out


def product_kernel(scal_ref, all_ref, ginv_ref, *refs):
    sends = refs[0:4]
    keeps = refs[4:8]
    cross_ref = refs[8]
    two_ref, left_ref = refs[9:]
    row = scal_ref[16]
    target = scal_ref[17]
    ginv = split(ginv_ref[...])

    def correct(m, carry):
        packed = all_ref[m, 256:288, :]
        par = jnp.concatenate([packed[:, 128 * i : 128 * i + 128] for i in range(4)], axis=0)
        one = all_ref[scal_ref[m], 0:128, :]
        fix = dot_split(split(par), split(one), ((1,), (0,)))
        two_ref[m] = all_ref[m, 128:256, :] - fix
        return carry

    lax.fori_loop(0, 16, correct, 0)
    cross_ref[0:128, :] = all_ref[scal_ref[target], 0:128, :]
    cross_ref[128:384, :] = all_ref[target, 0:256, :]
    for variant in range(4):
        lo = 32 * variant
        for half in (1, 0):
            for slot in range(8):
                dest = row ^ slot_mask(variant, slot + 8 * half)
                left_ref[64 * slot : 64 * slot + 32, :] = all_ref[dest, lo : lo + 32, :]
                left_ref[64 * slot + 32 : 64 * slot + 64, :] = two_ref[dest, lo : lo + 32, :]
            value = dot_split(split(left_ref[...]), ginv, ((1,), (0,)))
            out = sends[variant] if half else keeps[variant]
            out[...] = -value.reshape(8, 64, KA)


def products(scalars, gathered, ginv):
    part = jax.ShapeDtypeStruct((8, 64, KA), jnp.float32)
    vmem = pl.BlockSpec(memory_space=pltpu.VMEM)
    return pl.pallas_call(
        product_kernel,
        out_shape=[part] * 8 + [jax.ShapeDtypeStruct((384, KA), jnp.float32)],
        in_specs=[pl.BlockSpec(memory_space=pltpu.SMEM), vmem, vmem],
        out_specs=[vmem] * 9,
        scratch_shapes=[
            pltpu.VMEM((16, 128, KA), jnp.float32),
            pltpu.VMEM((512, KA), jnp.float32),
        ],
        compiler_params=pltpu.CompilerParams(vmem_limit_bytes=48 * 1024 * 1024),
        cost_estimate=pl.CostEstimate(
            flops=8_000_000_000, bytes_accessed=20_000_000, transcendentals=0
        ),
    )(scalars, gathered, ginv)


def block_kernel(a_ref, b_ref, c_ref, d_ref, swap_ref, one_ref, two_ref, sums_ref):
    for variant, ref in enumerate((a_ref, b_ref, c_ref, d_ref)):
        one_ref[32 * variant : 32 * variant + 32, :] = ref[0:32, :]
        two_ref[32 * variant : 32 * variant + 32, :] = ref[32:64, :]
    one = split(one_ref[...])
    two = split(two_ref[...])
    nt = ((1,), (1,))
    sums_ref[0] = dot_split(one, split(swap_ref[128:256, :]), nt)
    sums_ref[1] = dot_split(two, split(swap_ref[0:128, :]), nt)
    sums_ref[2] = dot_split(two, split(swap_ref[256:384, :]), nt)


def blocks(parts, swapped):
    vmem = pl.BlockSpec(memory_space=pltpu.VMEM)
    return pl.pallas_call(
        block_kernel,
        out_shape=[
            jax.ShapeDtypeStruct((128, KA), jnp.float32),
            jax.ShapeDtypeStruct((128, KA), jnp.float32),
            jax.ShapeDtypeStruct((3, 128, 128), jnp.float32),
        ],
        in_specs=[vmem] * 5,
        out_specs=[vmem] * 3,
        compiler_params=pltpu.CompilerParams(vmem_limit_bytes=24 * 1024 * 1024),
    )(*parts, swapped)


def reduce_rows(sends, keeps):
    parts = list(keeps)
    going = list(sends)
    for step in range(4):
        got = [
            lax.ppermute(
                going[v], "prow", [(r, r ^ MASKS[v][step]) for r in range(ROWS)]
            )
            for v in range(4)
        ]
        half = parts[0].shape[0] // 2
        if step < 3:
            going = [parts[v][half:] + got[v][half:] for v in range(4)]
            parts = [parts[v][:half] + got[v][:half] for v in range(4)]
        else:
            parts = [(parts[v] + got[v])[0] for v in range(4)]
    return parts


def sum_cols(values):
    for mask in (1, 2, 6, 8):
        values = values + lax.ppermute(values, "pcol", [(c, c ^ mask) for c in range(COLS)])
    return values


def masked_turn(factor, pattern, row, col):
    blocks_per = KA // B
    picks = lax.dynamic_slice(pattern, (row * blocks_per, col), (blocks_per, 1))
    mask = jnp.repeat(picks[:, 0].astype(jnp.float32), B)
    return factor.T * mask[None, :]


def local(
    ginv_anc,
    factor_one,
    pattern_one,
    dinv_one,
    factor_two,
    factor_parent,
    pattern_two,
    parent,
    dinv_two,
):
    row = lax.axis_index("prow")
    col = lax.axis_index("pcol")
    one = masked_turn(factor_one, pattern_one, row, col)
    two = masked_turn(factor_two, pattern_two, row, col)
    par = factor_parent.T
    packed = jnp.concatenate([par[32 * i : 32 * i + 32] for i in range(4)], axis=1)
    own = jnp.concatenate([one, two, packed], axis=0)
    gathered = lax.all_gather(own, "pcol", axis=0, tiled=False)
    scalars = jnp.concatenate(
        [parent, jnp.stack([row, row ^ col]).astype(jnp.int32)]
    )
    outs = products(scalars, gathered, ginv_anc)
    swapped = lax.ppermute(
        outs[8],
        ("prow", "pcol"),
        [(c * COLS + q, (c ^ q) * COLS + c) for c in range(ROWS) for q in range(COLS)],
    )
    parts = reduce_rows(outs[0:4], outs[4:8])
    anc_one, anc_two, part = blocks(parts, swapped)
    sums = sum_cols(part)
    own_pack = lax.dynamic_index_in_dim(gathered, row, 0, keepdims=False)[256:288]
    own_par = jnp.concatenate([own_pack[:, 128 * i : 128 * i + 128] for i in range(4)], axis=0)
    own_parent = lax.dynamic_index_in_dim(parent, row, 0, keepdims=False)
    one_dinv = lax.dynamic_slice_in_dim(dinv_one, row * B, B, 0)
    par_dinv = lax.dynamic_slice_in_dim(dinv_one, own_parent * B, B, 0)
    diag_one = one_dinv - sums[0]
    cross = -(sums[1] + jnp.dot(own_par, par_dinv, precision=precise))
    diag_two = dinv_two - (
        sums[2]
        + lax.dot_general(cross, own_par, (((1,), (1,)), ((), ())), precision=precise)
    )
    return anc_one, diag_one, anc_two, cross, diag_two


def solution(mesh):
    return jax.shard_map(
        local,
        mesh=mesh,
        in_specs=(
            P("prow", "pcol"),
            P("prow", "pcol"),
            P(),
            P(),
            P("prow", "pcol"),
            P(None, "pcol"),
            P(),
            P(),
            P("prow", None),
        ),
        out_specs=(
            P("prow", "pcol"),
            P("prow", None),
            P("prow", "pcol"),
            P("prow", None),
            P("prow", None),
        ),
        check_vma=False,
    )
```

```python
import jax
import jax.numpy as jnp
from jax import lax
from jax.experimental import pallas as pl
from jax.experimental.pallas import tpu as pltpu
from jax.sharding import PartitionSpec as P

N = 16
B = 128
KA = 512
ALL = ("prow", "pcol")
MASKS = (((1, 3, 4, 12), (3, 1, 12, 4)), ((4, 12, 1, 3), (12, 4, 3, 1)))
VMEM = pl.BlockSpec(memory_space=pltpu.VMEM)
SMEM = pl.BlockSpec(memory_space=pltpu.SMEM)
ANY = pl.BlockSpec(memory_space=pl.ANY)
MIB = 1024 * 1024


def f32(*shape):
    return jax.ShapeDtypeStruct(shape, jnp.float32)


def slot_mask(core, variant, slot):
    mask = 0
    for bit in range(4):
        if (slot >> (3 - bit)) & 1:
            mask ^= MASKS[core][variant][bit]
    return mask


def destination(row, core, variant, slot):
    first, second = slot_mask(0, variant, slot), slot_mask(1, variant, slot)
    return row ^ jnp.where(core == 0, first, second)


def split(value):
    high = value.astype(jnp.bfloat16)
    low = (value - high.astype(jnp.float32)).astype(jnp.bfloat16)
    return high, low


def dot_split(left, right, dims):
    out = None
    for a, b in ((left[0], right[0]), (left[0], right[1]), (left[1], right[0])):
        term = lax.dot_general(a, b, (dims, ((), ())), preferred_element_type=jnp.float32)
        out = term if out is None else out + term
    return out


def unpack(packed):
    return jnp.concatenate([packed[:, B * i : B * i + B] for i in range(4)], axis=0)


def permute(value, move):
    pairs = []
    for r in range(N):
        for c in range(N):
            nr, nc = move(r, c)
            pairs.append((r * N + c, nr * N + nc))
    return lax.ppermute(value, ALL, pairs)


def swap(value):
    return permute(value, lambda r, c: (r, c ^ 1))


def ring(value):
    return permute(value, lambda r, c: (r, (c + (2 if c % 2 == 0 else -2)) % N))


def prep_kernel(scal, pat_one, pat_two, fac_one, fac_two, par, one_out, two_out):
    row, col = scal[16], scal[17]
    turned = par[...].T
    for i in range(4):
        cut = pl.ds(B * i, B)
        w_one = pat_one[4 * row + i, col].astype(jnp.float32)
        w_two = pat_two[4 * row + i, col].astype(jnp.float32)
        one_out[:, cut] = fac_one[cut, :].T * w_one
        two_out[0:128, cut] = fac_two[cut, :].T * w_two
        two_out[128:160, cut] = turned[32 * i : 32 * i + 32, :]


def prepare(scal, pat_one, pat_two, fac_one, fac_two, par):
    return pl.pallas_call(
        prep_kernel,
        out_shape=[f32(B, KA), f32(160, KA)],
        in_specs=[SMEM] * 3 + [VMEM] * 3,
        out_specs=[VMEM] * 2,
        compiler_params=pltpu.CompilerParams(vmem_limit_bytes=8 * MIB),
    )(scal, pat_one, pat_two, fac_one, fac_two, par)


def gather(own):
    pair = jnp.stack([own, swap(own)])
    blocks = [pair]
    going = pair
    for step in range(4):
        if step == 3:
            going = going[0:1]
        going = ring(going)
        blocks += [going, swap(going)]
    return blocks


def fetch(scal, refs, target, sems):
    col = scal[17]
    z, core = col // 2, lax.rem(col, 2)
    copies = []
    for at, ref in enumerate(refs):
        step = (at + 1) // 2
        swapped = at > 0 and at % 2 == 0
        side = (1 - core) if swapped else core
        away = jnp.where(side == 0, 8 - step, step)
        plane = lax.rem(z + away, 8)
        for i in range(ref.shape[0]):
            parity = side if i == 0 else 1 - side
            copies.append(
                pltpu.make_async_copy(
                    ref.at[i], target.at[plane * 2 + parity], sems.at[len(copies)]
                )
            )
    return copies


def one_kernel(scal, ginv, *refs):
    blocks, refs = refs[:9], refs[9:]
    sends, keeps, one, turn, left, sems = refs[0:2], refs[2:4], refs[4], refs[5], refs[6], refs[7]
    row, col, target = scal[16], scal[17], scal[18]
    core = lax.rem(col, 2)
    copies = fetch(scal, blocks, one, sems)
    for copy in copies:
        copy.start()
    high, low = split(ginv[...])
    for copy in copies:
        copy.wait()
    turn[0:128, :] = one[scal[target]]
    turn[128:256, :] = one[target]
    for variant in range(2):
        for half in (1, 0):
            for slot in range(8):
                dest = destination(row, core, variant, slot + 8 * half)
                left[64 * slot : 64 * slot + 64, :] = one[dest, 64 * variant : 64 * variant + 64, :]
            value = dot_split(split(left[...]), (high, low), ((1,), (0,)))
            out = sends[variant] if half else keeps[variant]
            out[...] = -value.reshape(8, 64, KA)


def first_level(scal, ginv, blocks):
    return pl.pallas_call(
        one_kernel,
        out_shape=[f32(8, 64, KA)] * 4 + [f32(16, B, KA), f32(256, KA)],
        in_specs=[SMEM, VMEM] + [ANY] * 9,
        out_specs=[VMEM] * 6,
        scratch_shapes=[pltpu.VMEM((512, KA), jnp.float32), pltpu.SemaphoreType.DMA((16,))],
        compiler_params=pltpu.CompilerParams(vmem_limit_bytes=32 * MIB),
        cost_estimate=pl.CostEstimate(
            flops=4_000_000_000, bytes_accessed=14_000_000, transcendentals=0
        ),
    )(scal, ginv, *blocks)


def two_kernel(half, scal, ginv, one, *refs):
    blocks, refs = refs[:9], refs[9:]
    outs, turn, two, left, sems = refs[0:2], refs[2], refs[3], refs[4], refs[5]
    row, col, target = scal[16], scal[17], scal[18]
    core = lax.rem(col, 2)
    copies = fetch(scal, blocks, two, sems)
    for copy in copies:
        copy.start()
    high, low = split(ginv[...])
    for copy in copies:
        copy.wait()
    if half:
        turn[...] = two[target, 0:128, :]
    else:
        turn[...] = unpack(two[row, 128:160, :])
    for variant in range(2):
        lo = 64 * variant

        def correct(slot, carry):
            dest = row ^ scal[32 + 32 * core + 16 * variant + 8 * half + slot]
            par = unpack(two[dest, 128:160, :])[lo : lo + 64, :]
            fix = dot_split(split(par), split(one[scal[dest]]), ((1,), (0,)))
            at = pl.multiple_of(slot * 64, 64)
            left[pl.ds(at, 64), :] = two[dest, lo : lo + 64, :] - fix
            return carry

        lax.fori_loop(0, 8, correct, 0)
        value = dot_split(split(left[...]), (high, low), ((1,), (0,)))
        outs[variant][...] = -value.reshape(8, 64, KA)


def second_level(half, scal, ginv, one, blocks):
    def body(*refs):
        two_kernel(half, *refs)

    return pl.pallas_call(
        body,
        out_shape=[f32(8, 64, KA)] * 2 + [f32(128, KA) if half else f32(128, 128)],
        in_specs=[SMEM, VMEM, VMEM] + [ANY] * 9,
        out_specs=[VMEM] * 3,
        scratch_shapes=[
            pltpu.VMEM((16, 160, KA), jnp.float32),
            pltpu.VMEM((512, KA), jnp.float32),
            pltpu.SemaphoreType.DMA((16,)),
        ],
        compiler_params=pltpu.CompilerParams(vmem_limit_bytes=32 * MIB),
        cost_estimate=pl.CostEstimate(
            flops=3_000_000_000, bytes_accessed=10_000_000, transcendentals=0
        ),
    )(scal, ginv, one, *blocks)


def row_step(value, variant, step):
    return permute(value, lambda r, c: (r ^ MASKS[c % 2][variant][step], c))


def block_kernel(scal, a_ref, b_ref, turn_one, turn_two, one_out, two_out, send_out, keep_out, sums):
    core = lax.rem(scal[17], 2)
    for variant, ref in enumerate((a_ref, b_ref)):
        one_out[64 * variant : 64 * variant + 64, :] = ref[0:64, :]
        two_out[64 * variant : 64 * variant + 64, :] = ref[64:128, :]
    one = split(one_out[...])
    two = split(two_out[...])
    nt = ((1,), (1,))
    for i, (left, right) in enumerate(
        ((one, turn_one[128:256, :]), (two, turn_one[0:128, :]), (two, turn_two[...]))
    ):
        value = dot_split(left, split(right), nt)
        sums[0, 64 * i : 64 * i + 64, :] = value[0:64]
        sums[1, 64 * i : 64 * i + 64, :] = value[64:128]
    keep_out[...] = sums[core]
    send_out[...] = sums[1 - core]


def blocks_of(scal, parts, turn_one, turn_two):
    return pl.pallas_call(
        block_kernel,
        out_shape=[f32(B, KA), f32(B, KA), f32(192, B), f32(192, B)],
        in_specs=[SMEM] + [VMEM] * 4,
        out_specs=[VMEM] * 4,
        scratch_shapes=[pltpu.VMEM((2, 192, B), jnp.float32)],
        compiler_params=pltpu.CompilerParams(vmem_limit_bytes=8 * MIB),
    )(scal, *parts, turn_one, turn_two)


def base_kernel(scal, par, dinv_one, dinv_two, base):
    row, col = scal[16], scal[17]
    top = pl.multiple_of(lax.rem(col, 2) * 64, 64)
    at = pl.multiple_of(row * B, B)
    up = pl.multiple_of(scal[row] * B, B)
    base[0:64, :] = dinv_one[pl.ds(at + top, 64), :]
    base[64:128, :] = -jnp.dot(
        par[pl.ds(top, 64), :],
        dinv_one[pl.ds(up, B), :],
        precision=lax.Precision.HIGHEST,
        preferred_element_type=jnp.float32,
    )
    base[128:192, :] = dinv_two[pl.ds(top, 64), :]


def base_of(scal, par, dinv_one, dinv_two):
    return pl.pallas_call(
        base_kernel,
        out_shape=f32(192, B),
        in_specs=[SMEM] + [VMEM] * 3,
        out_specs=VMEM,
        compiler_params=pltpu.CompilerParams(vmem_limit_bytes=8 * MIB),
    )(scal, par, dinv_one, dinv_two)


def final_kernel(base, par, first, second, out):
    total = first[...] + second[...]
    out[0:64, :] = base[0:64, :] - total[0:64, :]
    cross = base[64:128, :] - total[64:128, :]
    out[64:128, :] = cross
    out[128:192, :] = base[128:192, :] - (
        total[128:192, :]
        + lax.dot_general(
            cross,
            par[...],
            (((1,), (1,)), ((), ())),
            precision=lax.Precision.HIGHEST,
            preferred_element_type=jnp.float32,
        )
    )


def final_of(base, par, first, second):
    return pl.pallas_call(
        final_kernel,
        out_shape=f32(192, B),
        in_specs=[VMEM] * 4,
        out_specs=VMEM,
        compiler_params=pltpu.CompilerParams(vmem_limit_bytes=4 * MIB),
    )(base, par, first, second)


def join_kernel(scal, own, other, a_out, b_out, c_out):
    core = lax.rem(scal[17], 2)
    mine = pl.multiple_of(core * 64, 64)
    rest = pl.multiple_of((1 - core) * 64, 64)
    for i, out in enumerate((a_out, b_out, c_out)):
        out[pl.ds(mine, 64), :] = own[64 * i : 64 * i + 64, :]
        out[pl.ds(rest, 64), :] = other[64 * i : 64 * i + 64, :]


def join(scal, own, other):
    return pl.pallas_call(
        join_kernel,
        out_shape=[f32(B, B)] * 3,
        in_specs=[SMEM] + [VMEM] * 2,
        out_specs=[VMEM] * 3,
        compiler_params=pltpu.CompilerParams(vmem_limit_bytes=4 * MIB),
    )(scal, own, other)


def local(
    ginv_anc,
    factor_one,
    pattern_one,
    dinv_one,
    factor_two,
    factor_parent,
    pattern_two,
    parent,
    dinv_two,
):
    row = lax.axis_index("prow")
    col = lax.axis_index("pcol")
    table = [slot_mask(c, v, s) for c in range(2) for v in range(2) for s in range(16)]
    place = jnp.stack([row, col, lax.rem(row + col, N)]).astype(jnp.int32)
    scal = jnp.concatenate(
        [parent, place, jnp.zeros((13,), jnp.int32), jnp.array(table, jnp.int32)]
    )
    own_one, own_two = prepare(
        scal, pattern_one, pattern_two, factor_one, factor_two, factor_parent
    )
    blocks_one = gather(own_one)
    blocks_two = gather(own_two)
    s1a, s1b, k1a, k1b, one, turn_one = first_level(scal, ginv_anc, blocks_one)
    s2a, s2b, turn_two = second_level(1, scal, ginv_anc, one, blocks_two)
    k2a, k2b, par = second_level(0, scal, ginv_anc, one, blocks_two)
    base = base_of(scal, par, dinv_one, dinv_two)

    def spread(value):
        value = permute(value, lambda r, c: ((r + c) % N, c))
        return permute(value, lambda r, c: (r, (r - c) % N))

    turn_one = spread(turn_one)
    turn_two = spread(turn_two)
    first = [[k1a, row_step(s1a, 0, 0)], [k1b, row_step(s1b, 1, 0)]]
    second = [[k2a, row_step(s2a, 0, 0)], [k2b, row_step(s2b, 1, 0)]]
    going, kept = [], []
    for v in range(2):
        going.append(
            jnp.concatenate([first[v][0][4:] + first[v][1][4:], second[v][0][4:] + second[v][1][4:]], axis=1)
        )
        kept.append(
            jnp.concatenate([first[v][0][:4] + first[v][1][:4], second[v][0][:4] + second[v][1][:4]], axis=1)
        )
    for step in range(1, 4):
        got = [row_step(going[v], v, step) for v in range(2)]
        half = kept[0].shape[0] // 2
        if step < 3:
            going = [kept[v][half:] + got[v][half:] for v in range(2)]
            kept = [kept[v][:half] + got[v][:half] for v in range(2)]
        else:
            kept = [(kept[v] + got[v])[0] for v in range(2)]
    anc_one, anc_two, send, keep = blocks_of(scal, kept, turn_one, turn_two)
    sums = keep + swap(send)
    for mask in (2, 6):
        sums = sums + permute(sums, lambda r, c: (r, c ^ mask))
    done = final_of(base, par, sums, permute(sums, lambda r, c: (r, c ^ 8)))
    diag_one, cross, diag_two = join(scal, done, swap(done))
    return anc_one, diag_one, anc_two, cross, diag_two


def solution(mesh):
    return jax.shard_map(
        local,
        mesh=mesh,
        in_specs=(
            P("prow", "pcol"),
            P("prow", "pcol"),
            P(),
            P(),
            P("prow", "pcol"),
            P(None, "pcol"),
            P(),
            P(),
            P("prow", None),
        ),
        out_specs=(
            P("prow", "pcol"),
            P("prow", None),
            P("prow", "pcol"),
            P("prow", None),
            P("prow", None),
        ),
        check_vma=False,
    )
```

```python
import jax
import jax.numpy as jnp
from jax import lax
from jax.experimental import pallas as pl
from jax.experimental.pallas import tpu as pltpu
from jax.sharding import PartitionSpec as P

N = 16
B = 128
KA = 512
ALL = ("prow", "pcol")
MASKS = (((1, 3, 4, 12), (3, 1, 12, 4)), ((4, 12, 1, 3), (12, 4, 3, 1)))
LAG = 1
SPREAD = (1, 6, 2)
VMEM = pl.BlockSpec(memory_space=pltpu.VMEM)
SMEM = pl.BlockSpec(memory_space=pltpu.SMEM)
ANY = pl.BlockSpec(memory_space=pl.ANY)
HBM = pl.BlockSpec(memory_space=pltpu.HBM)
MIB = 1024 * 1024


def f32(*shape):
    return jax.ShapeDtypeStruct(shape, jnp.float32)


def slot_mask(core, variant, slot):
    mask = 0
    for bit in range(4):
        if (slot >> (3 - bit)) & 1:
            mask ^= MASKS[core][variant][bit]
    return mask


def destination(row, core, variant, slot):
    first, second = slot_mask(0, variant, slot), slot_mask(1, variant, slot)
    return row ^ jnp.where(core == 0, first, second)


def split(value):
    high = value.astype(jnp.bfloat16)
    low = (value - high.astype(jnp.float32)).astype(jnp.bfloat16)
    return high, low


def dot_split(left, right, dims):
    out = None
    for a, b in ((left[0], right[0]), (left[0], right[1]), (left[1], right[0])):
        term = lax.dot_general(a, b, (dims, ((), ())), preferred_element_type=jnp.float32)
        out = term if out is None else out + term
    return out


def unpack(packed):
    return jnp.concatenate([packed[:, B * i : B * i + B] for i in range(4)], axis=0)


def permute(value, move):
    pairs = []
    for r in range(N):
        for c in range(N):
            nr, nc = move(r, c)
            pairs.append((r * N + c, nr * N + nc))
    return lax.ppermute(value, ALL, pairs)


def swap(value):
    return permute(value, lambda r, c: (r, c ^ 1))


def ring(value):
    return permute(value, lambda r, c: (r, (c + (2 if c % 2 == 0 else -2)) % N))


def spread_mask(col):
    mask = 10 if col % 2 else 0
    for bit, part in enumerate(SPREAD):
        if ((col // 2) >> bit) & 1:
            mask ^= part
    return mask


def prep_kernel(pattern, factor, *refs):
    if len(refs) > 4:
        par, out, staged, par_in, sems = refs
        pltpu.make_async_copy(par, par_in, sems.at[4]).start()
    else:
        _, out, staged, sems = refs
    row, col = lax.axis_index("prow"), lax.axis_index("pcol")
    copies = []
    for i in range(4):
        cut = pl.ds(B * i, B)
        copies.append(pltpu.make_async_copy(factor.at[cut], staged.at[cut], sems.at[i]))
        copies[i].start()
    for i in range(4):
        cut = pl.ds(B * i, B)
        weight = pattern[4 * row + i, col].astype(jnp.float32)
        copies[i].wait()
        out[0:128, cut] = staged[cut, :].T * weight
    if len(refs) > 4:
        pltpu.make_async_copy(par, par_in, sems.at[4]).wait()
        turned = par_in[...].T
        for i in range(4):
            out[128:160, B * i : B * i + B] = turned[32 * i : 32 * i + 32, :]


def prepare(pattern, factor, extra, rows):
    scratch = [pltpu.VMEM((KA, B), jnp.float32)]
    if rows > B:
        scratch.append(pltpu.VMEM((B, B), jnp.float32))
    return pl.pallas_call(
        prep_kernel,
        out_shape=f32(rows, KA),
        in_specs=[SMEM, HBM, HBM if rows > B else ANY],
        out_specs=VMEM,
        scratch_shapes=scratch + [pltpu.SemaphoreType.DMA((5,))],
        compiler_params=pltpu.CompilerParams(vmem_limit_bytes=(60 if rows > B else 4) * MIB),
    )(pattern, factor, extra)


def pair_up(own):
    return jnp.stack([own, swap(own)])


def gather(pair):
    blocks = [pair]
    going = pair
    for step in range(4):
        if step == 3:
            going = going[0:1]
        going = ring(going)
        blocks += [going, swap(going)]
    return blocks


def place():
    row, col = lax.axis_index("prow"), lax.axis_index("pcol")
    core = lax.rem(col, 2)
    z = lax.div(col, 2)
    target = row ^ (core * 10)
    for bit, mask in enumerate(SPREAD):
        target = target ^ (lax.rem(lax.shift_right_logical(z, bit), 2) * mask)
    return row, col, core, target


def fetch(refs, target, sems):
    col = lax.axis_index("pcol")
    z, core = lax.div(col, 2), lax.rem(col, 2)
    copies = []
    for at, ref in enumerate(refs):
        step = (at + 1) // 2
        swapped = at > 0 and at % 2 == 0
        side = (1 - core) if swapped else core
        away = jnp.where(side == 0, 8 - step, step)
        plane = lax.rem(z + away, 8)
        for i in range(ref.shape[0]):
            parity = side if i == 0 else 1 - side
            copies.append(
                pltpu.make_async_copy(
                    ref.at[i], target.at[plane * 2 + parity], sems.at[len(copies)]
                )
            )
    return copies


def one_kernel(parent, ginv, *refs):
    blocks, refs = refs[:9], refs[9:]
    sends, keeps, one, turn, left, sems = (
        refs[0:2], refs[2:4], refs[4], refs[5], refs[6], refs[7],
    )
    row, col, core, target = place()
    copies = fetch(blocks, one, sems)
    for copy in copies:
        copy.start()
    high, low = split(ginv[...])
    for copy in copies:
        copy.wait()
    turn[0:128, :] = one[parent[target], 0:128, :]
    turn[128:256, :] = one[target, 0:128, :]
    for variant in range(2):
        for half in (1, 0):
            for slot in range(8):
                dest = destination(row, core, variant, slot + 8 * half)
                left[64 * slot : 64 * slot + 64, :] = one[dest, 64 * variant : 64 * variant + 64, :]
            value = dot_split(split(left[...]), (high, low), ((1,), (0,)))
            out = sends[variant] if half else keeps[variant]
            out[...] = -value.reshape(8, 64, KA)


def first_level(parent, ginv, blocks):
    return pl.pallas_call(
        one_kernel,
        out_shape=[f32(8, 64, KA)] * 4 + [f32(16, 160, KA), f32(256, KA)],
        in_specs=[SMEM, VMEM] + [ANY] * 9,
        out_specs=[VMEM] * 6,
        scratch_shapes=[pltpu.VMEM((512, KA), jnp.float32), pltpu.SemaphoreType.DMA((16,))],
        compiler_params=pltpu.CompilerParams(vmem_limit_bytes=20 * MIB),
        cost_estimate=pl.CostEstimate(
            flops=4_000_000_000, bytes_accessed=1_000_000, transcendentals=0
        ),
    )(parent, ginv, *blocks)


def fix_kernel(parent, one, dinv_one, dinv_two, fix, par_out, base, dinv, sems):
    row, col, core, target = place()
    top = pl.multiple_of(core * 64, 64)
    sources = (
        dinv_one.at[pl.ds(pl.multiple_of(row * B, B), B)],
        dinv_one.at[pl.ds(pl.multiple_of(parent[row] * B, B), B)],
        dinv_two,
    )
    copies = [
        pltpu.make_async_copy(source, dinv.at[i], sems.at[i]) for i, source in enumerate(sources)
    ]
    for copy in copies:
        copy.start()

    def correct(m, carry):
        par = unpack(one[m, 128:160, :])
        fix[m] = dot_split(split(par), split(one[parent[m], 0:128, :]), ((1,), (0,)))
        return carry

    lax.fori_loop(0, 16, correct, 0)
    par_out[...] = unpack(one[row, 128:160, :])
    for copy in copies:
        copy.wait()
    base[0:64, :] = dinv[0, pl.ds(top, 64), :]
    base[64:128, :] = -jnp.dot(
        par_out[pl.ds(top, 64), :],
        dinv[1],
        precision=lax.Precision.HIGHEST,
        preferred_element_type=jnp.float32,
    )
    base[128:192, :] = dinv[2, pl.ds(top, 64), :]


def corrections(parent, one, dinv_one, dinv_two):
    return pl.pallas_call(
        fix_kernel,
        out_shape=[f32(16, B, KA), f32(B, B), f32(192, B)],
        in_specs=[SMEM, VMEM, HBM, HBM],
        out_specs=[VMEM] * 3,
        scratch_shapes=[pltpu.VMEM((3, B, B), jnp.float32), pltpu.SemaphoreType.DMA((3,))],
        compiler_params=pltpu.CompilerParams(vmem_limit_bytes=14 * MIB),
        cost_estimate=pl.CostEstimate(
            flops=4_000_000_000, bytes_accessed=1_000_000, transcendentals=0
        ),
    )(parent, one, dinv_one, dinv_two)


def two_kernel(half, waits, ginv, fix, *refs):
    blocks, refs = refs[:9], refs[9 + waits :]
    outs, refs = refs[0:2], refs[2:]
    two, left, sems = refs[-3:]
    row, col, core, target = place()
    copies = fetch(blocks, two, sems)
    for copy in copies:
        copy.start()
    high, low = split(ginv[...])
    for copy in copies:
        copy.wait()
    if half:
        refs[0][...] = two[target]
    for variant in range(2):
        for slot in range(8):
            dest = destination(row, core, variant, slot + 8 * half)
            rows = pl.ds(64 * variant, 64)
            left[64 * slot : 64 * slot + 64, :] = two[dest, rows, :] - fix[dest, rows, :]
        value = dot_split(split(left[...]), (high, low), ((1,), (0,)))
        outs[variant][...] = -value.reshape(8, 64, KA)


def second_level(half, ginv, fix, blocks, order):
    def body(*refs):
        two_kernel(half, len(order), *refs)

    return pl.pallas_call(
        body,
        out_shape=[f32(8, 64, KA)] * 2 + ([f32(128, KA)] if half else []),
        in_specs=[VMEM, VMEM] + [ANY] * (9 + len(order)),
        out_specs=[VMEM] * (2 + half),
        scratch_shapes=[
            pltpu.VMEM((16, B, KA), jnp.float32),
            pltpu.VMEM((512, KA), jnp.float32),
            pltpu.SemaphoreType.DMA((16,)),
        ],
        compiler_params=pltpu.CompilerParams(vmem_limit_bytes=16 * MIB),
        cost_estimate=pl.CostEstimate(
            flops=1_500_000_000, bytes_accessed=8_000_000, transcendentals=0
        ),
    )(ginv, fix, *blocks, *order)


def merge(part, keep_one, got_one, keep_two, got_two):
    def body(a, b, c, d, out):
        for i in range(4):
            out[i, 0:64, :] = a[4 * part + i] + b[4 * part + i]
            out[i, 64:128, :] = c[4 * part + i] + d[4 * part + i]

    return pl.pallas_call(
        body,
        out_shape=f32(4, B, KA),
        in_specs=[VMEM] * 4,
        out_specs=VMEM,
        compiler_params=pltpu.CompilerParams(vmem_limit_bytes=10 * MIB),
        cost_estimate=pl.CostEstimate(flops=300_000, bytes_accessed=3_000_000, transcendentals=0),
    )(keep_one, got_one, keep_two, got_two)


def row_step(value, variant, step):
    return permute(value, lambda r, c: (r ^ MASKS[c % 2][variant][step], c))


def block_kernel(a_ref, b_ref, turn_one, turn_two, one_out, two_out, send_out, keep_out, sums):
    core = lax.rem(lax.axis_index("pcol"), 2)
    for variant, ref in enumerate((a_ref, b_ref)):
        one_out[64 * variant : 64 * variant + 64, :] = ref[0:64, :]
        two_out[64 * variant : 64 * variant + 64, :] = ref[64:128, :]
    one = split(one_out[...])
    two = split(two_out[...])
    nt = ((1,), (1,))
    for i, (left, right) in enumerate(
        ((one, turn_one[128:256, :]), (two, turn_one[0:128, :]), (two, turn_two[...]))
    ):
        value = dot_split(left, split(right), nt)
        sums[0, 64 * i : 64 * i + 64, :] = value[0:64]
        sums[1, 64 * i : 64 * i + 64, :] = value[64:128]
    keep_out[...] = sums[core]
    send_out[...] = sums[1 - core]


def blocks_of(parts, turn_one, turn_two):
    return pl.pallas_call(
        block_kernel,
        out_shape=[f32(B, KA), f32(B, KA), f32(192, B), f32(192, B)],
        in_specs=[VMEM] * 4,
        out_specs=[VMEM] * 4,
        scratch_shapes=[pltpu.VMEM((2, 192, B), jnp.float32)],
        compiler_params=pltpu.CompilerParams(vmem_limit_bytes=8 * MIB),
    )(*parts, turn_one, turn_two)


def add(kept, got, order):
    half = kept.shape[0] // 2

    def body(a, b, *refs):
        outs = refs[len(order) :]
        if half == 0:
            outs[0][...] = a[0] + b[0]
            return
        outs[1][...] = a[half:] + b[half:]
        outs[0][...] = a[:half] + b[:half]

    shapes = [f32(half, B, KA)] * 2 if half else [f32(B, KA)]
    return pl.pallas_call(
        body,
        out_shape=shapes,
        in_specs=[VMEM] * 2 + [ANY] * len(order),
        out_specs=[VMEM] * len(shapes),
        compiler_params=pltpu.CompilerParams(vmem_limit_bytes=8 * MIB),
        cost_estimate=pl.CostEstimate(flops=300_000, bytes_accessed=1_000_000, transcendentals=0),
    )(kept, got, *order)


def final_kernel(base, par, first, second, out):
    total = first[...] + second[...]
    out[0:64, :] = base[0:64, :] - total[0:64, :]
    cross = base[64:128, :] - total[64:128, :]
    out[64:128, :] = cross
    out[128:192, :] = base[128:192, :] - (
        total[128:192, :]
        + lax.dot_general(
            cross,
            par[...],
            (((1,), (1,)), ((), ())),
            precision=lax.Precision.HIGHEST,
            preferred_element_type=jnp.float32,
        )
    )


def final_of(base, par, first, second):
    return pl.pallas_call(
        final_kernel,
        out_shape=f32(192, B),
        in_specs=[VMEM] * 4,
        out_specs=VMEM,
        compiler_params=pltpu.CompilerParams(vmem_limit_bytes=4 * MIB),
    )(base, par, first, second)


def join_kernel(own, other, a_out, b_out, c_out):
    core = lax.rem(lax.axis_index("pcol"), 2)
    mine = pl.multiple_of(core * 64, 64)
    rest = pl.multiple_of((1 - core) * 64, 64)
    for i, out in enumerate((a_out, b_out, c_out)):
        out[pl.ds(mine, 64), :] = own[64 * i : 64 * i + 64, :]
        out[pl.ds(rest, 64), :] = other[64 * i : 64 * i + 64, :]


def join(own, other):
    return pl.pallas_call(
        join_kernel,
        out_shape=[f32(B, B)] * 3,
        in_specs=[VMEM] * 2,
        out_specs=[VMEM] * 3,
        compiler_params=pltpu.CompilerParams(vmem_limit_bytes=4 * MIB),
    )(own, other)


def local(
    ginv_anc,
    factor_one,
    pattern_one,
    dinv_one,
    factor_two,
    factor_parent,
    pattern_two,
    parent,
    dinv_two,
):
    pair_one = pair_up(prepare(pattern_one, factor_one, factor_parent, 160))
    blocks_one = gather(pair_one)
    pair_two = pair_up(prepare(pattern_two, factor_two, blocks_one[LAG], B))
    blocks_two = gather(pair_two)
    s1a, s1b, k1a, k1b, one, turn_one = first_level(parent, ginv_anc, blocks_one)
    fix, par, base = corrections(parent, one, dinv_one, dinv_two)

    def spread(value):
        return permute(value, lambda r, c: (r ^ spread_mask(c), c))

    def settle(value):
        return permute(value, lambda r, c: (r, r ^ spread_mask(c)))

    turn_one = spread(turn_one)
    r1a, r1b = row_step(s1a, 0, 0), row_step(s1b, 1, 0)
    s2a, s2b, turn_two = second_level(1, ginv_anc, fix, blocks_two, [])
    k2a, k2b = second_level(0, ginv_anc, fix, blocks_two, [r1a, r1b, turn_one])
    turn_one = settle(turn_one)
    turn_two = spread(turn_two)
    r2a, r2b = row_step(s2a, 0, 0), row_step(s2b, 1, 0)
    going = [merge(1, k1a, r1a, k2a, r2a), merge(1, k1b, r1b, k2b, r2b)]
    kept = [merge(0, k1a, r1a, k2a, r2a), merge(0, k1b, r1b, k2b, r2b)]
    got = [row_step(going[v], v, 1) for v in range(2)]
    kept[0], first = add(kept[0], got[0], [turn_two])
    kept[1], second = add(kept[1], got[1], [])
    turn_two = settle(turn_two)
    got = [row_step(first, 0, 2), row_step(second, 1, 2)]
    kept[0], first = add(kept[0], got[0], [])
    kept[1], second = add(kept[1], got[1], [turn_one])
    got = [row_step(first, 0, 3), row_step(second, 1, 3)]
    kept = [add(kept[v], got[v], [])[0] for v in range(2)]
    anc_one, anc_two, send, keep = blocks_of(kept, turn_one, turn_two)
    sums = keep + swap(send)
    for mask in (2, 6):
        sums = sums + permute(sums, lambda r, c: (r, c ^ mask))
    done = final_of(base, par, sums, permute(sums, lambda r, c: (r, c ^ 14)))
    diag_one, cross, diag_two = join(done, swap(done))
    return anc_one, diag_one, anc_two, cross, diag_two


def solution(mesh):
    return jax.shard_map(
        local,
        mesh=mesh,
        in_specs=(
            P("prow", "pcol"),
            P("prow", "pcol"),
            P(),
            P(),
            P("prow", "pcol"),
            P(None, "pcol"),
            P(),
            P(),
            P("prow", None),
        ),
        out_specs=(
            P("prow", "pcol"),
            P("prow", None),
            P("prow", "pcol"),
            P("prow", None),
            P("prow", None),
        ),
        check_vma=False,
    )
```

```python
import jax
import jax.numpy as jnp
from jax import lax
from jax.experimental import pallas as pl
from jax.experimental.pallas import tpu as pltpu
from jax.sharding import PartitionSpec as P

N = 16
B = 128
KA = 512
ALL = ("prow", "pcol")
MASKS = (((1, 3, 4, 12), (3, 1, 12, 4)), ((4, 12, 1, 3), (12, 4, 3, 1)))
SPREAD = (1, 6, 2)
VMEM = pl.BlockSpec(memory_space=pltpu.VMEM)
SMEM = pl.BlockSpec(memory_space=pltpu.SMEM)
ANY = pl.BlockSpec(memory_space=pl.ANY)
HBM = pl.BlockSpec(memory_space=pltpu.HBM)
MIB = 1024 * 1024


def f32(*shape):
    return jax.ShapeDtypeStruct(shape, jnp.float32)


def slot_mask(core, variant, slot):
    mask = 0
    for bit in range(4):
        if (slot >> (3 - bit)) & 1:
            mask ^= MASKS[core][variant][bit]
    return mask


def destination(row, core, variant, slot):
    first, second = slot_mask(0, variant, slot), slot_mask(1, variant, slot)
    return row ^ jnp.where(core == 0, first, second)


def split(value):
    high = value.astype(jnp.bfloat16)
    low = (value - high.astype(jnp.float32)).astype(jnp.bfloat16)
    return high, low


def dot_split(left, right, dims):
    out = None
    for a, b in ((left[0], right[0]), (left[0], right[1]), (left[1], right[0])):
        term = lax.dot_general(a, b, (dims, ((), ())), preferred_element_type=jnp.float32)
        out = term if out is None else out + term
    return out


def unpack(packed):
    return jnp.concatenate([packed[:, B * i : B * i + B] for i in range(4)], axis=0)


def permute(value, move):
    pairs = []
    for r in range(N):
        for c in range(N):
            nr, nc = move(r, c)
            pairs.append((r * N + c, nr * N + nc))
    return lax.ppermute(value, ALL, pairs)


def swap(value):
    return permute(value, lambda r, c: (r, c ^ 1))


def ring(value):
    return permute(value, lambda r, c: (r, (c + (2 if c % 2 == 0 else -2)) % N))


def spread_mask(col):
    mask = 10 if col % 2 else 0
    for bit, part in enumerate(SPREAD):
        if ((col // 2) >> bit) & 1:
            mask ^= part
    return mask


def prep_kernel(pat_one, pat_two, fac_one, fac_two, par, one, two, pat, fac, par_in, sems):
    row, col = lax.axis_index("prow"), lax.axis_index("pcol")
    copies = [
        pltpu.make_async_copy(pat_one, pat.at[0], sems.at[0]),
        pltpu.make_async_copy(fac_one, fac.at[0], sems.at[1]),
        pltpu.make_async_copy(par, par_in, sems.at[2]),
        pltpu.make_async_copy(pat_two, pat.at[1], sems.at[3]),
        pltpu.make_async_copy(fac_two, fac.at[1], sems.at[4]),
    ]
    for copy in copies:
        copy.start()
    lanes = lax.broadcasted_iota(jnp.int32, (1, 64), 1)

    def turn(level, out):
        for i in range(4):
            cut = pl.ds(B * i, B)
            flags = jnp.where(lanes == 4 * row + i, pat[level, pl.ds(col, 1), :], 0)
            weight = jnp.sum(flags.astype(jnp.float32), axis=1, keepdims=True)
            out[0:128, cut] = fac[level, cut, :].T * weight

    copies[0].wait()
    copies[1].wait()
    turn(0, one)
    copies[2].wait()
    turned = par_in[...].T
    for i in range(4):
        one[128:160, B * i : B * i + B] = turned[32 * i : 32 * i + 32, :]
    copies[3].wait()
    copies[4].wait()
    turn(1, two)


def prepare(pat_one, pat_two, fac_one, fac_two, par):
    return pl.pallas_call(
        prep_kernel,
        out_shape=[f32(160, KA), f32(B, KA)],
        in_specs=[HBM] * 5,
        out_specs=[VMEM] * 2,
        scratch_shapes=[
            pltpu.VMEM((2, N, 64), jnp.int32),
            pltpu.VMEM((2, KA, B), jnp.float32),
            pltpu.VMEM((B, B), jnp.float32),
            pltpu.SemaphoreType.DMA((5,)),
        ],
        compiler_params=pltpu.CompilerParams(vmem_limit_bytes=56 * MIB),
    )(pat_one, pat_two, fac_one, fac_two, par)


def pair_up(own):
    return jnp.stack([own, swap(own)])


def gather(pair):
    blocks = [pair]
    going = pair
    for step in range(4):
        if step == 3:
            going = going[0:1]
        going = ring(going)
        blocks += [going, swap(going)]
    return blocks


def place():
    row, col = lax.axis_index("prow"), lax.axis_index("pcol")
    core = lax.rem(col, 2)
    z = lax.div(col, 2)
    target = row ^ (core * 10)
    for bit, mask in enumerate(SPREAD):
        target = target ^ (lax.rem(lax.shift_right_logical(z, bit), 2) * mask)
    return row, col, core, target


def fetch(refs, target, sems):
    col = lax.axis_index("pcol")
    z, core = lax.div(col, 2), lax.rem(col, 2)
    copies = []
    for at, ref in enumerate(refs):
        step = (at + 1) // 2
        swapped = at > 0 and at % 2 == 0
        side = (1 - core) if swapped else core
        away = jnp.where(side == 0, 8 - step, step)
        plane = lax.rem(z + away, 8)
        for i in range(ref.shape[0]):
            parity = side if i == 0 else 1 - side
            copies.append(
                pltpu.make_async_copy(
                    ref.at[i], target.at[plane * 2 + parity], sems.at[len(copies)]
                )
            )
    return copies


def one_kernel(parent, ginv, *refs):
    blocks, refs = refs[:9], refs[9:]
    sends, keeps, one, turn, left, sems = (
        refs[0:2], refs[2:4], refs[4], refs[5], refs[6], refs[7],
    )
    row, col, core, target = place()
    copies = fetch(blocks, one, sems)
    for copy in copies:
        copy.start()
    high, low = split(ginv[...])
    for copy in copies:
        copy.wait()
    turn[0:128, :] = one[parent[target], 0:128, :]
    turn[128:256, :] = one[target, 0:128, :]
    for variant in range(2):
        for half in (1, 0):
            for slot in range(8):
                dest = destination(row, core, variant, slot + 8 * half)
                left[64 * slot : 64 * slot + 64, :] = one[dest, 64 * variant : 64 * variant + 64, :]
            value = dot_split(split(left[...]), (high, low), ((1,), (0,)))
            out = sends[variant] if half else keeps[variant]
            out[...] = -value.reshape(8, 64, KA)


def first_level(parent, ginv, blocks):
    return pl.pallas_call(
        one_kernel,
        out_shape=[f32(8, 64, KA)] * 4 + [f32(16, 160, KA), f32(256, KA)],
        in_specs=[SMEM, VMEM] + [ANY] * 9,
        out_specs=[VMEM] * 6,
        scratch_shapes=[pltpu.VMEM((512, KA), jnp.float32), pltpu.SemaphoreType.DMA((16,))],
        compiler_params=pltpu.CompilerParams(vmem_limit_bytes=8 * MIB),
        cost_estimate=pl.CostEstimate(
            flops=4_000_000_000, bytes_accessed=1_000_000, transcendentals=0
        ),
    )(parent, ginv, *blocks)


def fix_kernel(parent, one, dinv_one, dinv_two, fix, par_out, base, dinv, sems):
    row, col, core, target = place()
    top = pl.multiple_of(core * 64, 64)
    sources = (
        dinv_one.at[pl.ds(pl.multiple_of(row * B, B), B)],
        dinv_one.at[pl.ds(pl.multiple_of(parent[row] * B, B), B)],
        dinv_two,
    )
    copies = [
        pltpu.make_async_copy(source, dinv.at[i], sems.at[i]) for i, source in enumerate(sources)
    ]
    for copy in copies:
        copy.start()

    def correct(m, carry):
        par = unpack(one[m, 128:160, :])
        fix[m] = dot_split(split(par), split(one[parent[m], 0:128, :]), ((1,), (0,)))
        return carry

    lax.fori_loop(0, 16, correct, 0)
    par_out[...] = unpack(one[row, 128:160, :])
    for copy in copies:
        copy.wait()
    base[0:64, :] = dinv[0, pl.ds(top, 64), :]
    base[64:128, :] = -jnp.dot(
        par_out[pl.ds(top, 64), :],
        dinv[1],
        precision=lax.Precision.HIGHEST,
        preferred_element_type=jnp.float32,
    )
    base[128:192, :] = dinv[2, pl.ds(top, 64), :]


def corrections(parent, one, dinv_one, dinv_two):
    return pl.pallas_call(
        fix_kernel,
        out_shape=[f32(16, B, KA), f32(B, B), f32(192, B)],
        in_specs=[SMEM, VMEM, HBM, HBM],
        out_specs=[VMEM] * 3,
        scratch_shapes=[pltpu.VMEM((3, B, B), jnp.float32), pltpu.SemaphoreType.DMA((3,))],
        compiler_params=pltpu.CompilerParams(vmem_limit_bytes=6 * MIB),
        cost_estimate=pl.CostEstimate(
            flops=4_000_000_000, bytes_accessed=1_000_000, transcendentals=0
        ),
    )(parent, one, dinv_one, dinv_two)


def two_kernel(half, ginv, fix, two, outs, left):
    row, col, core, target = place()
    ginv = split(ginv[...])
    if half:
        outs[2][...] = two[target]
    for variant in range(2):
        for slot in range(8):
            dest = destination(row, core, variant, slot + 8 * half)
            rows = pl.ds(64 * variant, 64)
            left[64 * slot : 64 * slot + 64, :] = two[dest, rows, :] - fix[dest, rows, :]
        value = dot_split(split(left[...]), ginv, ((1,), (0,)))
        outs[variant][...] = -value.reshape(8, 64, KA)


def second_level(half, ginv, fix, gathered, order):
    def body(ginv, fix, two, *refs):
        two_kernel(half, ginv, fix, two, refs[len(order) : -1], refs[-1])

    return pl.pallas_call(
        body,
        out_shape=[f32(8, 64, KA)] * 2 + ([f32(128, KA)] if half else []),
        in_specs=[VMEM] * 3 + [ANY] * len(order),
        out_specs=[VMEM] * (2 + half),
        scratch_shapes=[pltpu.VMEM((512, KA), jnp.float32)],
        compiler_params=pltpu.CompilerParams(vmem_limit_bytes=8 * MIB),
        cost_estimate=pl.CostEstimate(
            flops=1_500_000_000, bytes_accessed=8_000_000, transcendentals=0
        ),
    )(ginv, fix, gathered, *order)


def merge(part, keep_one, got_one, keep_two, got_two):
    def body(a, b, c, d, out):
        for i in range(4):
            out[i, 0:64, :] = a[4 * part + i] + b[4 * part + i]
            out[i, 64:128, :] = c[4 * part + i] + d[4 * part + i]

    return pl.pallas_call(
        body,
        out_shape=f32(4, B, KA),
        in_specs=[VMEM] * 4,
        out_specs=VMEM,
        compiler_params=pltpu.CompilerParams(vmem_limit_bytes=4 * MIB),
        cost_estimate=pl.CostEstimate(flops=300_000, bytes_accessed=3_000_000, transcendentals=0),
    )(keep_one, got_one, keep_two, got_two)


def row_step(value, variant, step):
    return permute(value, lambda r, c: (r ^ MASKS[c % 2][variant][step], c))


def block_kernel(a_ref, b_ref, turn_one, turn_two, one_out, two_out, send_out, keep_out, sums):
    core = lax.rem(lax.axis_index("pcol"), 2)
    for variant, ref in enumerate((a_ref, b_ref)):
        one_out[64 * variant : 64 * variant + 64, :] = ref[0:64, :]
        two_out[64 * variant : 64 * variant + 64, :] = ref[64:128, :]
    one = split(one_out[...])
    two = split(two_out[...])
    nt = ((1,), (1,))
    for i, (left, right) in enumerate(
        ((one, turn_one[128:256, :]), (two, turn_one[0:128, :]), (two, turn_two[...]))
    ):
        value = dot_split(left, split(right), nt)
        sums[0, 64 * i : 64 * i + 64, :] = value[0:64]
        sums[1, 64 * i : 64 * i + 64, :] = value[64:128]
    keep_out[...] = sums[core]
    send_out[...] = sums[1 - core]


def blocks_of(parts, turn_one, turn_two):
    return pl.pallas_call(
        block_kernel,
        out_shape=[f32(B, KA), f32(B, KA), f32(192, B), f32(192, B)],
        in_specs=[VMEM] * 4,
        out_specs=[VMEM] * 4,
        scratch_shapes=[pltpu.VMEM((2, 192, B), jnp.float32)],
        compiler_params=pltpu.CompilerParams(vmem_limit_bytes=8 * MIB),
    )(*parts, turn_one, turn_two)


def add(kept, got, order):
    half = kept.shape[0] // 2

    def body(a, b, *refs):
        outs = refs[len(order) :]
        if half == 0:
            outs[0][...] = a[0] + b[0]
            return
        outs[1][...] = a[half:] + b[half:]
        outs[0][...] = a[:half] + b[:half]

    shapes = [f32(half, B, KA)] * 2 if half else [f32(B, KA)]
    return pl.pallas_call(
        body,
        out_shape=shapes,
        in_specs=[VMEM] * 2 + [ANY] * len(order),
        out_specs=[VMEM] * len(shapes),
        compiler_params=pltpu.CompilerParams(vmem_limit_bytes=8 * MIB),
        cost_estimate=pl.CostEstimate(flops=300_000, bytes_accessed=1_000_000, transcendentals=0),
    )(kept, got, *order)


def final_kernel(base, par, first, second, out):
    total = first[...] + second[...]
    out[0:64, :] = base[0:64, :] - total[0:64, :]
    cross = base[64:128, :] - total[64:128, :]
    out[64:128, :] = cross
    out[128:192, :] = base[128:192, :] - (
        total[128:192, :]
        + lax.dot_general(
            cross,
            par[...],
            (((1,), (1,)), ((), ())),
            precision=lax.Precision.HIGHEST,
            preferred_element_type=jnp.float32,
        )
    )


def final_of(base, par, first, second):
    return pl.pallas_call(
        final_kernel,
        out_shape=f32(192, B),
        in_specs=[VMEM] * 4,
        out_specs=VMEM,
        compiler_params=pltpu.CompilerParams(vmem_limit_bytes=4 * MIB),
    )(base, par, first, second)


def join_kernel(own, other, a_out, b_out, c_out):
    core = lax.rem(lax.axis_index("pcol"), 2)
    mine = pl.multiple_of(core * 64, 64)
    rest = pl.multiple_of((1 - core) * 64, 64)
    for i, out in enumerate((a_out, b_out, c_out)):
        out[pl.ds(mine, 64), :] = own[64 * i : 64 * i + 64, :]
        out[pl.ds(rest, 64), :] = other[64 * i : 64 * i + 64, :]


def join(own, other):
    return pl.pallas_call(
        join_kernel,
        out_shape=[f32(B, B)] * 3,
        in_specs=[VMEM] * 2,
        out_specs=[VMEM] * 3,
        compiler_params=pltpu.CompilerParams(vmem_limit_bytes=4 * MIB),
    )(own, other)


def local(
    ginv_anc,
    factor_one,
    pattern_one,
    dinv_one,
    factor_two,
    factor_parent,
    pattern_two,
    parent,
    dinv_two,
):
    own_one, own_two = prepare(pattern_one.T, pattern_two.T, factor_one, factor_two, factor_parent)
    gathered = lax.all_gather(own_two, "pcol", axis=0, tiled=False)
    blocks_one = gather(pair_up(own_one))
    s1a, s1b, k1a, k1b, one, turn_one = first_level(parent, ginv_anc, blocks_one)
    fix, par, base = corrections(parent, one, dinv_one, dinv_two)

    def spread(value):
        return permute(value, lambda r, c: (r ^ spread_mask(c), c))

    def settle(value):
        return permute(value, lambda r, c: (r, r ^ spread_mask(c)))

    turn_one = spread(turn_one)
    r1a, r1b = row_step(s1a, 0, 0), row_step(s1b, 1, 0)
    s2a, s2b, turn_two = second_level(1, ginv_anc, fix, gathered, [r1a, r1b])
    k2a, k2b = second_level(0, ginv_anc, fix, gathered, [turn_one])
    turn_one = settle(turn_one)
    turn_two = spread(turn_two)
    r2a, r2b = row_step(s2a, 0, 0), row_step(s2b, 1, 0)
    going = [merge(1, k1a, r1a, k2a, r2a), merge(1, k1b, r1b, k2b, r2b)]
    kept = [merge(0, k1a, r1a, k2a, r2a), merge(0, k1b, r1b, k2b, r2b)]
    got = [row_step(going[v], v, 1) for v in range(2)]
    kept[0], first = add(kept[0], got[0], [turn_two])
    kept[1], second = add(kept[1], got[1], [])
    turn_two = settle(turn_two)
    got = [row_step(first, 0, 2), row_step(second, 1, 2)]
    kept[0], first = add(kept[0], got[0], [])
    kept[1], second = add(kept[1], got[1], [turn_one])
    got = [row_step(first, 0, 3), row_step(second, 1, 3)]
    kept = [add(kept[0], got[0], [])[0], add(kept[1], got[1], [])[0]]
    anc_one, anc_two, send, keep = blocks_of(kept, turn_one, turn_two)
    sums = keep + swap(send)
    for mask in (2, 6):
        sums = sums + permute(sums, lambda r, c: (r, c ^ mask))
    done = final_of(base, par, sums, permute(sums, lambda r, c: (r, c ^ 14)))
    diag_one, cross, diag_two = join(done, swap(done))
    return anc_one, diag_one, anc_two, cross, diag_two


def solution(mesh):
    return jax.shard_map(
        local,
        mesh=mesh,
        in_specs=(
            P("prow", "pcol"),
            P("prow", "pcol"),
            P(),
            P(),
            P("prow", "pcol"),
            P(None, "pcol"),
            P(),
            P(),
            P("prow", None),
        ),
        out_specs=(
            P("prow", "pcol"),
            P("prow", None),
            P("prow", "pcol"),
            P("prow", None),
            P("prow", None),
        ),
        check_vma=False,
    )
```

```python
import jax
import jax.numpy as jnp
from jax import lax
from jax.experimental import pallas as pl
from jax.experimental.pallas import tpu as pltpu
from jax.sharding import PartitionSpec as P

N = 16
B = 128
KA = 512
ALL = ("prow", "pcol")
MASKS = (((1, 3, 4, 12), (3, 1, 12, 4)), ((4, 12, 1, 3), (12, 4, 3, 1)))
SPREAD = (1, 6, 2)
VMEM = pl.BlockSpec(memory_space=pltpu.VMEM)
SMEM = pl.BlockSpec(memory_space=pltpu.SMEM)
ANY = pl.BlockSpec(memory_space=pl.ANY)
HBM = pl.BlockSpec(memory_space=pltpu.HBM)
MIB = 1024 * 1024


def f32(*shape):
    return jax.ShapeDtypeStruct(shape, jnp.float32)


def slot_mask(core, variant, slot):
    mask = 0
    for bit in range(4):
        if (slot >> (3 - bit)) & 1:
            mask ^= MASKS[core][variant][bit]
    return mask


def destination(row, core, variant, slot):
    first, second = slot_mask(0, variant, slot), slot_mask(1, variant, slot)
    return row ^ jnp.where(core == 0, first, second)


def split(value):
    high = value.astype(jnp.bfloat16)
    low = (value - high.astype(jnp.float32)).astype(jnp.bfloat16)
    return high, low


def dot_split(left, right, dims):
    out = None
    for a, b in ((left[0], right[0]), (left[0], right[1]), (left[1], right[0])):
        term = lax.dot_general(a, b, (dims, ((), ())), preferred_element_type=jnp.float32)
        out = term if out is None else out + term
    return out


def unpack(packed):
    return jnp.concatenate([packed[:, B * i : B * i + B] for i in range(4)], axis=0)


def permute(value, move):
    pairs = []
    for r in range(N):
        for c in range(N):
            nr, nc = move(r, c)
            pairs.append((r * N + c, nr * N + nc))
    return lax.ppermute(value, ALL, pairs)


def swap(value):
    return permute(value, lambda r, c: (r, c ^ 1))


def ring(value):
    return permute(value, lambda r, c: (r, (c + (2 if c % 2 == 0 else -2)) % N))


def spread_mask(col):
    mask = 10 if col % 2 else 0
    for bit, part in enumerate(SPREAD):
        if ((col // 2) >> bit) & 1:
            mask ^= part
    return mask


def prep_kernel(pat_one, pat_two, fac_one, fac_two, par, own, pat, fac, par_in, sems):
    row, col = lax.axis_index("prow"), lax.axis_index("pcol")
    copies = [
        pltpu.make_async_copy(pat_one, pat.at[0], sems.at[0]),
        pltpu.make_async_copy(fac_one, fac.at[0], sems.at[1]),
        pltpu.make_async_copy(par, par_in, sems.at[2]),
        pltpu.make_async_copy(pat_two, pat.at[1], sems.at[3]),
        pltpu.make_async_copy(fac_two, fac.at[1], sems.at[4]),
    ]
    for copy in copies:
        copy.start()
    lanes = lax.broadcasted_iota(jnp.int32, (1, 64), 1)

    def turn(level, top):
        for i in range(4):
            cut = pl.ds(B * i, B)
            flags = jnp.where(lanes == 4 * row + i, pat[level, pl.ds(col, 1), :], 0)
            weight = jnp.sum(flags.astype(jnp.float32), axis=1, keepdims=True)
            own[top : top + 128, cut] = fac[level, cut, :].T * weight

    copies[0].wait()
    copies[1].wait()
    turn(0, 0)
    copies[2].wait()
    turned = par_in[...].T
    for i in range(4):
        own[128:160, B * i : B * i + B] = turned[32 * i : 32 * i + 32, :]
    copies[3].wait()
    copies[4].wait()
    turn(1, 160)


def prepare(pat_one, pat_two, fac_one, fac_two, par):
    return pl.pallas_call(
        prep_kernel,
        out_shape=f32(288, KA),
        in_specs=[HBM] * 5,
        out_specs=VMEM,
        scratch_shapes=[
            pltpu.VMEM((2, N, 64), jnp.int32),
            pltpu.VMEM((2, KA, B), jnp.float32),
            pltpu.VMEM((B, B), jnp.float32),
            pltpu.SemaphoreType.DMA((5,)),
        ],
        compiler_params=pltpu.CompilerParams(vmem_limit_bytes=56 * MIB),
    )(pat_one, pat_two, fac_one, fac_two, par)


def pair_up(own, other):
    def body(a, b, one, two):
        for i, ref in enumerate((a, b)):
            one[i] = ref[0:160, :]
            two[i] = ref[160:288, :]

    return pl.pallas_call(
        body,
        out_shape=[f32(2, 160, KA), f32(2, B, KA)],
        in_specs=[VMEM] * 2,
        out_specs=[VMEM] * 2,
        compiler_params=pltpu.CompilerParams(vmem_limit_bytes=4 * MIB),
    )(own, other)


def gather(pair):
    blocks = [pair]
    going = pair
    for step in range(4):
        if step == 3:
            going = going[0:1]
        going = ring(going)
        blocks += [going, swap(going)]
    return blocks


def place():
    row, col = lax.axis_index("prow"), lax.axis_index("pcol")
    core = lax.rem(col, 2)
    z = lax.div(col, 2)
    target = row ^ (core * 10)
    for bit, mask in enumerate(SPREAD):
        target = target ^ (lax.rem(lax.shift_right_logical(z, bit), 2) * mask)
    return row, col, core, target


def fetch(refs, target, sems):
    col = lax.axis_index("pcol")
    z, core = lax.div(col, 2), lax.rem(col, 2)
    copies = []
    for at, ref in enumerate(refs):
        step = (at + 1) // 2
        swapped = at > 0 and at % 2 == 0
        side = (1 - core) if swapped else core
        away = jnp.where(side == 0, 8 - step, step)
        plane = lax.rem(z + away, 8)
        for i in range(ref.shape[0]):
            parity = side if i == 0 else 1 - side
            copies.append(
                pltpu.make_async_copy(
                    ref.at[i], target.at[plane * 2 + parity], sems.at[len(copies)]
                )
            )
    return copies


def assemble(left, level, row, core, variant, half, fix=None):
    rows = pl.ds(64 * variant, 64)
    for slot in range(8):
        dest = destination(row, core, variant, slot + 8 * half)
        value = level[dest, rows, :]
        if fix is not None:
            value = value - fix[dest, rows, :]
        left[64 * slot : 64 * slot + 64, :] = value


def send_kernel(second, ginv, *refs):
    refs = list(refs)
    fix = refs.pop(0) if second else None
    lower = refs.pop(0) if second else None
    parent = refs.pop(0) if second else None
    blocks, refs = refs[:9], refs[9:]
    sends, level = refs[0:2], refs[2]
    left, sems = refs[-2:]
    row, col, core, target = place()
    copies = fetch(blocks, level, sems)
    for copy in copies:
        copy.start()
    ginv = split(ginv[...])
    for copy in copies:
        copy.wait()
    for variant in range(2):
        assemble(left, level, row, core, variant, 1, fix)
        value = dot_split(split(left[...]), ginv, ((1,), (0,)))
        sends[variant][...] = -value.reshape(8, 64, KA)
    if second:
        turn = refs[3]
        turn[0:128, :] = lower[parent[target], 0:128, :]
        turn[128:256, :] = lower[target, 0:128, :]
        turn[256:384, :] = level[target]


def send_half(second, ginv, blocks, extra):
    def body(*refs):
        send_kernel(second, *refs)

    rows = B if second else 160
    shapes = [f32(8, 64, KA)] * 2 + [f32(16, rows, KA)] + ([f32(384, KA)] if second else [])
    return pl.pallas_call(
        body,
        out_shape=shapes,
        in_specs=[VMEM] + ([VMEM, VMEM, SMEM] if second else []) + [ANY] * 9,
        out_specs=[VMEM] * len(shapes),
        scratch_shapes=[pltpu.VMEM((512, KA), jnp.float32), pltpu.SemaphoreType.DMA((16,))],
        compiler_params=pltpu.CompilerParams(vmem_limit_bytes=8 * MIB),
        cost_estimate=pl.CostEstimate(
            flops=2_000_000_000, bytes_accessed=1_000_000, transcendentals=0
        ),
    )(ginv, *extra, *blocks)


def keep_kernel(ginv, fix, one, two, outs, left):
    row, col, core, target = place()
    ginv = split(ginv[...])
    for variant in range(2):
        for at, level in enumerate((one, two)):
            assemble(left, level, row, core, variant, 0, fix if at else None)
            value = dot_split(split(left[...]), ginv, ((1,), (0,)))
            outs[variant][:, 64 * at : 64 * at + 64, :] = -value.reshape(8, 64, KA)


def keep_half(ginv, fix, one, two, order):
    def body(ginv, fix, one, two, *refs):
        keep_kernel(ginv, fix, one, two, refs[len(order) : -1], refs[-1])

    return pl.pallas_call(
        body,
        out_shape=[f32(8, B, KA)] * 2,
        in_specs=[VMEM] * 4 + [ANY] * len(order),
        out_specs=[VMEM] * 2,
        scratch_shapes=[pltpu.VMEM((512, KA), jnp.float32)],
        compiler_params=pltpu.CompilerParams(vmem_limit_bytes=8 * MIB),
        cost_estimate=pl.CostEstimate(
            flops=4_000_000_000, bytes_accessed=1_000_000, transcendentals=0
        ),
    )(ginv, fix, one, two, *order)


def fix_kernel(parent, one, dinv_one, dinv_two, fix, par_out, base, dinv, sems):
    row, col, core, target = place()
    top = pl.multiple_of(core * 64, 64)
    sources = (
        dinv_one.at[pl.ds(pl.multiple_of(row * B, B), B)],
        dinv_one.at[pl.ds(pl.multiple_of(parent[row] * B, B), B)],
        dinv_two,
    )
    copies = [
        pltpu.make_async_copy(source, dinv.at[i], sems.at[i]) for i, source in enumerate(sources)
    ]
    for copy in copies:
        copy.start()

    for m in range(16):
        par = unpack(one[m, 128:160, :])
        fix[m] = dot_split(split(par), split(one[parent[m], 0:128, :]), ((1,), (0,)))
    par_out[...] = unpack(one[row, 128:160, :])
    for copy in copies:
        copy.wait()
    base[0:64, :] = dinv[0, pl.ds(top, 64), :]
    base[64:128, :] = -jnp.dot(
        par_out[pl.ds(top, 64), :],
        dinv[1],
        precision=lax.Precision.HIGHEST,
        preferred_element_type=jnp.float32,
    )
    base[128:192, :] = dinv[2, pl.ds(top, 64), :]


def corrections(parent, one, dinv_one, dinv_two):
    return pl.pallas_call(
        fix_kernel,
        out_shape=[f32(16, B, KA), f32(B, B), f32(192, B)],
        in_specs=[SMEM, VMEM, HBM, HBM],
        out_specs=[VMEM] * 3,
        scratch_shapes=[pltpu.VMEM((3, B, B), jnp.float32), pltpu.SemaphoreType.DMA((3,))],
        compiler_params=pltpu.CompilerParams(vmem_limit_bytes=6 * MIB),
        cost_estimate=pl.CostEstimate(
            flops=4_000_000_000, bytes_accessed=1_000_000, transcendentals=0
        ),
    )(parent, one, dinv_one, dinv_two)


def merge(part, keep, got_one, got_two, order):
    def body(a, b, c, *refs):
        out = refs[-1]
        for i in range(4):
            out[i, 0:64, :] = a[4 * part + i, 0:64, :] + b[4 * part + i]
            out[i, 64:128, :] = a[4 * part + i, 64:128, :] + c[4 * part + i]

    return pl.pallas_call(
        body,
        out_shape=f32(4, B, KA),
        in_specs=[VMEM] * 3 + [ANY] * len(order),
        out_specs=VMEM,
        compiler_params=pltpu.CompilerParams(vmem_limit_bytes=4 * MIB),
        cost_estimate=pl.CostEstimate(flops=300_000, bytes_accessed=1_000_000, transcendentals=0),
    )(keep, got_one, got_two, *order)


def row_step(value, variant, step):
    return permute(value, lambda r, c: (r ^ MASKS[c % 2][variant][step], c))


def block_kernel(a_ref, b_ref, turn, one_out, two_out, send_out, keep_out, sums):
    core = lax.rem(lax.axis_index("pcol"), 2)
    for variant, ref in enumerate((a_ref, b_ref)):
        one_out[64 * variant : 64 * variant + 64, :] = ref[0:64, :]
        two_out[64 * variant : 64 * variant + 64, :] = ref[64:128, :]
    one = split(one_out[...])
    two = split(two_out[...])
    nt = ((1,), (1,))
    for i, (left, right) in enumerate(
        ((one, turn[128:256, :]), (two, turn[0:128, :]), (two, turn[256:384, :]))
    ):
        value = dot_split(left, split(right), nt)
        sums[0, 64 * i : 64 * i + 64, :] = value[0:64]
        sums[1, 64 * i : 64 * i + 64, :] = value[64:128]
    keep_out[...] = sums[core]
    send_out[...] = sums[1 - core]


def blocks_of(parts, turn):
    return pl.pallas_call(
        block_kernel,
        out_shape=[f32(B, KA), f32(B, KA), f32(192, B), f32(192, B)],
        in_specs=[VMEM] * 3,
        out_specs=[VMEM] * 4,
        scratch_shapes=[pltpu.VMEM((2, 192, B), jnp.float32)],
        compiler_params=pltpu.CompilerParams(vmem_limit_bytes=8 * MIB),
    )(*parts, turn)


def add(kept, got, order):
    half = kept.shape[0] // 2

    def body(a, b, *refs):
        outs = refs[len(order) :]
        if half == 0:
            outs[0][...] = a[0] + b[0]
            return
        outs[1][...] = a[half:] + b[half:]
        outs[0][...] = a[:half] + b[:half]

    shapes = [f32(half, B, KA)] * 2 if half else [f32(B, KA)]
    return pl.pallas_call(
        body,
        out_shape=shapes,
        in_specs=[VMEM] * 2 + [ANY] * len(order),
        out_specs=[VMEM] * len(shapes),
        compiler_params=pltpu.CompilerParams(vmem_limit_bytes=8 * MIB),
        cost_estimate=pl.CostEstimate(flops=300_000, bytes_accessed=1_000_000, transcendentals=0),
    )(kept, got, *order)


def final_kernel(base, par, first, second, out):
    total = first[...] + second[...]
    out[0:64, :] = base[0:64, :] - total[0:64, :]
    cross = base[64:128, :] - total[64:128, :]
    out[64:128, :] = cross
    out[128:192, :] = base[128:192, :] - (
        total[128:192, :]
        + lax.dot_general(
            cross,
            par[...],
            (((1,), (1,)), ((), ())),
            precision=lax.Precision.HIGHEST,
            preferred_element_type=jnp.float32,
        )
    )


def final_of(base, par, first, second):
    return pl.pallas_call(
        final_kernel,
        out_shape=f32(192, B),
        in_specs=[VMEM] * 4,
        out_specs=VMEM,
        compiler_params=pltpu.CompilerParams(vmem_limit_bytes=4 * MIB),
    )(base, par, first, second)


def join_kernel(own, other, a_out, b_out, c_out):
    core = lax.rem(lax.axis_index("pcol"), 2)
    mine = pl.multiple_of(core * 64, 64)
    rest = pl.multiple_of((1 - core) * 64, 64)
    for i, out in enumerate((a_out, b_out, c_out)):
        out[pl.ds(mine, 64), :] = own[64 * i : 64 * i + 64, :]
        out[pl.ds(rest, 64), :] = other[64 * i : 64 * i + 64, :]


def join(own, other):
    return pl.pallas_call(
        join_kernel,
        out_shape=[f32(B, B)] * 3,
        in_specs=[VMEM] * 2,
        out_specs=[VMEM] * 3,
        compiler_params=pltpu.CompilerParams(vmem_limit_bytes=4 * MIB),
    )(own, other)


def local(
    ginv_anc,
    factor_one,
    pattern_one,
    dinv_one,
    factor_two,
    factor_parent,
    pattern_two,
    parent,
    dinv_two,
):
    own = prepare(pattern_one.T, pattern_two.T, factor_one, factor_two, factor_parent)
    pair_one, pair_two = pair_up(own, swap(own))
    blocks_one = gather(pair_one)
    blocks_two = gather(pair_two)
    s1a, s1b, one = send_half(0, ginv_anc, blocks_one, [])
    fix, par, base = corrections(parent, one, dinv_one, dinv_two)
    r1a, r1b = row_step(s1a, 0, 0), row_step(s1b, 1, 0)
    s2a, s2b, two, turn = send_half(1, ginv_anc, blocks_two, [fix, one, parent])
    r2a, r2b = row_step(s2a, 0, 0), row_step(s2b, 1, 0)
    turn = permute(turn, lambda r, c: (r ^ spread_mask(c), c))
    keep_a, keep_b = keep_half(ginv_anc, fix, one, two, [r1a, r1b, turn])
    going = [merge(1, keep_a, r1a, r2a, []), merge(1, keep_b, r1b, r2b, [])]
    kept = [merge(0, keep_a, r1a, r2a, []), merge(0, keep_b, r1b, r2b, [])]
    turn = permute(turn, lambda r, c: (r, r ^ spread_mask(c)))
    got = [row_step(going[v], v, 1) for v in range(2)]
    kept[0], first = add(kept[0], got[0], [])
    kept[1], second = add(kept[1], got[1], [])
    got = [row_step(first, 0, 2), row_step(second, 1, 2)]
    kept[0], first = add(kept[0], got[0], [])
    kept[1], second = add(kept[1], got[1], [turn])
    got = [row_step(first, 0, 3), row_step(second, 1, 3)]
    kept = [add(kept[0], got[0], [])[0], add(kept[1], got[1], [])[0]]
    anc_one, anc_two, send, keep = blocks_of(kept, turn)
    sums = keep + swap(send)
    for mask in (2, 6):
        sums = sums + permute(sums, lambda r, c: (r, c ^ mask))
    done = final_of(base, par, sums, permute(sums, lambda r, c: (r, c ^ 14)))
    diag_one, cross, diag_two = join(done, swap(done))
    return anc_one, diag_one, anc_two, cross, diag_two


def solution(mesh):
    return jax.shard_map(
        local,
        mesh=mesh,
        in_specs=(
            P("prow", "pcol"),
            P("prow", "pcol"),
            P(),
            P(),
            P("prow", "pcol"),
            P(None, "pcol"),
            P(),
            P(),
            P("prow", None),
        ),
        out_specs=(
            P("prow", "pcol"),
            P("prow", None),
            P("prow", "pcol"),
            P("prow", None),
            P("prow", None),
        ),
        check_vma=False,
    )
```

```python
import jax
import jax.numpy as jnp
from jax import lax
from jax.experimental import pallas as pl
from jax.experimental.pallas import tpu as pltpu
from jax.sharding import PartitionSpec as P

N = 16
B = 128
KA = 512
ALL = ("prow", "pcol")
MASKS = (((1, 3, 4, 12), (3, 1, 12, 4)), ((4, 12, 1, 3), (12, 4, 3, 1)))
SPREAD = (1, 6, 2)
VMEM = pl.BlockSpec(memory_space=pltpu.VMEM)
SMEM = pl.BlockSpec(memory_space=pltpu.SMEM)
ANY = pl.BlockSpec(memory_space=pl.ANY)
HBM = pl.BlockSpec(memory_space=pltpu.HBM)
MIB = 1024 * 1024


def f32(*shape):
    return jax.ShapeDtypeStruct(shape, jnp.float32)


def slot_mask(core, variant, slot):
    mask = 0
    for bit in range(4):
        if (slot >> (3 - bit)) & 1:
            mask ^= MASKS[core][variant][bit]
    return mask


def destination(row, core, variant, slot):
    first, second = slot_mask(0, variant, slot), slot_mask(1, variant, slot)
    return row ^ jnp.where(core == 0, first, second)


def split(value):
    high = value.astype(jnp.bfloat16)
    low = (value - high.astype(jnp.float32)).astype(jnp.bfloat16)
    return high, low


def dot_split(left, right, dims):
    out = None
    for a, b in ((left[0], right[0]), (left[0], right[1]), (left[1], right[0])):
        term = lax.dot_general(a, b, (dims, ((), ())), preferred_element_type=jnp.float32)
        out = term if out is None else out + term
    return out


def unpack(packed):
    return jnp.concatenate([packed[:, B * i : B * i + B] for i in range(4)], axis=0)


def permute(value, move):
    pairs = []
    for r in range(N):
        for c in range(N):
            nr, nc = move(r, c)
            pairs.append((r * N + c, nr * N + nc))
    return lax.ppermute(value, ALL, pairs)


def swap(value):
    return permute(value, lambda r, c: (r, c ^ 1))


def ring(value):
    return permute(value, lambda r, c: (r, (c + (2 if c % 2 == 0 else -2)) % N))


def spread_mask(col):
    mask = 10 if col % 2 else 0
    for bit, part in enumerate(SPREAD):
        if ((col // 2) >> bit) & 1:
            mask ^= part
    return mask


def prep_kernel(pat_one, pat_two, fac_one, fac_two, par, own, pat, fac, par_in, sems):
    row, col = lax.axis_index("prow"), lax.axis_index("pcol")
    copies = [
        pltpu.make_async_copy(pat_one, pat.at[0], sems.at[0]),
        pltpu.make_async_copy(fac_one, fac.at[0], sems.at[1]),
        pltpu.make_async_copy(par, par_in, sems.at[2]),
        pltpu.make_async_copy(pat_two, pat.at[1], sems.at[3]),
        pltpu.make_async_copy(fac_two, fac.at[1], sems.at[4]),
    ]
    for copy in copies:
        copy.start()
    lanes = lax.broadcasted_iota(jnp.int32, (1, 64), 1)

    def turn(level, top):
        for i in range(4):
            cut = pl.ds(B * i, B)
            flags = jnp.where(lanes == 4 * row + i, pat[level, pl.ds(col, 1), :], 0)
            weight = jnp.sum(flags.astype(jnp.float32), axis=1, keepdims=True)
            own[top : top + 128, cut] = fac[level, cut, :].T * weight

    copies[0].wait()
    copies[1].wait()
    turn(0, 0)
    copies[2].wait()
    turned = par_in[...].T
    for i in range(4):
        own[128:160, B * i : B * i + B] = turned[32 * i : 32 * i + 32, :]
    copies[3].wait()
    copies[4].wait()
    turn(1, 160)


def prepare(pat_one, pat_two, fac_one, fac_two, par):
    return pl.pallas_call(
        prep_kernel,
        out_shape=f32(288, KA),
        in_specs=[HBM] * 5,
        out_specs=VMEM,
        scratch_shapes=[
            pltpu.VMEM((2, N, 64), jnp.int32),
            pltpu.VMEM((2, KA, B), jnp.float32),
            pltpu.VMEM((B, B), jnp.float32),
            pltpu.SemaphoreType.DMA((5,)),
        ],
        compiler_params=pltpu.CompilerParams(vmem_limit_bytes=56 * MIB),
    )(pat_one, pat_two, fac_one, fac_two, par)


def pair_up(own, other):
    def body(a, b, one, two, sems):
        copies = []
        for i, ref in enumerate((a, b)):
            copies.append(
                pltpu.make_async_copy(ref.at[pl.ds(0, 160)], one.at[i], sems.at[2 * i])
            )
            copies.append(
                pltpu.make_async_copy(ref.at[pl.ds(160, 128)], two.at[i], sems.at[2 * i + 1])
            )
        for copy in copies:
            copy.start()
        for copy in copies:
            copy.wait()

    return pl.pallas_call(
        body,
        out_shape=[f32(2, 160, KA), f32(2, B, KA)],
        in_specs=[HBM, ANY],
        out_specs=[VMEM] * 2,
        scratch_shapes=[pltpu.SemaphoreType.DMA((4,))],
        compiler_params=pltpu.CompilerParams(vmem_limit_bytes=4 * MIB),
    )(own, other)


def gather(pair):
    blocks = [pair]
    going = pair
    for step in range(4):
        if step == 3:
            going = going[0:1]
        going = ring(going)
        blocks += [going, swap(going)]
    return blocks


def place():
    row, col = lax.axis_index("prow"), lax.axis_index("pcol")
    core = lax.rem(col, 2)
    z = lax.div(col, 2)
    target = row ^ (core * 10)
    for bit, mask in enumerate(SPREAD):
        target = target ^ (lax.rem(lax.shift_right_logical(z, bit), 2) * mask)
    return row, col, core, target


def fetch(refs, target, sems, first):
    col = lax.axis_index("pcol")
    z, core = lax.div(col, 2), lax.rem(col, 2)
    copies = []
    for at, ref in enumerate(refs):
        step = (at + 1) // 2
        swapped = at > 0 and at % 2 == 0
        side = (1 - core) if swapped else core
        away = jnp.where(side == 0, 8 - step, step)
        plane = lax.rem(z + away, 8)
        for i in range(ref.shape[0]):
            parity = side if i == 0 else 1 - side
            copies.append(
                pltpu.make_async_copy(
                    ref.at[i], target.at[plane * 2 + parity], sems.at[first + len(copies)]
                )
            )
    return copies


def products(ginv, one, two, row, core, half, left, outs):
    for variant in range(2):
        rows = pl.ds(64 * variant, 64)
        for at, level in enumerate((one, two)):
            for slot in range(8):
                dest = destination(row, core, variant, slot + 8 * half)
                left[64 * slot : 64 * slot + 64, :] = level[dest, rows, :]
            value = dot_split(split(left[...]), ginv, ((1,), (0,)))
            outs[variant][:, 64 * at : 64 * at + 64, :] = -value.reshape(8, 64, KA)


def send_kernel(parent, ginv, *refs):
    first, second, refs = refs[:9], refs[9:18], refs[18:]
    sends, one, two, turn, left, block, sems = refs[0:2], *refs[2:]
    row, col, core, target = place()
    load = pltpu.make_async_copy(ginv, block, sems.at[32])
    low = fetch(first, one, sems, 0)
    high = fetch(second, two, sems, 16)
    for copy in low + [load] + high:
        copy.start()
    for copy in low:
        copy.wait()
    turn[0:128, :] = one[parent[target], 0:128, :]
    turn[128:256, :] = one[target, 0:128, :]
    for copy in high:
        copy.wait()
    turn[256:384, :] = two[target]
    for m in range(16):
        par = split(unpack(one[m, 128:160, :]))
        two[m] = two[m] - dot_split(par, split(one[parent[m], 0:128, :]), ((1,), (0,)))
    load.wait()
    products(split(block[...]), one, two, row, core, 1, left, sends)


def send_half(parent, ginv, first, second):
    return pl.pallas_call(
        send_kernel,
        out_shape=[f32(8, B, KA)] * 2
        + [f32(16, 160, KA), f32(16, B, KA), f32(384, KA)],
        in_specs=[SMEM, HBM] + [ANY] * 18,
        out_specs=[VMEM] * 5,
        scratch_shapes=[
            pltpu.VMEM((512, KA), jnp.float32),
            pltpu.VMEM((512, KA), jnp.float32),
            pltpu.SemaphoreType.DMA((33,)),
        ],
        compiler_params=pltpu.CompilerParams(vmem_limit_bytes=8 * MIB),
        cost_estimate=pl.CostEstimate(
            flops=8_000_000_000, bytes_accessed=1_000_000, transcendentals=0
        ),
    )(parent, ginv, *first, *second)


def keep_half(parent, ginv, one, two, dinv_one, dinv_two, order):
    def body(parent, ginv, one, two, dinv_one, dinv_two, *refs):
        outs, refs = refs[len(order) : len(order) + 2], refs[len(order) + 2 :]
        par_out, base, left, dinv, sems = refs
        row, col, core, target = place()
        base_parts(parent, one, dinv_one, dinv_two, par_out, base, dinv, sems, row, core)
        products(split(ginv[...]), one, two, row, core, 0, left, outs)

    return pl.pallas_call(
        body,
        out_shape=[f32(8, B, KA)] * 2 + [f32(B, B), f32(192, B)],
        in_specs=[SMEM] + [VMEM] * 3 + [HBM] * 2 + [ANY] * len(order),
        out_specs=[VMEM] * 4,
        scratch_shapes=[
            pltpu.VMEM((512, KA), jnp.float32),
            pltpu.VMEM((3, B, B), jnp.float32),
            pltpu.SemaphoreType.DMA((3,)),
        ],
        compiler_params=pltpu.CompilerParams(vmem_limit_bytes=8 * MIB),
        cost_estimate=pl.CostEstimate(
            flops=4_000_000_000, bytes_accessed=1_000_000, transcendentals=0
        ),
    )(parent, ginv, one, two, dinv_one, dinv_two, *order)


def base_parts(parent, one, dinv_one, dinv_two, par_out, base, dinv, sems, row, core):
    top = pl.multiple_of(core * 64, 64)
    sources = (
        dinv_one.at[pl.ds(pl.multiple_of(row * B, B), B)],
        dinv_one.at[pl.ds(pl.multiple_of(parent[row] * B, B), B)],
        dinv_two,
    )
    copies = [
        pltpu.make_async_copy(source, dinv.at[i], sems.at[i]) for i, source in enumerate(sources)
    ]
    for copy in copies:
        copy.start()
    par_out[...] = unpack(one[row, 128:160, :])
    for copy in copies:
        copy.wait()
    base[0:64, :] = dinv[0, pl.ds(top, 64), :]
    base[64:128, :] = -jnp.dot(
        par_out[pl.ds(top, 64), :],
        dinv[1],
        precision=lax.Precision.HIGHEST,
        preferred_element_type=jnp.float32,
    )
    base[128:192, :] = dinv[2, pl.ds(top, 64), :]


def row_step(value, variant, step):
    return permute(value, lambda r, c: (r ^ MASKS[c % 2][variant][step], c))


def block_kernel(a_ref, b_ref, turn, one_out, two_out, send_out, keep_out, sums):
    core = lax.rem(lax.axis_index("pcol"), 2)
    for variant, ref in enumerate((a_ref, b_ref)):
        one_out[64 * variant : 64 * variant + 64, :] = ref[0:64, :]
        two_out[64 * variant : 64 * variant + 64, :] = ref[64:128, :]
    one = split(one_out[...])
    two = split(two_out[...])
    nt = ((1,), (1,))
    for i, (left, right) in enumerate(
        ((one, turn[128:256, :]), (two, turn[0:128, :]), (two, turn[256:384, :]))
    ):
        value = dot_split(left, split(right), nt)
        sums[0, 64 * i : 64 * i + 64, :] = value[0:64]
        sums[1, 64 * i : 64 * i + 64, :] = value[64:128]
    keep_out[...] = sums[core]
    send_out[...] = sums[1 - core]


def blocks_of(parts, turn):
    return pl.pallas_call(
        block_kernel,
        out_shape=[f32(B, KA), f32(B, KA), f32(192, B), f32(192, B)],
        in_specs=[VMEM] * 3,
        out_specs=[VMEM] * 4,
        scratch_shapes=[pltpu.VMEM((2, 192, B), jnp.float32)],
        compiler_params=pltpu.CompilerParams(vmem_limit_bytes=8 * MIB),
    )(*parts, turn)


def add(part, kept, got, order=()):
    half = kept.shape[0] // 2

    def body(a, b, *refs):
        out = refs[-1]
        if half == 0:
            out[...] = a[0] + b[0]
        else:
            at = pl.ds(half * part, half)
            out[...] = a[at] + b[at]

    return pl.pallas_call(
        body,
        out_shape=f32(half, B, KA) if half else f32(B, KA),
        in_specs=[VMEM] * 2 + [ANY] * len(order),
        out_specs=VMEM,
        compiler_params=pltpu.CompilerParams(vmem_limit_bytes=8 * MIB),
        cost_estimate=pl.CostEstimate(flops=300_000, bytes_accessed=1_000_000, transcendentals=0),
    )(kept, got, *order)


def final_kernel(base, par, first, second, out):
    total = first[...] + second[...]
    out[0:64, :] = base[0:64, :] - total[0:64, :]
    cross = base[64:128, :] - total[64:128, :]
    out[64:128, :] = cross
    out[128:192, :] = base[128:192, :] - (
        total[128:192, :]
        + lax.dot_general(
            cross,
            par[...],
            (((1,), (1,)), ((), ())),
            precision=lax.Precision.HIGHEST,
            preferred_element_type=jnp.float32,
        )
    )


def final_of(base, par, first, second):
    return pl.pallas_call(
        final_kernel,
        out_shape=f32(192, B),
        in_specs=[VMEM] * 4,
        out_specs=VMEM,
        compiler_params=pltpu.CompilerParams(vmem_limit_bytes=4 * MIB),
    )(base, par, first, second)


def join_kernel(own, other, a_out, b_out, c_out):
    core = lax.rem(lax.axis_index("pcol"), 2)
    mine = pl.multiple_of(core * 64, 64)
    rest = pl.multiple_of((1 - core) * 64, 64)
    for i, out in enumerate((a_out, b_out, c_out)):
        out[pl.ds(mine, 64), :] = own[64 * i : 64 * i + 64, :]
        out[pl.ds(rest, 64), :] = other[64 * i : 64 * i + 64, :]


def join(own, other):
    return pl.pallas_call(
        join_kernel,
        out_shape=[f32(B, B)] * 3,
        in_specs=[VMEM] * 2,
        out_specs=[VMEM] * 3,
        compiler_params=pltpu.CompilerParams(vmem_limit_bytes=4 * MIB),
    )(own, other)


def local(
    ginv_anc,
    factor_one,
    pattern_one,
    dinv_one,
    factor_two,
    factor_parent,
    pattern_two,
    parent,
    dinv_two,
):
    own = prepare(pattern_one.T, pattern_two.T, factor_one, factor_two, factor_parent)
    pair_one, pair_two = pair_up(own, swap(own))
    blocks_one = gather(pair_one)
    blocks_two = gather(pair_two)
    send_a, send_b, one, two, turn = send_half(parent, ginv_anc, blocks_one, blocks_two)
    got = [row_step(send_a, 0, 0), row_step(send_b, 1, 0)]
    turn = permute(turn, lambda r, c: (r ^ spread_mask(c), c))
    keep_a, keep_b, par, base = keep_half(
        parent, ginv_anc, one, two, dinv_one, dinv_two, [turn]
    )
    kept = [keep_a, keep_b]
    turn = permute(turn, lambda r, c: (r, r ^ spread_mask(c)))
    for step in range(1, 4):
        order = [turn] if step == 3 else []
        going = [add(1, kept[0], got[0]), add(1, kept[1], got[1], order)]
        kept = [add(0, kept[v], got[v]) for v in range(2)]
        got = [row_step(going[v], v, step) for v in range(2)]
    kept = [add(0, kept[v], got[v]) for v in range(2)]
    anc_one, anc_two, send, keep = blocks_of(kept, turn)
    sums = keep + swap(send)
    for mask in (2, 6):
        sums = sums + permute(sums, lambda r, c: (r, c ^ mask))
    done = final_of(base, par, sums, permute(sums, lambda r, c: (r, c ^ 14)))
    diag_one, cross, diag_two = join(done, swap(done))
    return anc_one, diag_one, anc_two, cross, diag_two


def solution(mesh):
    return jax.shard_map(
        local,
        mesh=mesh,
        in_specs=(
            P("prow", "pcol"),
            P("prow", "pcol"),
            P(),
            P(),
            P("prow", "pcol"),
            P(None, "pcol"),
            P(),
            P(),
            P("prow", None),
        ),
        out_specs=(
            P("prow", "pcol"),
            P("prow", None),
            P("prow", "pcol"),
            P("prow", None),
            P("prow", None),
        ),
        check_vma=False,
    )
```

```python
import jax
import jax.numpy as jnp
from jax import lax
from jax.experimental import pallas as pl
from jax.experimental.pallas import tpu as pltpu
from jax.sharding import PartitionSpec as P

N = 16
B = 128
KA = 512
ALL = ("prow", "pcol")
MASKS = (((1, 3, 4, 12), (3, 1, 12, 4)), ((4, 12, 1, 3), (12, 4, 3, 1)))
SPREAD = (1, 6, 2)
VMEM = pl.BlockSpec(memory_space=pltpu.VMEM)
SMEM = pl.BlockSpec(memory_space=pltpu.SMEM)
ANY = pl.BlockSpec(memory_space=pl.ANY)
HBM = pl.BlockSpec(memory_space=pltpu.HBM)
MIB = 1024 * 1024


def f32(*shape):
    return jax.ShapeDtypeStruct(shape, jnp.float32)


def slot_mask(core, variant, slot):
    mask = 0
    for bit in range(4):
        if (slot >> (3 - bit)) & 1:
            mask ^= MASKS[core][variant][bit]
    return mask


def destination(row, core, variant, slot):
    first, second = slot_mask(0, variant, slot), slot_mask(1, variant, slot)
    return row ^ jnp.where(core == 0, first, second)


def split(value):
    high = value.astype(jnp.bfloat16)
    low = (value - high.astype(jnp.float32)).astype(jnp.bfloat16)
    return high, low


def dot_split(left, right, dims):
    out = None
    for a, b in ((left[0], right[0]), (left[0], right[1]), (left[1], right[0])):
        term = lax.dot_general(a, b, (dims, ((), ())), preferred_element_type=jnp.float32)
        out = term if out is None else out + term
    return out


def unpack(packed):
    return jnp.concatenate([packed[:, B * i : B * i + B] for i in range(4)], axis=0)


def permute(value, move):
    pairs = []
    for r in range(N):
        for c in range(N):
            nr, nc = move(r, c)
            pairs.append((r * N + c, nr * N + nc))
    return lax.ppermute(value, ALL, pairs)


def swap(value):
    return permute(value, lambda r, c: (r, c ^ 1))


def ring(value):
    return permute(value, lambda r, c: (r, (c + (2 if c % 2 == 0 else -2)) % N))


def spread_mask(col):
    mask = 10 if col % 2 else 0
    for bit, part in enumerate(SPREAD):
        if ((col // 2) >> bit) & 1:
            mask ^= part
    return mask


def prep_kernel(pat_one, pat_two, fac_one, fac_two, par, own, pat, fac, par_in, sems):
    row, col = lax.axis_index("prow"), lax.axis_index("pcol")
    copies = [
        pltpu.make_async_copy(pat_one, pat.at[0], sems.at[0]),
        pltpu.make_async_copy(fac_one, fac.at[0], sems.at[1]),
        pltpu.make_async_copy(par, par_in, sems.at[2]),
        pltpu.make_async_copy(pat_two, pat.at[1], sems.at[3]),
        pltpu.make_async_copy(fac_two, fac.at[1], sems.at[4]),
    ]
    for copy in copies:
        copy.start()
    lanes = lax.broadcasted_iota(jnp.int32, (1, 64), 1)

    def turn(level, top):
        for i in range(4):
            cut = pl.ds(B * i, B)
            flags = jnp.where(lanes == 4 * row + i, pat[level, pl.ds(col, 1), :], 0)
            weight = jnp.sum(flags.astype(jnp.float32), axis=1, keepdims=True)
            own[top : top + 128, cut] = fac[level, cut, :].T * weight

    copies[0].wait()
    copies[1].wait()
    turn(0, 0)
    copies[2].wait()
    turned = par_in[...].T
    for i in range(4):
        own[128:160, B * i : B * i + B] = turned[32 * i : 32 * i + 32, :]
    copies[3].wait()
    copies[4].wait()
    turn(1, 160)


def prepare(pat_one, pat_two, fac_one, fac_two, par):
    return pl.pallas_call(
        prep_kernel,
        out_shape=f32(288, KA),
        in_specs=[HBM] * 5,
        out_specs=VMEM,
        scratch_shapes=[
            pltpu.VMEM((2, N, 64), jnp.int32),
            pltpu.VMEM((2, KA, B), jnp.float32),
            pltpu.VMEM((B, B), jnp.float32),
            pltpu.SemaphoreType.DMA((5,)),
        ],
        compiler_params=pltpu.CompilerParams(vmem_limit_bytes=56 * MIB),
    )(pat_one, pat_two, fac_one, fac_two, par)


def pair_up(own, other):
    def body(a, b, one, two, sems):
        copies = []
        for i, ref in enumerate((a, b)):
            copies.append(
                pltpu.make_async_copy(ref.at[pl.ds(0, 160)], one.at[i], sems.at[2 * i])
            )
            copies.append(
                pltpu.make_async_copy(ref.at[pl.ds(160, 128)], two.at[i], sems.at[2 * i + 1])
            )
        for copy in copies:
            copy.start()
        for copy in copies:
            copy.wait()

    return pl.pallas_call(
        body,
        out_shape=[f32(2, 160, KA), f32(2, B, KA)],
        in_specs=[HBM, ANY],
        out_specs=[VMEM] * 2,
        scratch_shapes=[pltpu.SemaphoreType.DMA((4,))],
        compiler_params=pltpu.CompilerParams(vmem_limit_bytes=4 * MIB),
    )(own, other)


def gather(pair):
    blocks = [pair]
    going = pair
    for step in range(4):
        if step == 3:
            going = going[0:1]
        going = ring(going)
        blocks += [going, swap(going)]
    return blocks


def place():
    row, col = lax.axis_index("prow"), lax.axis_index("pcol")
    core = lax.rem(col, 2)
    z = lax.div(col, 2)
    target = row ^ (core * 10)
    for bit, mask in enumerate(SPREAD):
        target = target ^ (lax.rem(lax.shift_right_logical(z, bit), 2) * mask)
    return row, col, core, target


def sources(refs):
    col = lax.axis_index("pcol")
    z, core = lax.div(col, 2), lax.rem(col, 2)
    found = []
    for at, ref in enumerate(refs):
        step = (at + 1) // 2
        swapped = at > 0 and at % 2 == 0
        side = (1 - core) if swapped else core
        away = jnp.where(side == 0, 8 - step, step)
        plane = lax.rem(z + away, 8)
        for i in range(ref.shape[0]):
            parity = side if i == 0 else 1 - side
            found.append((ref.at[i], plane * 2 + parity))
    return found


def fetch(refs, target, sems, first):
    return [
        pltpu.make_async_copy(source, target.at[m], sems.at[first + k])
        for k, (source, m) in enumerate(sources(refs))
    ]


def turn_kernel(parent, *refs):
    first, second, turn, sems = refs[:9], refs[9:18], refs[18], refs[19]
    row, col, core, target = place()
    wanted = ((first, parent[target]), (first, target), (second, target))
    for k, (blocks, which) in enumerate(wanted):
        for source, m in sources(blocks):

            @pl.when(m == which)
            def start():
                pltpu.make_async_copy(
                    source.at[pl.ds(0, 128)], turn.at[pl.ds(128 * k, 128)], sems.at[k]
                ).start()

    for k in range(3):
        part = turn.at[pl.ds(128 * k, 128)]
        pltpu.make_async_copy(part, part, sems.at[k]).wait()


def pick_turn(parent, first, second):
    return pl.pallas_call(
        turn_kernel,
        out_shape=f32(384, KA),
        in_specs=[SMEM] + [ANY] * 18,
        out_specs=VMEM,
        scratch_shapes=[pltpu.SemaphoreType.DMA((3,))],
        compiler_params=pltpu.CompilerParams(vmem_limit_bytes=4 * MIB),
        cost_estimate=pl.CostEstimate(flops=1000, bytes_accessed=1000, transcendentals=0),
    )(parent, *first, *second)


def products(ginv, level, at, row, core, half, left, outs):
    for variant in range(2):
        rows = pl.ds(64 * variant, 64)
        for slot in range(8):
            dest = destination(row, core, variant, slot + 8 * half)
            left[64 * slot : 64 * slot + 64, :] = level[dest, rows, :]
        value = dot_split(split(left[...]), ginv, ((1,), (0,)))
        outs[variant][:, 64 * at : 64 * at + 64, :] = -value.reshape(8, 64, KA)


def send_kernel(parent, ginv, turn, *refs):
    first, second, refs = refs[:9], refs[9:18], refs[18:]
    sends, one, two, left, block, sems = refs[0:2], *refs[2:]
    row, col, core, target = place()
    load = pltpu.make_async_copy(ginv, block, sems.at[32])
    low = fetch(first, one, sems, 0)
    high = fetch(second, two, sems, 16)
    for copy in [load] + low + high:
        copy.start()
    load.wait()
    ginv = split(block[...])
    for copy in low:
        copy.wait()
    products(ginv, one, 0, row, core, 1, left, sends)
    for copy in high:
        copy.wait()
    for m in range(16):
        par = split(unpack(one[m, 128:160, :]))
        two[m] = two[m] - dot_split(par, split(one[parent[m], 0:128, :]), ((1,), (0,)))
    products(ginv, two, 1, row, core, 1, left, sends)


def send_half(parent, ginv, turn, first, second):
    return pl.pallas_call(
        send_kernel,
        out_shape=[f32(8, B, KA)] * 2 + [f32(16, 160, KA), f32(16, B, KA)],
        in_specs=[SMEM, HBM] + [ANY] * 19,
        out_specs=[VMEM] * 4,
        scratch_shapes=[
            pltpu.VMEM((512, KA), jnp.float32),
            pltpu.VMEM((512, KA), jnp.float32),
            pltpu.SemaphoreType.DMA((33,)),
        ],
        compiler_params=pltpu.CompilerParams(vmem_limit_bytes=8 * MIB),
        cost_estimate=pl.CostEstimate(
            flops=20_000_000_000, bytes_accessed=1_000_000, transcendentals=0
        ),
    )(parent, ginv, turn, *first, *second)


def keep_half(parent, ginv, one, two, dinv_one, dinv_two, order):
    def body(parent, ginv, one, two, dinv_one, dinv_two, *refs):
        outs, refs = refs[len(order) : len(order) + 2], refs[len(order) + 2 :]
        par_out, base, left, dinv, sems = refs
        row, col, core, target = place()
        base_parts(parent, one, dinv_one, dinv_two, par_out, base, dinv, sems, row, core)
        ginv = split(ginv[...])
        products(ginv, one, 0, row, core, 0, left, outs)
        products(ginv, two, 1, row, core, 0, left, outs)

    return pl.pallas_call(
        body,
        out_shape=[f32(8, B, KA)] * 2 + [f32(B, B), f32(192, B)],
        in_specs=[SMEM] + [VMEM] * 3 + [HBM] * 2 + [ANY] * len(order),
        out_specs=[VMEM] * 4,
        scratch_shapes=[
            pltpu.VMEM((512, KA), jnp.float32),
            pltpu.VMEM((3, B, B), jnp.float32),
            pltpu.SemaphoreType.DMA((3,)),
        ],
        compiler_params=pltpu.CompilerParams(vmem_limit_bytes=8 * MIB),
        cost_estimate=pl.CostEstimate(
            flops=60_000_000_000, bytes_accessed=1_000_000, transcendentals=0
        ),
    )(parent, ginv, one, two, dinv_one, dinv_two, *order)


def base_parts(parent, one, dinv_one, dinv_two, par_out, base, dinv, sems, row, core):
    top = pl.multiple_of(core * 64, 64)
    sources = (
        dinv_one.at[pl.ds(pl.multiple_of(row * B, B), B)],
        dinv_one.at[pl.ds(pl.multiple_of(parent[row] * B, B), B)],
        dinv_two,
    )
    copies = [
        pltpu.make_async_copy(source, dinv.at[i], sems.at[i]) for i, source in enumerate(sources)
    ]
    for copy in copies:
        copy.start()
    par_out[...] = unpack(one[row, 128:160, :])
    for copy in copies:
        copy.wait()
    base[0:64, :] = dinv[0, pl.ds(top, 64), :]
    base[64:128, :] = -jnp.dot(
        par_out[pl.ds(top, 64), :],
        dinv[1],
        precision=lax.Precision.HIGHEST,
        preferred_element_type=jnp.float32,
    )
    base[128:192, :] = dinv[2, pl.ds(top, 64), :]


def row_step(value, variant, step):
    return permute(value, lambda r, c: (r ^ MASKS[c % 2][variant][step], c))


def block_kernel(a_ref, b_ref, turn, one_out, two_out, send_out, keep_out, sums):
    core = lax.rem(lax.axis_index("pcol"), 2)
    for variant, ref in enumerate((a_ref, b_ref)):
        one_out[64 * variant : 64 * variant + 64, :] = ref[0:64, :]
        two_out[64 * variant : 64 * variant + 64, :] = ref[64:128, :]
    one = split(one_out[...])
    two = split(two_out[...])
    nt = ((1,), (1,))
    for i, (left, right) in enumerate(
        ((one, turn[128:256, :]), (two, turn[0:128, :]), (two, turn[256:384, :]))
    ):
        value = dot_split(left, split(right), nt)
        sums[0, 64 * i : 64 * i + 64, :] = value[0:64]
        sums[1, 64 * i : 64 * i + 64, :] = value[64:128]
    keep_out[...] = sums[core]
    send_out[...] = sums[1 - core]


def blocks_of(parts, turn):
    return pl.pallas_call(
        block_kernel,
        out_shape=[f32(B, KA), f32(B, KA), f32(192, B), f32(192, B)],
        in_specs=[VMEM] * 3,
        out_specs=[VMEM] * 4,
        scratch_shapes=[pltpu.VMEM((2, 192, B), jnp.float32)],
        compiler_params=pltpu.CompilerParams(vmem_limit_bytes=8 * MIB),
    )(*parts, turn)


def add(part, kept, got, order=()):
    half = kept.shape[0] // 2

    def body(a, b, *refs):
        out = refs[-1]
        if half == 0:
            out[...] = a[0] + b[0]
        else:
            at = pl.ds(half * part, half)
            out[...] = a[at] + b[at]

    return pl.pallas_call(
        body,
        out_shape=f32(half, B, KA) if half else f32(B, KA),
        in_specs=[VMEM] * 2 + [ANY] * len(order),
        out_specs=VMEM,
        compiler_params=pltpu.CompilerParams(vmem_limit_bytes=8 * MIB),
        cost_estimate=pl.CostEstimate(flops=300_000, bytes_accessed=1_000_000, transcendentals=0),
    )(kept, got, *order)


def final_kernel(base, par, first, second, out):
    total = first[...] + second[...]
    out[0:64, :] = base[0:64, :] - total[0:64, :]
    cross = base[64:128, :] - total[64:128, :]
    out[64:128, :] = cross
    out[128:192, :] = base[128:192, :] - (
        total[128:192, :]
        + lax.dot_general(
            cross,
            par[...],
            (((1,), (1,)), ((), ())),
            precision=lax.Precision.HIGHEST,
            preferred_element_type=jnp.float32,
        )
    )


def final_of(base, par, first, second):
    return pl.pallas_call(
        final_kernel,
        out_shape=f32(192, B),
        in_specs=[VMEM] * 4,
        out_specs=VMEM,
        compiler_params=pltpu.CompilerParams(vmem_limit_bytes=4 * MIB),
    )(base, par, first, second)


def join_kernel(own, other, a_out, b_out, c_out):
    core = lax.rem(lax.axis_index("pcol"), 2)
    mine = pl.multiple_of(core * 64, 64)
    rest = pl.multiple_of((1 - core) * 64, 64)
    for i, out in enumerate((a_out, b_out, c_out)):
        out[pl.ds(mine, 64), :] = own[64 * i : 64 * i + 64, :]
        out[pl.ds(rest, 64), :] = other[64 * i : 64 * i + 64, :]


def join(own, other):
    return pl.pallas_call(
        join_kernel,
        out_shape=[f32(B, B)] * 3,
        in_specs=[VMEM] * 2,
        out_specs=[VMEM] * 3,
        compiler_params=pltpu.CompilerParams(vmem_limit_bytes=4 * MIB),
    )(own, other)


def local(
    ginv_anc,
    factor_one,
    pattern_one,
    dinv_one,
    factor_two,
    factor_parent,
    pattern_two,
    parent,
    dinv_two,
):
    own = prepare(pattern_one.T, pattern_two.T, factor_one, factor_two, factor_parent)
    pair_one, pair_two = pair_up(own, swap(own))
    blocks_one = gather(pair_one)
    blocks_two = gather(pair_two)
    turn = pick_turn(parent, blocks_one, blocks_two)
    send_a, send_b, one, two = send_half(parent, ginv_anc, turn, blocks_one, blocks_two)
    turn = permute(turn, lambda r, c: (r ^ spread_mask(c), c))
    got = [row_step(send_a, 0, 0), row_step(send_b, 1, 0)]
    keep_a, keep_b, par, base = keep_half(
        parent, ginv_anc, one, two, dinv_one, dinv_two, [turn]
    )
    kept = [keep_a, keep_b]
    turn = permute(turn, lambda r, c: (r, r ^ spread_mask(c)))
    for step in range(1, 4):
        order = [turn] if step == 3 else []
        going = [add(1, kept[0], got[0]), add(1, kept[1], got[1], order)]
        kept = [add(0, kept[v], got[v]) for v in range(2)]
        got = [row_step(going[v], v, step) for v in range(2)]
    kept = [add(0, kept[v], got[v]) for v in range(2)]
    anc_one, anc_two, send, keep = blocks_of(kept, turn)
    sums = keep + swap(send)
    for mask in (2, 6):
        sums = sums + permute(sums, lambda r, c: (r, c ^ mask))
    done = final_of(base, par, sums, permute(sums, lambda r, c: (r, c ^ 14)))
    diag_one, cross, diag_two = join(done, swap(done))
    return anc_one, diag_one, anc_two, cross, diag_two


def solution(mesh):
    return jax.shard_map(
        local,
        mesh=mesh,
        in_specs=(
            P("prow", "pcol"),
            P("prow", "pcol"),
            P(),
            P(),
            P("prow", "pcol"),
            P(None, "pcol"),
            P(),
            P(),
            P("prow", None),
        ),
        out_specs=(
            P("prow", "pcol"),
            P("prow", None),
            P("prow", "pcol"),
            P("prow", None),
            P("prow", None),
        ),
        check_vma=False,
    )
```

```python
import jax
import jax.numpy as jnp
from jax import lax
from jax.experimental import pallas as pl
from jax.experimental.pallas import tpu as pltpu
from jax.sharding import PartitionSpec as P

N = 16
B = 128
KA = 512
ALL = ("prow", "pcol")
MASKS = (((1, 3, 4, 12), (3, 1, 12, 4)), ((4, 12, 1, 3), (12, 4, 3, 1)))
SPREAD = (1, 6, 2)
VMEM = pl.BlockSpec(memory_space=pltpu.VMEM)
SMEM = pl.BlockSpec(memory_space=pltpu.SMEM)
ANY = pl.BlockSpec(memory_space=pl.ANY)
HBM = pl.BlockSpec(memory_space=pltpu.HBM)
MIB = 1024 * 1024


def f32(*shape):
    return jax.ShapeDtypeStruct(shape, jnp.float32)


def slot_mask(core, variant, slot):
    mask = 0
    for bit in range(4):
        if (slot >> (3 - bit)) & 1:
            mask ^= MASKS[core][variant][bit]
    return mask


def destination(row, core, variant, slot):
    first, second = slot_mask(0, variant, slot), slot_mask(1, variant, slot)
    return row ^ jnp.where(core == 0, first, second)


def split(value):
    high = value.astype(jnp.bfloat16)
    low = (value - high.astype(jnp.float32)).astype(jnp.bfloat16)
    return high, low


def dot_split(left, right, dims):
    out = None
    for a, b in ((left[0], right[0]), (left[0], right[1]), (left[1], right[0])):
        term = lax.dot_general(a, b, (dims, ((), ())), preferred_element_type=jnp.float32)
        out = term if out is None else out + term
    return out


def unpack(packed):
    return jnp.concatenate([packed[:, B * i : B * i + B] for i in range(4)], axis=0)


def permute(value, move):
    pairs = []
    for r in range(N):
        for c in range(N):
            nr, nc = move(r, c)
            pairs.append((r * N + c, nr * N + nc))
    return lax.ppermute(value, ALL, pairs)


def swap(value):
    return permute(value, lambda r, c: (r, c ^ 1))


def ring(value):
    return permute(value, lambda r, c: (r, (c + (2 if c % 2 == 0 else -2)) % N))


def spread_mask(col):
    mask = 10 if col % 2 else 0
    for bit, part in enumerate(SPREAD):
        if ((col // 2) >> bit) & 1:
            mask ^= part
    return mask


def prep_kernel(pat_one, pat_two, fac_one, fac_two, par, own, pat, fac, par_in, sems):
    row, col = lax.axis_index("prow"), lax.axis_index("pcol")
    copies = [
        pltpu.make_async_copy(pat_one, pat.at[0], sems.at[0]),
        pltpu.make_async_copy(fac_one, fac.at[0], sems.at[1]),
        pltpu.make_async_copy(par, par_in, sems.at[2]),
        pltpu.make_async_copy(pat_two, pat.at[1], sems.at[3]),
        pltpu.make_async_copy(fac_two, fac.at[1], sems.at[4]),
    ]
    for copy in copies:
        copy.start()
    lanes = lax.broadcasted_iota(jnp.int32, (1, 64), 1)

    def turn(level, top):
        for i in range(4):
            cut = pl.ds(B * i, B)
            flags = jnp.where(lanes == 4 * row + i, pat[level, pl.ds(col, 1), :], 0)
            weight = jnp.sum(flags.astype(jnp.float32), axis=1, keepdims=True)
            own[top : top + 128, cut] = fac[level, cut, :].T * weight

    copies[0].wait()
    copies[1].wait()
    turn(0, 0)
    copies[2].wait()
    turned = par_in[...].T
    for i in range(4):
        own[128:160, B * i : B * i + B] = turned[32 * i : 32 * i + 32, :]
    copies[3].wait()
    copies[4].wait()
    turn(1, 160)


def prepare(pat_one, pat_two, fac_one, fac_two, par):
    return pl.pallas_call(
        prep_kernel,
        out_shape=f32(288, KA),
        in_specs=[HBM] * 5,
        out_specs=VMEM,
        scratch_shapes=[
            pltpu.VMEM((2, N, 64), jnp.int32),
            pltpu.VMEM((2, KA, B), jnp.float32),
            pltpu.VMEM((B, B), jnp.float32),
            pltpu.SemaphoreType.DMA((5,)),
        ],
        compiler_params=pltpu.CompilerParams(vmem_limit_bytes=56 * MIB),
    )(pat_one, pat_two, fac_one, fac_two, par)


def pair_up(own, other):
    def body(a, b, one, two, sems):
        copies = []
        for i, ref in enumerate((a, b)):
            copies.append(
                pltpu.make_async_copy(ref.at[pl.ds(0, 160)], one.at[i], sems.at[2 * i])
            )
            copies.append(
                pltpu.make_async_copy(ref.at[pl.ds(160, 128)], two.at[i], sems.at[2 * i + 1])
            )
        for copy in copies:
            copy.start()
        for copy in copies:
            copy.wait()

    return pl.pallas_call(
        body,
        out_shape=[f32(2, 160, KA), f32(2, B, KA)],
        in_specs=[HBM, ANY],
        out_specs=[VMEM] * 2,
        scratch_shapes=[pltpu.SemaphoreType.DMA((4,))],
        compiler_params=pltpu.CompilerParams(vmem_limit_bytes=4 * MIB),
    )(own, other)


def gather(pair):
    blocks = [pair]
    going = pair
    for step in range(4):
        if step == 3:
            going = going[0:1]
        going = ring(going)
        blocks += [going, swap(going)]
    return blocks


def place():
    row, col = lax.axis_index("prow"), lax.axis_index("pcol")
    core = lax.rem(col, 2)
    z = lax.div(col, 2)
    target = row ^ (core * 10)
    for bit, mask in enumerate(SPREAD):
        target = target ^ (lax.rem(lax.shift_right_logical(z, bit), 2) * mask)
    return row, col, core, target


def sources(refs):
    col = lax.axis_index("pcol")
    z, core = lax.div(col, 2), lax.rem(col, 2)
    found = []
    for at, ref in enumerate(refs):
        step = (at + 1) // 2
        swapped = at > 0 and at % 2 == 0
        side = (1 - core) if swapped else core
        away = jnp.where(side == 0, 8 - step, step)
        plane = lax.rem(z + away, 8)
        for i in range(ref.shape[0]):
            parity = side if i == 0 else 1 - side
            found.append((ref.at[i], plane * 2 + parity))
    return found


def fetch(refs, target, sems, first):
    return [
        pltpu.make_async_copy(source, target.at[m], sems.at[first + k])
        for k, (source, m) in enumerate(sources(refs))
    ]


def turn_kernel(parent, *refs):
    first, second, turn, sems = refs[:9], refs[9:18], refs[18], refs[19]
    row, col, core, target = place()
    wanted = ((first, parent[target]), (first, target), (second, target))
    for k, (blocks, which) in enumerate(wanted):
        for source, m in sources(blocks):

            @pl.when(m == which)
            def start():
                pltpu.make_async_copy(
                    source.at[pl.ds(0, 128)], turn.at[pl.ds(128 * k, 128)], sems.at[k]
                ).start()

    for k in range(3):
        part = turn.at[pl.ds(128 * k, 128)]
        pltpu.make_async_copy(part, part, sems.at[k]).wait()


def pick_turn(parent, first, second):
    return pl.pallas_call(
        turn_kernel,
        out_shape=f32(384, KA),
        in_specs=[SMEM] + [ANY] * 18,
        out_specs=VMEM,
        scratch_shapes=[pltpu.SemaphoreType.DMA((3,))],
        compiler_params=pltpu.CompilerParams(vmem_limit_bytes=4 * MIB),
        cost_estimate=pl.CostEstimate(flops=1000, bytes_accessed=1000, transcendentals=0),
    )(parent, *first, *second)


def products(ginv, level, at, row, core, half, left, outs):
    for variant in range(2):
        rows = pl.ds(64 * variant, 64)
        for slot in range(8):
            dest = destination(row, core, variant, slot + 8 * half)
            left[64 * slot : 64 * slot + 64, :] = level[dest, rows, :]
        value = dot_split(split(left[...]), ginv, ((1,), (0,)))
        outs[variant][:, 64 * at : 64 * at + 64, :] = -value.reshape(8, 64, KA)


def send_kernel(parent, ginv, turn, *refs):
    first, second, refs = refs[:9], refs[9:18], refs[18:]
    sends, one, two, left, block, sems = refs[0:2], *refs[2:]
    row, col, core, target = place()
    load = pltpu.make_async_copy(ginv, block, sems.at[32])
    low = fetch(first, one, sems, 0)
    high = fetch(second, two, sems, 16)
    for copy in [load] + low + high:
        copy.start()
    load.wait()
    ginv = split(block[...])
    for copy in low:
        copy.wait()
    products(ginv, one, 0, row, core, 1, left, sends)
    for copy in high:
        copy.wait()
    for m in range(16):
        par = split(unpack(one[m, 128:160, :]))
        two[m] = two[m] - dot_split(par, split(one[parent[m], 0:128, :]), ((1,), (0,)))
    products(ginv, two, 1, row, core, 1, left, sends)


def send_half(parent, ginv, turn, first, second):
    return pl.pallas_call(
        send_kernel,
        out_shape=[f32(8, B, KA)] * 2 + [f32(16, 160, KA), f32(16, B, KA)],
        in_specs=[SMEM, HBM] + [ANY] * 19,
        out_specs=[VMEM] * 4,
        scratch_shapes=[
            pltpu.VMEM((512, KA), jnp.float32),
            pltpu.VMEM((512, KA), jnp.float32),
            pltpu.SemaphoreType.DMA((33,)),
        ],
        compiler_params=pltpu.CompilerParams(vmem_limit_bytes=8 * MIB),
        cost_estimate=pl.CostEstimate(
            flops=20_000_000_000, bytes_accessed=1_000_000, transcendentals=0
        ),
    )(parent, ginv, turn, *first, *second)


def keep_half(parent, ginv, one, two, dinv_one, dinv_two, order):
    def body(parent, ginv, one, two, dinv_one, dinv_two, *refs):
        outs, refs = refs[len(order) : len(order) + 2], refs[len(order) + 2 :]
        par_out, base, left, dinv, sems = refs
        row, col, core, target = place()
        base_parts(parent, one, dinv_one, dinv_two, par_out, base, dinv, sems, row, core)
        ginv = split(ginv[...])
        products(ginv, one, 0, row, core, 0, left, outs)
        products(ginv, two, 1, row, core, 0, left, outs)

    return pl.pallas_call(
        body,
        out_shape=[f32(8, B, KA)] * 2 + [f32(B, B), f32(192, B)],
        in_specs=[SMEM] + [VMEM] * 3 + [HBM] * 2 + [ANY] * len(order),
        out_specs=[VMEM] * 4,
        scratch_shapes=[
            pltpu.VMEM((512, KA), jnp.float32),
            pltpu.VMEM((3, B, B), jnp.float32),
            pltpu.SemaphoreType.DMA((3,)),
        ],
        compiler_params=pltpu.CompilerParams(vmem_limit_bytes=8 * MIB),
        cost_estimate=pl.CostEstimate(
            flops=60_000_000_000, bytes_accessed=1_000_000, transcendentals=0
        ),
    )(parent, ginv, one, two, dinv_one, dinv_two, *order)


def base_parts(parent, one, dinv_one, dinv_two, par_out, base, dinv, sems, row, core):
    top = pl.multiple_of(core * 64, 64)
    sources = (
        dinv_one.at[pl.ds(pl.multiple_of(row * B, B), B)],
        dinv_one.at[pl.ds(pl.multiple_of(parent[row] * B, B), B)],
        dinv_two,
    )
    copies = [
        pltpu.make_async_copy(source, dinv.at[i], sems.at[i]) for i, source in enumerate(sources)
    ]
    for copy in copies:
        copy.start()
    par_out[...] = unpack(one[row, 128:160, :])
    for copy in copies:
        copy.wait()
    base[0:64, :] = dinv[0, pl.ds(top, 64), :]
    base[64:128, :] = -jnp.dot(
        par_out[pl.ds(top, 64), :],
        dinv[1],
        precision=lax.Precision.HIGHEST,
        preferred_element_type=jnp.float32,
    )
    base[128:192, :] = dinv[2, pl.ds(top, 64), :]


def row_step(value, variant, step):
    return permute(value, lambda r, c: (r ^ MASKS[c % 2][variant][step], c))


def block_kernel(a_ref, b_ref, turn, one_out, two_out, send_out, keep_out, sums):
    core = lax.rem(lax.axis_index("pcol"), 2)
    for variant, ref in enumerate((a_ref, b_ref)):
        one_out[64 * variant : 64 * variant + 64, :] = ref[0:64, :]
        two_out[64 * variant : 64 * variant + 64, :] = ref[64:128, :]
    one = split(one_out[...])
    two = split(two_out[...])
    nt = ((1,), (1,))
    for i, (left, right) in enumerate(
        ((one, turn[128:256, :]), (two, turn[0:128, :]), (two, turn[256:384, :]))
    ):
        value = dot_split(left, split(right), nt)
        sums[0, 64 * i : 64 * i + 64, :] = value[0:64]
        sums[1, 64 * i : 64 * i + 64, :] = value[64:128]
    keep_out[...] = sums[core]
    send_out[...] = sums[1 - core]


def blocks_of(parts, turn):
    return pl.pallas_call(
        block_kernel,
        out_shape=[f32(B, KA), f32(B, KA), f32(192, B), f32(192, B)],
        in_specs=[VMEM] * 3,
        out_specs=[VMEM] * 4,
        scratch_shapes=[pltpu.VMEM((2, 192, B), jnp.float32)],
        compiler_params=pltpu.CompilerParams(vmem_limit_bytes=8 * MIB),
    )(*parts, turn)


def add(part, kept, got, order=()):
    half = kept.shape[0] // 2

    def body(a, b, *refs):
        out = refs[-1]
        if half == 0:
            out[...] = a[0] + b[0]
        else:
            at = pl.ds(half * part, half)
            out[...] = a[at] + b[at]

    return pl.pallas_call(
        body,
        out_shape=f32(half, B, KA) if half else f32(B, KA),
        in_specs=[VMEM] * 2 + [ANY] * len(order),
        out_specs=VMEM,
        compiler_params=pltpu.CompilerParams(vmem_limit_bytes=8 * MIB),
        cost_estimate=pl.CostEstimate(flops=300_000, bytes_accessed=1_000_000, transcendentals=0),
    )(kept, got, *order)


def final_kernel(base, par, first, second, out):
    total = first[...] + second[...]
    out[0:64, :] = base[0:64, :] - total[0:64, :]
    cross = base[64:128, :] - total[64:128, :]
    out[64:128, :] = cross
    out[128:192, :] = base[128:192, :] - (
        total[128:192, :]
        + lax.dot_general(
            cross,
            par[...],
            (((1,), (1,)), ((), ())),
            precision=lax.Precision.HIGHEST,
            preferred_element_type=jnp.float32,
        )
    )


def final_of(base, par, first, second):
    return pl.pallas_call(
        final_kernel,
        out_shape=f32(192, B),
        in_specs=[VMEM] * 4,
        out_specs=VMEM,
        compiler_params=pltpu.CompilerParams(vmem_limit_bytes=4 * MIB),
    )(base, par, first, second)


def join_kernel(own, other, a_out, b_out, c_out):
    core = lax.rem(lax.axis_index("pcol"), 2)
    mine = pl.multiple_of(core * 64, 64)
    rest = pl.multiple_of((1 - core) * 64, 64)
    for i, out in enumerate((a_out, b_out, c_out)):
        out[pl.ds(mine, 64), :] = own[64 * i : 64 * i + 64, :]
        out[pl.ds(rest, 64), :] = other[64 * i : 64 * i + 64, :]


def join(own, other):
    return pl.pallas_call(
        join_kernel,
        out_shape=[f32(B, B)] * 3,
        in_specs=[VMEM] * 2,
        out_specs=[VMEM] * 3,
        compiler_params=pltpu.CompilerParams(vmem_limit_bytes=4 * MIB),
    )(own, other)


def local(
    ginv_anc,
    factor_one,
    pattern_one,
    dinv_one,
    factor_two,
    factor_parent,
    pattern_two,
    parent,
    dinv_two,
):
    own = prepare(pattern_one.T, pattern_two.T, factor_one, factor_two, factor_parent)
    pair_one, pair_two = pair_up(own, swap(own))
    blocks_one = gather(pair_one)
    blocks_two = gather(pair_two)
    turn = pick_turn(parent, blocks_one, blocks_two)
    send_a, send_b, one, two = send_half(parent, ginv_anc, turn, blocks_one, blocks_two)
    turn = permute(turn, lambda r, c: (r ^ spread_mask(c), c))
    got = [row_step(send_a, 0, 0), row_step(send_b, 1, 0)]
    keep_a, keep_b, par, base = keep_half(
        parent, ginv_anc, one, two, dinv_one, dinv_two, [turn]
    )
    kept = [keep_a, keep_b]
    turn = permute(turn, lambda r, c: (r, r ^ spread_mask(c)))
    for step in range(1, 4):
        order = [turn] if step == 1 else []
        going = [add(1, kept[0], got[0], order), add(1, kept[1], got[1], [])]
        kept = [add(0, kept[v], got[v]) for v in range(2)]
        got = [row_step(going[v], v, step) for v in range(2)]
    kept = [add(0, kept[v], got[v]) for v in range(2)]
    anc_one, anc_two, send, keep = blocks_of(kept, turn)
    sums = keep + swap(send)
    for mask in (2, 6):
        sums = sums + permute(sums, lambda r, c: (r, c ^ mask))
    done = final_of(base, par, sums, permute(sums, lambda r, c: (r, c ^ 14)))
    diag_one, cross, diag_two = join(done, swap(done))
    return anc_one, diag_one, anc_two, cross, diag_two


def solution(mesh):
    return jax.shard_map(
        local,
        mesh=mesh,
        in_specs=(
            P("prow", "pcol"),
            P("prow", "pcol"),
            P(),
            P(),
            P("prow", "pcol"),
            P(None, "pcol"),
            P(),
            P(),
            P("prow", None),
        ),
        out_specs=(
            P("prow", "pcol"),
            P("prow", None),
            P("prow", "pcol"),
            P("prow", None),
            P("prow", None),
        ),
        check_vma=False,
    )
```

```python
import jax
import jax.numpy as jnp
from jax import lax
from jax.experimental import pallas as pl
from jax.experimental.pallas import tpu as pltpu
from jax.sharding import PartitionSpec as P

N = 16
B = 128
KA = 512
ALL = ("prow", "pcol")
MASKS = (((1, 3, 4, 12), (3, 1, 12, 4)), ((4, 12, 1, 3), (12, 4, 3, 1)))
SPREAD = (1, 6, 2)
VMEM = pl.BlockSpec(memory_space=pltpu.VMEM)
SMEM = pl.BlockSpec(memory_space=pltpu.SMEM)
ANY = pl.BlockSpec(memory_space=pl.ANY)
HBM = pl.BlockSpec(memory_space=pltpu.HBM)
MIB = 1024 * 1024


def f32(*shape):
    return jax.ShapeDtypeStruct(shape, jnp.float32)


def slot_mask(core, variant, slot):
    mask = 0
    for bit in range(4):
        if (slot >> (3 - bit)) & 1:
            mask ^= MASKS[core][variant][bit]
    return mask


def destination(row, core, variant, slot):
    first, second = slot_mask(0, variant, slot), slot_mask(1, variant, slot)
    return row ^ jnp.where(core == 0, first, second)


def split(value):
    high = value.astype(jnp.bfloat16)
    low = (value - high.astype(jnp.float32)).astype(jnp.bfloat16)
    return high, low


def dot_split(left, right, dims):
    out = None
    for a, b in ((left[0], right[0]), (left[0], right[1]), (left[1], right[0])):
        term = lax.dot_general(a, b, (dims, ((), ())), preferred_element_type=jnp.float32)
        out = term if out is None else out + term
    return out


def unpack(packed):
    return jnp.concatenate([packed[:, B * i : B * i + B] for i in range(4)], axis=0)


def permute(value, move):
    pairs = []
    for r in range(N):
        for c in range(N):
            nr, nc = move(r, c)
            pairs.append((r * N + c, nr * N + nc))
    return lax.ppermute(value, ALL, pairs)


def swap(value):
    return permute(value, lambda r, c: (r, c ^ 1))


def ring(value):
    return permute(value, lambda r, c: (r, (c + (2 if c % 2 == 0 else -2)) % N))


def spread_mask(col):
    mask = 10 if col % 2 else 0
    for bit, part in enumerate(SPREAD):
        if ((col // 2) >> bit) & 1:
            mask ^= part
    return mask


def prep_kernel(pat_one, pat_two, fac_one, fac_two, par, own, pat, fac, par_in, sems):
    row, col = lax.axis_index("prow"), lax.axis_index("pcol")
    copies = [
        pltpu.make_async_copy(pat_one, pat.at[0], sems.at[0]),
        pltpu.make_async_copy(fac_one, fac.at[0], sems.at[1]),
        pltpu.make_async_copy(par, par_in, sems.at[2]),
        pltpu.make_async_copy(pat_two, pat.at[1], sems.at[3]),
        pltpu.make_async_copy(fac_two, fac.at[1], sems.at[4]),
    ]
    for copy in copies:
        copy.start()
    lanes = lax.broadcasted_iota(jnp.int32, (1, 64), 1)

    def turn(level, top):
        for i in range(4):
            cut = pl.ds(B * i, B)
            flags = jnp.where(lanes == 4 * row + i, pat[level, pl.ds(col, 1), :], 0)
            weight = jnp.sum(flags.astype(jnp.float32), axis=1, keepdims=True)
            own[top : top + 128, cut] = fac[level, cut, :].T * weight

    copies[0].wait()
    copies[1].wait()
    turn(0, 0)
    copies[2].wait()
    turned = par_in[...].T
    for i in range(4):
        own[128:160, B * i : B * i + B] = turned[32 * i : 32 * i + 32, :]
    copies[3].wait()
    copies[4].wait()
    turn(1, 160)


def prepare(pat_one, pat_two, fac_one, fac_two, par):
    return pl.pallas_call(
        prep_kernel,
        out_shape=f32(288, KA),
        in_specs=[HBM] * 5,
        out_specs=VMEM,
        scratch_shapes=[
            pltpu.VMEM((2, N, 64), jnp.int32),
            pltpu.VMEM((2, KA, B), jnp.float32),
            pltpu.VMEM((B, B), jnp.float32),
            pltpu.SemaphoreType.DMA((5,)),
        ],
        compiler_params=pltpu.CompilerParams(vmem_limit_bytes=56 * MIB),
    )(pat_one, pat_two, fac_one, fac_two, par)


def gather(block, steps):
    blocks = [block]
    for _ in range(steps):
        block = ring(block)
        blocks += [block, swap(block)]
    return blocks


def stage(own):
    def body(source, out, sem):
        copy = pltpu.make_async_copy(source, out, sem)
        copy.start()
        copy.wait()

    return pl.pallas_call(
        body,
        out_shape=f32(288, KA),
        in_specs=[ANY],
        out_specs=VMEM,
        scratch_shapes=[pltpu.SemaphoreType.DMA],
        compiler_params=pltpu.CompilerParams(vmem_limit_bytes=4 * MIB),
        cost_estimate=pl.CostEstimate(flops=1000, bytes_accessed=1000, transcendentals=0),
    )(own)


def place():
    row, col = lax.axis_index("prow"), lax.axis_index("pcol")
    core = lax.rem(col, 2)
    z = lax.div(col, 2)
    target = row ^ (core * 10)
    for bit, mask in enumerate(SPREAD):
        target = target ^ (lax.rem(lax.shift_right_logical(z, bit), 2) * mask)
    return row, col, core, target


def sources(own, other, start, rows):
    col = lax.axis_index("pcol")
    z, core = lax.div(col, 2), lax.rem(col, 2)
    found = []
    for sibling, refs in enumerate((own, other)):
        for at, ref in enumerate(refs):
            step = (at + 1) // 2
            swapped = at > 0 and at % 2 == 0
            side = (1 - core) if swapped else core
            away = jnp.where(side == 0, 8 - step, step)
            plane = lax.rem(z + away, 8)
            parity = (1 - side) if sibling else side
            found.append((ref.at[pl.ds(start, rows)], plane * 2 + parity))
    return found


def fetch(own, other, start, rows, target, sems, first):
    return [
        pltpu.make_async_copy(source, target.at[m], sems.at[first + k])
        for k, (source, m) in enumerate(sources(own, other, start, rows))
    ]


def turn_kernel(parent, *refs):
    own, other, turn, sems = refs[:7], refs[7:16], refs[16], refs[17]
    row, col, core, target = place()
    for k, (start_row, which) in enumerate(((0, parent[target]), (0, target), (160, target))):
        for source, m in sources(own, other, start_row, B):

            @pl.when(m == which)
            def start():
                pltpu.make_async_copy(source, turn.at[pl.ds(B * k, B)], sems.at[k]).start()

    for k in range(3):
        part = turn.at[pl.ds(B * k, B)]
        pltpu.make_async_copy(part, part, sems.at[k]).wait()


def pick_turn(parent, own, other):
    return pl.pallas_call(
        turn_kernel,
        out_shape=f32(384, KA),
        in_specs=[SMEM] + [ANY] * 16,
        out_specs=VMEM,
        scratch_shapes=[pltpu.SemaphoreType.DMA((3,))],
        compiler_params=pltpu.CompilerParams(vmem_limit_bytes=4 * MIB),
        cost_estimate=pl.CostEstimate(flops=1000, bytes_accessed=1000, transcendentals=0),
    )(parent, *own, *other)


def products(ginv, level, at, row, core, half, left, outs):
    for variant in range(2):
        rows = pl.ds(64 * variant, 64)
        for slot in range(8):
            dest = destination(row, core, variant, slot + 8 * half)
            left[64 * slot : 64 * slot + 64, :] = level[dest, rows, :]
        value = dot_split(split(left[...]), ginv, ((1,), (0,)))
        outs[variant][:, 64 * at : 64 * at + 64, :] = -value.reshape(8, 64, KA)


def send_kernel(parent, ginv, turn, *refs):
    own, other, refs = refs[:7], refs[7:16], refs[16:]
    sends, one, two, left, block, sems = refs[0:2], *refs[2:]
    row, col, core, target = place()
    load = pltpu.make_async_copy(ginv, block, sems.at[32])
    low = fetch(own, other, 0, 160, one, sems, 0)
    high = fetch(own, other, 160, B, two, sems, 16)
    for copy in [load] + low + high:
        copy.start()
    load.wait()
    ginv = split(block[...])
    for copy in low:
        copy.wait()
    products(ginv, one, 0, row, core, 1, left, sends)
    for copy in high:
        copy.wait()
    for m in range(16):
        par = split(unpack(one[m, 128:160, :]))
        two[m] = two[m] - dot_split(par, split(one[parent[m], 0:128, :]), ((1,), (0,)))
    products(ginv, two, 1, row, core, 1, left, sends)


def send_half(parent, ginv, turn, first, second):
    return pl.pallas_call(
        send_kernel,
        out_shape=[f32(8, B, KA)] * 2 + [f32(16, 160, KA), f32(16, B, KA)],
        in_specs=[SMEM, HBM] + [ANY] * 17,
        out_specs=[VMEM] * 4,
        scratch_shapes=[
            pltpu.VMEM((512, KA), jnp.float32),
            pltpu.VMEM((512, KA), jnp.float32),
            pltpu.SemaphoreType.DMA((33,)),
        ],
        compiler_params=pltpu.CompilerParams(vmem_limit_bytes=8 * MIB),
        cost_estimate=pl.CostEstimate(
            flops=20_000_000_000, bytes_accessed=1_000_000, transcendentals=0
        ),
    )(parent, ginv, turn, *first, *second)


def keep_half(parent, ginv, one, two, dinv_one, dinv_two, order):
    def body(parent, ginv, one, two, dinv_one, dinv_two, *refs):
        outs, refs = refs[len(order) : len(order) + 2], refs[len(order) + 2 :]
        par_out, base, left, dinv, sems = refs
        row, col, core, target = place()
        base_parts(parent, one, dinv_one, dinv_two, par_out, base, dinv, sems, row, core)
        ginv = split(ginv[...])
        products(ginv, one, 0, row, core, 0, left, outs)
        products(ginv, two, 1, row, core, 0, left, outs)

    return pl.pallas_call(
        body,
        out_shape=[f32(8, B, KA)] * 2 + [f32(B, B), f32(192, B)],
        in_specs=[SMEM] + [VMEM] * 3 + [HBM] * 2 + [ANY] * len(order),
        out_specs=[VMEM] * 4,
        scratch_shapes=[
            pltpu.VMEM((512, KA), jnp.float32),
            pltpu.VMEM((3, B, B), jnp.float32),
            pltpu.SemaphoreType.DMA((3,)),
        ],
        compiler_params=pltpu.CompilerParams(vmem_limit_bytes=8 * MIB),
        cost_estimate=pl.CostEstimate(
            flops=60_000_000_000, bytes_accessed=1_000_000, transcendentals=0
        ),
    )(parent, ginv, one, two, dinv_one, dinv_two, *order)


def base_parts(parent, one, dinv_one, dinv_two, par_out, base, dinv, sems, row, core):
    top = pl.multiple_of(core * 64, 64)
    sources = (
        dinv_one.at[pl.ds(pl.multiple_of(row * B, B), B)],
        dinv_one.at[pl.ds(pl.multiple_of(parent[row] * B, B), B)],
        dinv_two,
    )
    copies = [
        pltpu.make_async_copy(source, dinv.at[i], sems.at[i]) for i, source in enumerate(sources)
    ]
    for copy in copies:
        copy.start()
    par_out[...] = unpack(one[row, 128:160, :])
    for copy in copies:
        copy.wait()
    base[0:64, :] = dinv[0, pl.ds(top, 64), :]
    base[64:128, :] = -jnp.dot(
        par_out[pl.ds(top, 64), :],
        dinv[1],
        precision=lax.Precision.HIGHEST,
        preferred_element_type=jnp.float32,
    )
    base[128:192, :] = dinv[2, pl.ds(top, 64), :]


def row_step(value, variant, step):
    return permute(value, lambda r, c: (r ^ MASKS[c % 2][variant][step], c))


def block_kernel(a_ref, b_ref, turn, one_out, two_out, send_out, keep_out, sums):
    core = lax.rem(lax.axis_index("pcol"), 2)
    for variant, ref in enumerate((a_ref, b_ref)):
        one_out[64 * variant : 64 * variant + 64, :] = ref[0:64, :]
        two_out[64 * variant : 64 * variant + 64, :] = ref[64:128, :]
    one = split(one_out[...])
    two = split(two_out[...])
    nt = ((1,), (1,))
    for i, (left, right) in enumerate(
        ((one, turn[128:256, :]), (two, turn[0:128, :]), (two, turn[256:384, :]))
    ):
        value = dot_split(left, split(right), nt)
        sums[0, 64 * i : 64 * i + 64, :] = value[0:64]
        sums[1, 64 * i : 64 * i + 64, :] = value[64:128]
    keep_out[...] = sums[core]
    send_out[...] = sums[1 - core]


def blocks_of(parts, turn):
    return pl.pallas_call(
        block_kernel,
        out_shape=[f32(B, KA), f32(B, KA), f32(192, B), f32(192, B)],
        in_specs=[VMEM] * 3,
        out_specs=[VMEM] * 4,
        scratch_shapes=[pltpu.VMEM((2, 192, B), jnp.float32)],
        compiler_params=pltpu.CompilerParams(vmem_limit_bytes=8 * MIB),
    )(*parts, turn)


def add(part, kept, got, order=()):
    half = kept.shape[0] // 2

    def body(a, b, *refs):
        out = refs[-1]
        if half == 0:
            out[...] = a[0] + b[0]
        else:
            at = pl.ds(half * part, half)
            out[...] = a[at] + b[at]

    return pl.pallas_call(
        body,
        out_shape=f32(half, B, KA) if half else f32(B, KA),
        in_specs=[VMEM] * 2 + [ANY] * len(order),
        out_specs=VMEM,
        compiler_params=pltpu.CompilerParams(vmem_limit_bytes=8 * MIB),
        cost_estimate=pl.CostEstimate(flops=300_000, bytes_accessed=1_000_000, transcendentals=0),
    )(kept, got, *order)


def final_kernel(base, par, first, second, out):
    total = first[...] + second[...]
    out[0:64, :] = base[0:64, :] - total[0:64, :]
    cross = base[64:128, :] - total[64:128, :]
    out[64:128, :] = cross
    out[128:192, :] = base[128:192, :] - (
        total[128:192, :]
        + lax.dot_general(
            cross,
            par[...],
            (((1,), (1,)), ((), ())),
            precision=lax.Precision.HIGHEST,
            preferred_element_type=jnp.float32,
        )
    )


def final_of(base, par, first, second):
    return pl.pallas_call(
        final_kernel,
        out_shape=f32(192, B),
        in_specs=[VMEM] * 4,
        out_specs=VMEM,
        compiler_params=pltpu.CompilerParams(vmem_limit_bytes=4 * MIB),
    )(base, par, first, second)


def join_kernel(own, other, a_out, b_out, c_out):
    core = lax.rem(lax.axis_index("pcol"), 2)
    mine = pl.multiple_of(core * 64, 64)
    rest = pl.multiple_of((1 - core) * 64, 64)
    for i, out in enumerate((a_out, b_out, c_out)):
        out[pl.ds(mine, 64), :] = own[64 * i : 64 * i + 64, :]
        out[pl.ds(rest, 64), :] = other[64 * i : 64 * i + 64, :]


def join(own, other):
    return pl.pallas_call(
        join_kernel,
        out_shape=[f32(B, B)] * 3,
        in_specs=[VMEM] * 2,
        out_specs=[VMEM] * 3,
        compiler_params=pltpu.CompilerParams(vmem_limit_bytes=4 * MIB),
    )(own, other)


def local(
    ginv_anc,
    factor_one,
    pattern_one,
    dinv_one,
    factor_two,
    factor_parent,
    pattern_two,
    parent,
    dinv_two,
):
    own = prepare(pattern_one.T, pattern_two.T, factor_one, factor_two, factor_parent)
    blocks_own = gather(stage(own), 3)
    blocks_other = gather(swap(own), 4)
    turn = pick_turn(parent, blocks_own, blocks_other)
    send_a, send_b, one, two = send_half(parent, ginv_anc, turn, blocks_own, blocks_other)
    turn = permute(turn, lambda r, c: (r ^ spread_mask(c), c))
    got = [row_step(send_a, 0, 0), row_step(send_b, 1, 0)]
    keep_a, keep_b, par, base = keep_half(
        parent, ginv_anc, one, two, dinv_one, dinv_two, [turn]
    )
    kept = [keep_a, keep_b]
    turn = permute(turn, lambda r, c: (r, r ^ spread_mask(c)))
    for step in range(1, 4):
        order = [turn] if step == 3 else []
        going = [add(1, kept[0], got[0]), add(1, kept[1], got[1], order)]
        kept = [add(0, kept[v], got[v]) for v in range(2)]
        got = [row_step(going[v], v, step) for v in range(2)]
    kept = [add(0, kept[v], got[v]) for v in range(2)]
    anc_one, anc_two, send, keep = blocks_of(kept, turn)
    sums = keep + swap(send)
    for mask in (2, 6):
        sums = sums + permute(sums, lambda r, c: (r, c ^ mask))
    done = final_of(base, par, sums, permute(sums, lambda r, c: (r, c ^ 14)))
    diag_one, cross, diag_two = join(done, swap(done))
    return anc_one, diag_one, anc_two, cross, diag_two


def solution(mesh):
    return jax.shard_map(
        local,
        mesh=mesh,
        in_specs=(
            P("prow", "pcol"),
            P("prow", "pcol"),
            P(),
            P(),
            P("prow", "pcol"),
            P(None, "pcol"),
            P(),
            P(),
            P("prow", None),
        ),
        out_specs=(
            P("prow", "pcol"),
            P("prow", None),
            P("prow", "pcol"),
            P("prow", None),
            P("prow", None),
        ),
        check_vma=False,
    )
```

```python
import jax
import jax.numpy as jnp
from jax import lax
from jax.experimental import pallas as pl
from jax.experimental.pallas import tpu as pltpu
from jax.sharding import PartitionSpec as P

N = 16
B = 128
KA = 512
ALL = ("prow", "pcol")
MASKS = (((1, 3, 4, 12), (3, 1, 12, 4)), ((4, 12, 1, 3), (12, 4, 3, 1)))
SPREAD = (1, 6, 2)
VMEM = pl.BlockSpec(memory_space=pltpu.VMEM)
SMEM = pl.BlockSpec(memory_space=pltpu.SMEM)
ANY = pl.BlockSpec(memory_space=pl.ANY)
HBM = pl.BlockSpec(memory_space=pltpu.HBM)
MIB = 1024 * 1024


def f32(*shape):
    return jax.ShapeDtypeStruct(shape, jnp.float32)


def slot_mask(core, variant, slot):
    mask = 0
    for bit in range(4):
        if (slot >> (3 - bit)) & 1:
            mask ^= MASKS[core][variant][bit]
    return mask


def destination(row, core, variant, slot):
    first, second = slot_mask(0, variant, slot), slot_mask(1, variant, slot)
    return row ^ jnp.where(core == 0, first, second)


def split(value):
    high = value.astype(jnp.bfloat16)
    low = (value - high.astype(jnp.float32)).astype(jnp.bfloat16)
    return high, low


def dot_split(left, right, dims):
    out = None
    for a, b in ((left[0], right[0]), (left[0], right[1]), (left[1], right[0])):
        term = lax.dot_general(a, b, (dims, ((), ())), preferred_element_type=jnp.float32)
        out = term if out is None else out + term
    return out


def unpack(packed):
    return jnp.concatenate([packed[:, B * i : B * i + B] for i in range(4)], axis=0)


def permute(value, move):
    pairs = []
    for r in range(N):
        for c in range(N):
            nr, nc = move(r, c)
            pairs.append((r * N + c, nr * N + nc))
    return lax.ppermute(value, ALL, pairs)


def swap(value):
    return permute(value, lambda r, c: (r, c ^ 1))


def ring(value):
    return permute(value, lambda r, c: (r, (c + (2 if c % 2 == 0 else -2)) % N))


def spread_mask(col):
    mask = 10 if col % 2 else 0
    for bit, part in enumerate(SPREAD):
        if ((col // 2) >> bit) & 1:
            mask ^= part
    return mask


def prep_kernel(pat_one, pat_two, fac_one, fac_two, par, own, pat, fac, par_in, sems):
    row, col = lax.axis_index("prow"), lax.axis_index("pcol")
    copies = [
        pltpu.make_async_copy(pat_one, pat.at[0], sems.at[0]),
        pltpu.make_async_copy(fac_one, fac.at[0], sems.at[1]),
        pltpu.make_async_copy(par, par_in, sems.at[2]),
        pltpu.make_async_copy(pat_two, pat.at[1], sems.at[3]),
        pltpu.make_async_copy(fac_two, fac.at[1], sems.at[4]),
    ]
    for copy in copies:
        copy.start()
    lanes = lax.broadcasted_iota(jnp.int32, (1, 64), 1)

    def turn(level, top):
        for i in range(4):
            cut = pl.ds(B * i, B)
            flags = jnp.where(lanes == 4 * row + i, pat[level, pl.ds(col, 1), :], 0)
            weight = jnp.sum(flags.astype(jnp.float32), axis=1, keepdims=True)
            own[top : top + 128, cut] = fac[level, cut, :].T * weight

    copies[0].wait()
    copies[1].wait()
    turn(0, 0)
    copies[2].wait()
    turned = par_in[...].T
    for i in range(4):
        own[128:160, B * i : B * i + B] = turned[32 * i : 32 * i + 32, :]
    copies[3].wait()
    copies[4].wait()
    turn(1, 160)


def prepare(pat_one, pat_two, fac_one, fac_two, par):
    return pl.pallas_call(
        prep_kernel,
        out_shape=f32(288, KA),
        in_specs=[HBM] * 5,
        out_specs=VMEM,
        scratch_shapes=[
            pltpu.VMEM((2, N, 64), jnp.int32),
            pltpu.VMEM((2, KA, B), jnp.float32),
            pltpu.VMEM((B, B), jnp.float32),
            pltpu.SemaphoreType.DMA((5,)),
        ],
        compiler_params=pltpu.CompilerParams(vmem_limit_bytes=56 * MIB),
    )(pat_one, pat_two, fac_one, fac_two, par)


def gather(block, steps):
    blocks = [block]
    for _ in range(steps):
        block = ring(block)
        blocks += [block, swap(block)]
    return blocks


def stage(own):
    def body(source, out, sem):
        copy = pltpu.make_async_copy(source, out, sem)
        copy.start()
        copy.wait()

    return pl.pallas_call(
        body,
        out_shape=f32(288, KA),
        in_specs=[ANY],
        out_specs=VMEM,
        scratch_shapes=[pltpu.SemaphoreType.DMA],
        compiler_params=pltpu.CompilerParams(vmem_limit_bytes=4 * MIB),
        cost_estimate=pl.CostEstimate(flops=1000, bytes_accessed=1000, transcendentals=0),
    )(own)


def place():
    row, col = lax.axis_index("prow"), lax.axis_index("pcol")
    core = lax.rem(col, 2)
    z = lax.div(col, 2)
    target = row ^ (core * 10)
    for bit, mask in enumerate(SPREAD):
        target = target ^ (lax.rem(lax.shift_right_logical(z, bit), 2) * mask)
    return row, col, core, target


def sources(own, other, start, rows):
    col = lax.axis_index("pcol")
    z, core = lax.div(col, 2), lax.rem(col, 2)
    found = []
    for sibling, refs in enumerate((own, other)):
        for at, ref in enumerate(refs):
            step = (at + 1) // 2
            swapped = at > 0 and at % 2 == 0
            side = (1 - core) if swapped else core
            away = jnp.where(side == 0, 8 - step, step)
            plane = lax.rem(z + away, 8)
            parity = (1 - side) if sibling else side
            found.append((ref.at[pl.ds(start, rows)], plane * 2 + parity))
    return found


def fetch(own, other, start, rows, target, sems, first):
    return [
        pltpu.make_async_copy(source, target.at[m], sems.at[first + k])
        for k, (source, m) in enumerate(sources(own, other, start, rows))
    ]


def turn_kernel(parent, *refs):
    own, other, turn, sems = refs[:7], refs[7:16], refs[16], refs[17]
    row, col, core, target = place()
    for k, (start_row, which) in enumerate(((0, parent[target]), (0, target), (160, target))):
        for source, m in sources(own, other, start_row, B):

            @pl.when(m == which)
            def start():
                pltpu.make_async_copy(source, turn.at[pl.ds(B * k, B)], sems.at[k]).start()

    for k in range(3):
        part = turn.at[pl.ds(B * k, B)]
        pltpu.make_async_copy(part, part, sems.at[k]).wait()


def pick_turn(parent, own, other):
    return pl.pallas_call(
        turn_kernel,
        out_shape=f32(384, KA),
        in_specs=[SMEM] + [ANY] * 16,
        out_specs=VMEM,
        scratch_shapes=[pltpu.SemaphoreType.DMA((3,))],
        compiler_params=pltpu.CompilerParams(vmem_limit_bytes=4 * MIB),
        cost_estimate=pl.CostEstimate(flops=1000, bytes_accessed=1000, transcendentals=0),
    )(parent, *own, *other)


def products(ginv, level, at, row, core, half, left, outs):
    for variant in range(2):
        rows = pl.ds(64 * variant, 64)
        for slot in range(8):
            dest = destination(row, core, variant, slot + 8 * half)
            left[64 * slot : 64 * slot + 64, :] = level[dest, rows, :]
        value = dot_split(split(left[...]), ginv, ((1,), (0,)))
        outs[variant][:, 64 * at : 64 * at + 64, :] = -value.reshape(8, 64, KA)


def send_kernel(parent, ginv, turn, *refs):
    own, other, refs = refs[:7], refs[7:16], refs[16:]
    sends, one, two, left, block, sems = refs[0:2], *refs[2:]
    row, col, core, target = place()
    load = pltpu.make_async_copy(ginv, block, sems.at[32])
    low = fetch(own, other, 0, 160, one, sems, 0)
    high = fetch(own, other, 160, B, two, sems, 16)
    for copy in [load] + low + high:
        copy.start()
    load.wait()
    ginv = split(block[...])
    for copy in low:
        copy.wait()
    products(ginv, one, 0, row, core, 1, left, sends)
    for copy in high:
        copy.wait()
    for m in range(16):
        par = split(unpack(one[m, 128:160, :]))
        two[m] = two[m] - dot_split(par, split(one[parent[m], 0:128, :]), ((1,), (0,)))
    products(ginv, two, 1, row, core, 1, left, sends)


def send_half(parent, ginv, turn, first, second):
    return pl.pallas_call(
        send_kernel,
        out_shape=[f32(8, B, KA)] * 2 + [f32(16, 160, KA), f32(16, B, KA)],
        in_specs=[SMEM, HBM] + [ANY] * 17,
        out_specs=[VMEM] * 4,
        scratch_shapes=[
            pltpu.VMEM((512, KA), jnp.float32),
            pltpu.VMEM((512, KA), jnp.float32),
            pltpu.SemaphoreType.DMA((33,)),
        ],
        compiler_params=pltpu.CompilerParams(vmem_limit_bytes=8 * MIB),
        cost_estimate=pl.CostEstimate(
            flops=20_000_000_000, bytes_accessed=1_000_000, transcendentals=0
        ),
    )(parent, ginv, turn, *first, *second)


def keep_half(parent, ginv, one, two, dinv_one, dinv_two, order):
    def body(parent, ginv, one, two, dinv_one, dinv_two, *refs):
        outs, refs = refs[len(order) : len(order) + 2], refs[len(order) + 2 :]
        par_out, base, left, dinv, sems = refs
        row, col, core, target = place()
        base_parts(parent, one, dinv_one, dinv_two, par_out, base, dinv, sems, row, core)
        ginv = split(ginv[...])
        products(ginv, one, 0, row, core, 0, left, outs)
        products(ginv, two, 1, row, core, 0, left, outs)

    return pl.pallas_call(
        body,
        out_shape=[f32(8, B, KA)] * 2 + [f32(B, B), f32(384, B)],
        in_specs=[SMEM] + [VMEM] * 3 + [HBM] * 2 + [ANY] * len(order),
        out_specs=[VMEM] * 4,
        scratch_shapes=[
            pltpu.VMEM((512, KA), jnp.float32),
            pltpu.VMEM((3, B, B), jnp.float32),
            pltpu.SemaphoreType.DMA((3,)),
        ],
        compiler_params=pltpu.CompilerParams(vmem_limit_bytes=8 * MIB),
        cost_estimate=pl.CostEstimate(
            flops=60_000_000_000, bytes_accessed=1_000_000, transcendentals=0
        ),
    )(parent, ginv, one, two, dinv_one, dinv_two, *order)


def base_parts(parent, one, dinv_one, dinv_two, par_out, base, dinv, sems, row, core):
    sources = (
        dinv_one.at[pl.ds(pl.multiple_of(row * B, B), B)],
        dinv_one.at[pl.ds(pl.multiple_of(parent[row] * B, B), B)],
        dinv_two,
    )
    copies = [
        pltpu.make_async_copy(source, dinv.at[i], sems.at[i]) for i, source in enumerate(sources)
    ]
    for copy in copies:
        copy.start()
    par_out[...] = unpack(one[row, 128:160, :])
    for copy in copies:
        copy.wait()
    base[0:128, :] = dinv[0]
    side = -jnp.dot(
        par_out[...],
        dinv[1],
        precision=lax.Precision.HIGHEST,
        preferred_element_type=jnp.float32,
    )
    base[128:256, :] = side
    base[256:384, :] = dinv[2] - lax.dot_general(
        side,
        par_out[...],
        (((1,), (1,)), ((), ())),
        precision=lax.Precision.HIGHEST,
        preferred_element_type=jnp.float32,
    )


def row_step(value, variant, step):
    return permute(value, lambda r, c: (r ^ MASKS[c % 2][variant][step], c))


def block_kernel(a_ref, b_ref, turn, par, one_out, two_out, send_out, keep_out, sums):
    core = lax.rem(lax.axis_index("pcol"), 2)
    for variant, ref in enumerate((a_ref, b_ref)):
        one_out[64 * variant : 64 * variant + 64, :] = ref[0:64, :]
        two_out[64 * variant : 64 * variant + 64, :] = ref[64:128, :]
    one = split(one_out[...])
    two = split(two_out[...])
    nt = ((1,), (1,))
    upper = dot_split(one, split(turn[128:256, :]), nt)
    side = dot_split(two, split(turn[0:128, :]), nt)
    lower = dot_split(two, split(turn[256:384, :]), nt)
    lower = lower - dot_split(split(side), split(par[...]), nt)
    i = lax.broadcasted_iota(jnp.int32, (B, B), 0)
    j = lax.broadcasted_iota(jnp.int32, (B, B), 1)
    both = jnp.where(i >= j, upper, lower)
    middle = jnp.sum(jnp.where(i == j, lower, 0.0), axis=0, keepdims=True)
    for half in range(2):
        sums[half, 0:64, :] = both[64 * half : 64 * half + 64]
        sums[half, 64:128, :] = side[64 * half : 64 * half + 64]
        sums[half, 128:136, :] = jnp.broadcast_to(middle, (8, B))
    keep_out[...] = sums[core]
    send_out[...] = sums[1 - core]


def blocks_of(parts, turn, par):
    return pl.pallas_call(
        block_kernel,
        out_shape=[f32(B, KA), f32(B, KA), f32(136, B), f32(136, B)],
        in_specs=[VMEM] * 4,
        out_specs=[VMEM] * 4,
        scratch_shapes=[pltpu.VMEM((2, 136, B), jnp.float32)],
        compiler_params=pltpu.CompilerParams(vmem_limit_bytes=8 * MIB),
    )(*parts, turn, par)


def add(part, kept, got, order=()):
    half = kept.shape[0] // 2

    def body(a, b, *refs):
        out = refs[-1]
        if half == 0:
            out[...] = a[0] + b[0]
        else:
            at = pl.ds(half * part, half)
            out[...] = a[at] + b[at]

    return pl.pallas_call(
        body,
        out_shape=f32(half, B, KA) if half else f32(B, KA),
        in_specs=[VMEM] * 2 + [ANY] * len(order),
        out_specs=VMEM,
        compiler_params=pltpu.CompilerParams(vmem_limit_bytes=8 * MIB),
        cost_estimate=pl.CostEstimate(flops=300_000, bytes_accessed=1_000_000, transcendentals=0),
    )(kept, got, *order)


def join_kernel(base, own, other, a_out, b_out, c_out, full):
    core = lax.rem(lax.axis_index("pcol"), 2)
    for at, ref in ((core, own), (1 - core, other)):
        rows = pl.ds(pl.multiple_of(at * 64, 64), 64)
        full[rows, :] = ref[0:64, :]
        b_out[rows, :] = base[pl.ds(pl.multiple_of(B + at * 64, 64), 64), :] - ref[64:128, :]
    i = lax.broadcasted_iota(jnp.int32, (B, B), 0)
    j = lax.broadcasted_iota(jnp.int32, (B, B), 1)
    both = full[...]
    turned = both.T
    middle = jnp.broadcast_to(own[128:129, :], (B, B))
    a_out[...] = base[0:128, :] - jnp.where(i >= j, both, turned)
    lower = jnp.where(i == j, middle, jnp.where(i < j, both, turned))
    c_out[...] = base[256:384, :] - lower


def join(base, own, other):
    return pl.pallas_call(
        join_kernel,
        out_shape=[f32(B, B)] * 3,
        in_specs=[VMEM] * 3,
        out_specs=[VMEM] * 3,
        scratch_shapes=[pltpu.VMEM((B, B), jnp.float32)],
        compiler_params=pltpu.CompilerParams(vmem_limit_bytes=4 * MIB),
    )(base, own, other)


def local(
    ginv_anc,
    factor_one,
    pattern_one,
    dinv_one,
    factor_two,
    factor_parent,
    pattern_two,
    parent,
    dinv_two,
):
    own = prepare(pattern_one.T, pattern_two.T, factor_one, factor_two, factor_parent)
    blocks_own = gather(stage(own), 3)
    blocks_other = gather(swap(own), 4)
    turn = pick_turn(parent, blocks_own, blocks_other)
    send_a, send_b, one, two = send_half(parent, ginv_anc, turn, blocks_own, blocks_other)
    turn = permute(turn, lambda r, c: (r ^ spread_mask(c), c))
    got = [row_step(send_a, 0, 0), row_step(send_b, 1, 0)]
    keep_a, keep_b, par, base = keep_half(
        parent, ginv_anc, one, two, dinv_one, dinv_two, [turn]
    )
    kept = [keep_a, keep_b]
    turn = permute(turn, lambda r, c: (r, r ^ spread_mask(c)))
    for step in range(1, 4):
        order = [turn] if step == 3 else []
        going = [add(1, kept[0], got[0]), add(1, kept[1], got[1], order)]
        kept = [add(0, kept[v], got[v]) for v in range(2)]
        got = [row_step(going[v], v, step) for v in range(2)]
    kept = [add(0, kept[v], got[v]) for v in range(2)]
    anc_one, anc_two, send, keep = blocks_of(kept, turn, par)
    sums = keep + swap(send)
    for mask in (2, 6, 14):
        sums = sums + permute(sums, lambda r, c: (r, c ^ mask))
    diag_one, cross, diag_two = join(base, sums, swap(sums))
    return anc_one, diag_one, anc_two, cross, diag_two


def solution(mesh):
    return jax.shard_map(
        local,
        mesh=mesh,
        in_specs=(
            P("prow", "pcol"),
            P("prow", "pcol"),
            P(),
            P(),
            P("prow", "pcol"),
            P(None, "pcol"),
            P(),
            P(),
            P("prow", None),
        ),
        out_specs=(
            P("prow", "pcol"),
            P("prow", None),
            P("prow", "pcol"),
            P("prow", None),
            P("prow", None),
        ),
        check_vma=False,
    )
```

```python
import jax
import jax.numpy as jnp
from jax import lax
from jax.experimental import pallas as pl
from jax.experimental.pallas import tpu as pltpu
from jax.sharding import PartitionSpec as P

N = 16
B = 128
KA = 512
ALL = ("prow", "pcol")
MASKS = (((1, 3, 4, 12), (3, 1, 12, 4)), ((4, 12, 1, 3), (12, 4, 3, 1)))
SPREAD = (1, 6, 2)
VMEM = pl.BlockSpec(memory_space=pltpu.VMEM)
SMEM = pl.BlockSpec(memory_space=pltpu.SMEM)
ANY = pl.BlockSpec(memory_space=pl.ANY)
HBM = pl.BlockSpec(memory_space=pltpu.HBM)
MIB = 1024 * 1024


def f32(*shape):
    return jax.ShapeDtypeStruct(shape, jnp.float32)


def slot_mask(core, variant, slot):
    mask = 0
    for bit in range(4):
        if (slot >> (3 - bit)) & 1:
            mask ^= MASKS[core][variant][bit]
    return mask


def destination(row, core, variant, slot):
    first, second = slot_mask(0, variant, slot), slot_mask(1, variant, slot)
    return row ^ jnp.where(core == 0, first, second)


def split(value):
    high = value.astype(jnp.bfloat16)
    low = (value - high.astype(jnp.float32)).astype(jnp.bfloat16)
    return high, low


def dot_split(left, right, dims):
    out = None
    for a, b in ((left[0], right[0]), (left[0], right[1]), (left[1], right[0])):
        term = lax.dot_general(a, b, (dims, ((), ())), preferred_element_type=jnp.float32)
        out = term if out is None else out + term
    return out


def unpack(packed):
    return jnp.concatenate([packed[:, B * i : B * i + B] for i in range(4)], axis=0)


def permute(value, move):
    pairs = []
    for r in range(N):
        for c in range(N):
            nr, nc = move(r, c)
            pairs.append((r * N + c, nr * N + nc))
    return lax.ppermute(value, ALL, pairs)


def swap(value):
    return permute(value, lambda r, c: (r, c ^ 1))


def ring(value):
    return permute(value, lambda r, c: (r, (c + (2 if c % 2 == 0 else -2)) % N))


def spread_mask(col):
    mask = 10 if col % 2 else 0
    for bit, part in enumerate(SPREAD):
        if ((col // 2) >> bit) & 1:
            mask ^= part
    return mask


def prep_kernel(pat_one, pat_two, fac_one, fac_two, par, own, pat, fac, par_in, sems):
    row, col = lax.axis_index("prow"), lax.axis_index("pcol")
    copies = [
        pltpu.make_async_copy(pat_one, pat.at[0], sems.at[0]),
        pltpu.make_async_copy(fac_one, fac.at[0], sems.at[1]),
        pltpu.make_async_copy(par, par_in, sems.at[2]),
        pltpu.make_async_copy(pat_two, pat.at[1], sems.at[3]),
        pltpu.make_async_copy(fac_two, fac.at[1], sems.at[4]),
    ]
    for copy in copies:
        copy.start()
    lanes = lax.broadcasted_iota(jnp.int32, (1, 64), 1)

    def turn(level, top):
        for i in range(4):
            cut = pl.ds(B * i, B)
            flags = jnp.where(lanes == 4 * row + i, pat[level, pl.ds(col, 1), :], 0)
            weight = jnp.sum(flags.astype(jnp.float32), axis=1, keepdims=True)
            own[top : top + 128, cut] = fac[level, cut, :].T * weight

    copies[0].wait()
    copies[1].wait()
    turn(0, 0)
    copies[2].wait()
    turned = par_in[...].T
    for i in range(4):
        own[128:160, B * i : B * i + B] = turned[32 * i : 32 * i + 32, :]
    copies[3].wait()
    copies[4].wait()
    turn(1, 160)


def prepare(pat_one, pat_two, fac_one, fac_two, par):
    return pl.pallas_call(
        prep_kernel,
        out_shape=f32(288, KA),
        in_specs=[HBM] * 5,
        out_specs=VMEM,
        scratch_shapes=[
            pltpu.VMEM((2, N, 64), jnp.int32),
            pltpu.VMEM((2, KA, B), jnp.float32),
            pltpu.VMEM((B, B), jnp.float32),
            pltpu.SemaphoreType.DMA((5,)),
        ],
        compiler_params=pltpu.CompilerParams(vmem_limit_bytes=56 * MIB),
    )(pat_one, pat_two, fac_one, fac_two, par)


def gather(block, steps):
    blocks = [block]
    for _ in range(steps):
        block = ring(block)
        blocks += [block, swap(block)]
    return blocks


def stage(own):
    def body(source, out, sem):
        copy = pltpu.make_async_copy(source, out, sem)
        copy.start()
        copy.wait()

    return pl.pallas_call(
        body,
        out_shape=f32(288, KA),
        in_specs=[ANY],
        out_specs=VMEM,
        scratch_shapes=[pltpu.SemaphoreType.DMA],
        compiler_params=pltpu.CompilerParams(vmem_limit_bytes=4 * MIB),
        cost_estimate=pl.CostEstimate(flops=1000, bytes_accessed=1000, transcendentals=0),
    )(own)


def place():
    row, col = lax.axis_index("prow"), lax.axis_index("pcol")
    core = lax.rem(col, 2)
    z = lax.div(col, 2)
    target = row ^ (core * 10)
    for bit, mask in enumerate(SPREAD):
        target = target ^ (lax.rem(lax.shift_right_logical(z, bit), 2) * mask)
    return row, col, core, target


def sources(own, other, start, rows):
    col = lax.axis_index("pcol")
    z, core = lax.div(col, 2), lax.rem(col, 2)
    found = []
    for sibling, refs in enumerate((own, other)):
        for at, ref in enumerate(refs):
            step = (at + 1) // 2
            swapped = at > 0 and at % 2 == 0
            side = (1 - core) if swapped else core
            away = jnp.where(side == 0, 8 - step, step)
            plane = lax.rem(z + away, 8)
            parity = (1 - side) if sibling else side
            found.append((ref.at[pl.ds(start, rows)], plane * 2 + parity))
    return found


def fetch(own, other, start, rows, target, sems, first):
    return [
        pltpu.make_async_copy(source, target.at[m], sems.at[first + k])
        for k, (source, m) in enumerate(sources(own, other, start, rows))
    ]


def turn_kernel(parent, *refs):
    own, other, turn, sems = refs[:9], refs[9:16], refs[16], refs[17]
    row, col, core, target = place()
    for k, (start_row, which) in enumerate(((0, parent[target]), (0, target), (160, target))):
        for source, m in sources(own, other, start_row, B):

            @pl.when(m == which)
            def start():
                pltpu.make_async_copy(source, turn.at[pl.ds(B * k, B)], sems.at[k]).start()

    for k in range(3):
        part = turn.at[pl.ds(B * k, B)]
        pltpu.make_async_copy(part, part, sems.at[k]).wait()


def pick_turn(parent, own, other):
    return pl.pallas_call(
        turn_kernel,
        out_shape=f32(384, KA),
        in_specs=[SMEM] + [ANY] * 16,
        out_specs=VMEM,
        scratch_shapes=[pltpu.SemaphoreType.DMA((3,))],
        compiler_params=pltpu.CompilerParams(vmem_limit_bytes=4 * MIB),
        cost_estimate=pl.CostEstimate(flops=1000, bytes_accessed=1000, transcendentals=0),
    )(parent, *own, *other)


def products(ginv, level, at, row, core, half, left, outs):
    for variant in range(2):
        rows = pl.ds(64 * variant, 64)
        for slot in range(8):
            dest = destination(row, core, variant, slot + 8 * half)
            left[64 * slot : 64 * slot + 64, :] = level[dest, rows, :]
        value = dot_split(split(left[...]), ginv, ((1,), (0,)))
        outs[variant][:, 64 * at : 64 * at + 64, :] = -value.reshape(8, 64, KA)


def send_kernel(parent, ginv, turn, *refs):
    own, other, refs = refs[:9], refs[9:16], refs[16:]
    sends, one, two, left, block, sems = refs[0:2], *refs[2:]
    row, col, core, target = place()
    load = pltpu.make_async_copy(ginv, block, sems.at[32])
    low = fetch(own, other, 0, 160, one, sems, 0)
    high = fetch(own, other, 160, B, two, sems, 16)
    for copy in [load] + low + high:
        copy.start()
    load.wait()
    ginv = split(block[...])
    for copy in low:
        copy.wait()
    products(ginv, one, 0, row, core, 1, left, sends)
    for copy in high:
        copy.wait()
    for m in range(16):
        par = split(unpack(one[m, 128:160, :]))
        two[m] = two[m] - dot_split(par, split(one[parent[m], 0:128, :]), ((1,), (0,)))
    products(ginv, two, 1, row, core, 1, left, sends)


def send_half(parent, ginv, turn, first, second):
    return pl.pallas_call(
        send_kernel,
        out_shape=[f32(8, B, KA)] * 2 + [f32(16, 160, KA), f32(16, B, KA)],
        in_specs=[SMEM, HBM] + [ANY] * 17,
        out_specs=[VMEM] * 4,
        scratch_shapes=[
            pltpu.VMEM((512, KA), jnp.float32),
            pltpu.VMEM((512, KA), jnp.float32),
            pltpu.SemaphoreType.DMA((33,)),
        ],
        compiler_params=pltpu.CompilerParams(vmem_limit_bytes=8 * MIB),
        cost_estimate=pl.CostEstimate(
            flops=20_000_000_000, bytes_accessed=1_000_000, transcendentals=0
        ),
    )(parent, ginv, turn, *first, *second)


def keep_half(parent, ginv, one, two, dinv_one, dinv_two, order):
    def body(parent, ginv, one, two, dinv_one, dinv_two, *refs):
        outs, refs = refs[len(order) : len(order) + 2], refs[len(order) + 2 :]
        par_out, base, left, dinv, sems = refs
        row, col, core, target = place()
        base_parts(parent, one, dinv_one, dinv_two, par_out, base, dinv, sems, row, core)
        ginv = split(ginv[...])
        products(ginv, one, 0, row, core, 0, left, outs)
        products(ginv, two, 1, row, core, 0, left, outs)

    return pl.pallas_call(
        body,
        out_shape=[f32(8, B, KA)] * 2 + [f32(B, B), f32(384, B)],
        in_specs=[SMEM] + [VMEM] * 3 + [HBM] * 2 + [ANY] * len(order),
        out_specs=[VMEM] * 4,
        scratch_shapes=[
            pltpu.VMEM((512, KA), jnp.float32),
            pltpu.VMEM((3, B, B), jnp.float32),
            pltpu.SemaphoreType.DMA((3,)),
        ],
        compiler_params=pltpu.CompilerParams(vmem_limit_bytes=8 * MIB),
        cost_estimate=pl.CostEstimate(
            flops=60_000_000_000, bytes_accessed=1_000_000, transcendentals=0
        ),
    )(parent, ginv, one, two, dinv_one, dinv_two, *order)


def base_parts(parent, one, dinv_one, dinv_two, par_out, base, dinv, sems, row, core):
    sources = (
        dinv_one.at[pl.ds(pl.multiple_of(row * B, B), B)],
        dinv_one.at[pl.ds(pl.multiple_of(parent[row] * B, B), B)],
        dinv_two,
    )
    copies = [
        pltpu.make_async_copy(source, dinv.at[i], sems.at[i]) for i, source in enumerate(sources)
    ]
    for copy in copies:
        copy.start()
    par_out[...] = unpack(one[row, 128:160, :])
    for copy in copies:
        copy.wait()
    base[0:128, :] = dinv[0]
    side = -jnp.dot(
        par_out[...],
        dinv[1],
        precision=lax.Precision.HIGHEST,
        preferred_element_type=jnp.float32,
    )
    base[128:256, :] = side
    base[256:384, :] = dinv[2] - lax.dot_general(
        side,
        par_out[...],
        (((1,), (1,)), ((), ())),
        precision=lax.Precision.HIGHEST,
        preferred_element_type=jnp.float32,
    )


def row_step(value, variant, step):
    return permute(value, lambda r, c: (r ^ MASKS[c % 2][variant][step], c))


def block_kernel(a_ref, b_ref, turn, par, one_out, two_out, send_out, keep_out, sums):
    core = lax.rem(lax.axis_index("pcol"), 2)
    for variant, ref in enumerate((a_ref, b_ref)):
        one_out[64 * variant : 64 * variant + 64, :] = ref[0:64, :]
        two_out[64 * variant : 64 * variant + 64, :] = ref[64:128, :]
    one = split(one_out[...])
    two = split(two_out[...])
    nt = ((1,), (1,))
    upper = dot_split(one, split(turn[128:256, :]), nt)
    side = dot_split(two, split(turn[0:128, :]), nt)
    lower = dot_split(two, split(turn[256:384, :]), nt)
    lower = lower - dot_split(split(side), split(par[...]), nt)
    i = lax.broadcasted_iota(jnp.int32, (B, B), 0)
    j = lax.broadcasted_iota(jnp.int32, (B, B), 1)
    both = jnp.where(i >= j, upper, lower)
    middle = jnp.sum(jnp.where(i == j, lower, 0.0), axis=0, keepdims=True)
    for half in range(2):
        sums[half, 0:64, :] = both[64 * half : 64 * half + 64]
        sums[half, 64:128, :] = side[64 * half : 64 * half + 64]
        sums[half, 128:136, :] = jnp.broadcast_to(middle, (8, B))
    keep_out[...] = sums[core]
    send_out[...] = sums[1 - core]


def blocks_of(parts, turn, par):
    return pl.pallas_call(
        block_kernel,
        out_shape=[f32(B, KA), f32(B, KA), f32(136, B), f32(136, B)],
        in_specs=[VMEM] * 4,
        out_specs=[VMEM] * 4,
        scratch_shapes=[pltpu.VMEM((2, 136, B), jnp.float32)],
        compiler_params=pltpu.CompilerParams(vmem_limit_bytes=8 * MIB),
    )(*parts, turn, par)


def add(part, kept, got, order=()):
    half = kept.shape[0] // 2

    def body(a, b, *refs):
        out = refs[-1]
        if half == 0:
            out[...] = a[0] + b[0]
        else:
            at = pl.ds(half * part, half)
            out[...] = a[at] + b[at]

    return pl.pallas_call(
        body,
        out_shape=f32(half, B, KA) if half else f32(B, KA),
        in_specs=[VMEM] * 2 + [ANY] * len(order),
        out_specs=VMEM,
        compiler_params=pltpu.CompilerParams(vmem_limit_bytes=8 * MIB),
        cost_estimate=pl.CostEstimate(flops=300_000, bytes_accessed=1_000_000, transcendentals=0),
    )(kept, got, *order)


def join_kernel(base, own, other, a_out, b_out, c_out, full):
    core = lax.rem(lax.axis_index("pcol"), 2)
    for at, ref in ((core, own), (1 - core, other)):
        rows = pl.ds(pl.multiple_of(at * 64, 64), 64)
        full[rows, :] = ref[0:64, :]
        b_out[rows, :] = base[pl.ds(pl.multiple_of(B + at * 64, 64), 64), :] - ref[64:128, :]
    i = lax.broadcasted_iota(jnp.int32, (B, B), 0)
    j = lax.broadcasted_iota(jnp.int32, (B, B), 1)
    both = full[...]
    turned = both.T
    middle = jnp.broadcast_to(own[128:129, :], (B, B))
    a_out[...] = base[0:128, :] - jnp.where(i >= j, both, turned)
    lower = jnp.where(i == j, middle, jnp.where(i < j, both, turned))
    c_out[...] = base[256:384, :] - lower


def join(base, own, other):
    return pl.pallas_call(
        join_kernel,
        out_shape=[f32(B, B)] * 3,
        in_specs=[VMEM] * 3,
        out_specs=[VMEM] * 3,
        scratch_shapes=[pltpu.VMEM((B, B), jnp.float32)],
        compiler_params=pltpu.CompilerParams(vmem_limit_bytes=4 * MIB),
    )(base, own, other)


def local(
    ginv_anc,
    factor_one,
    pattern_one,
    dinv_one,
    factor_two,
    factor_parent,
    pattern_two,
    parent,
    dinv_two,
):
    own = prepare(pattern_one.T, pattern_two.T, factor_one, factor_two, factor_parent)
    near = stage(own)
    blocks_own = [near] + gather(own, 4)[1:]
    blocks_other = gather(swap(near), 3)
    turn = pick_turn(parent, blocks_own, blocks_other)
    send_a, send_b, one, two = send_half(parent, ginv_anc, turn, blocks_own, blocks_other)
    turn = permute(turn, lambda r, c: (r ^ spread_mask(c), c))
    got = [row_step(send_a, 0, 0), row_step(send_b, 1, 0)]
    keep_a, keep_b, par, base = keep_half(
        parent, ginv_anc, one, two, dinv_one, dinv_two, [turn]
    )
    kept = [keep_a, keep_b]
    turn = permute(turn, lambda r, c: (r, r ^ spread_mask(c)))
    for step in range(1, 4):
        order = [turn] if step == 3 else []
        going = [add(1, kept[0], got[0]), add(1, kept[1], got[1], order)]
        kept = [add(0, kept[v], got[v]) for v in range(2)]
        got = [row_step(going[v], v, step) for v in range(2)]
    kept = [add(0, kept[v], got[v]) for v in range(2)]
    anc_one, anc_two, send, keep = blocks_of(kept, turn, par)
    sums = keep + swap(send)
    for mask in (2, 6, 14):
        sums = sums + permute(sums, lambda r, c: (r, c ^ mask))
    diag_one, cross, diag_two = join(base, sums, swap(sums))
    return anc_one, diag_one, anc_two, cross, diag_two


def solution(mesh):
    return jax.shard_map(
        local,
        mesh=mesh,
        in_specs=(
            P("prow", "pcol"),
            P("prow", "pcol"),
            P(),
            P(),
            P("prow", "pcol"),
            P(None, "pcol"),
            P(),
            P(),
            P("prow", None),
        ),
        out_specs=(
            P("prow", "pcol"),
            P("prow", None),
            P("prow", "pcol"),
            P("prow", None),
            P("prow", None),
        ),
        check_vma=False,
    )
```

```python
import jax
import jax.numpy as jnp
from jax import lax
from jax.experimental import pallas as pl
from jax.experimental.pallas import tpu as pltpu
from jax.sharding import PartitionSpec as P

N = 16
B = 128
KA = 512
ALL = ("prow", "pcol")
MASKS = (((1, 3, 4, 12), (3, 1, 12, 4)), ((4, 12, 1, 3), (12, 4, 3, 1)))
SPREAD = (1, 6, 2)
VMEM = pl.BlockSpec(memory_space=pltpu.VMEM)
SMEM = pl.BlockSpec(memory_space=pltpu.SMEM)
ANY = pl.BlockSpec(memory_space=pl.ANY)
HBM = pl.BlockSpec(memory_space=pltpu.HBM)
MIB = 1024 * 1024


def f32(*shape):
    return jax.ShapeDtypeStruct(shape, jnp.float32)


def slot_mask(core, variant, slot):
    mask = 0
    for bit in range(4):
        if (slot >> (3 - bit)) & 1:
            mask ^= MASKS[core][variant][bit]
    return mask


def destination(row, core, variant, slot):
    first, second = slot_mask(0, variant, slot), slot_mask(1, variant, slot)
    return row ^ jnp.where(core == 0, first, second)


def split(value):
    high = value.astype(jnp.bfloat16)
    low = (value - high.astype(jnp.float32)).astype(jnp.bfloat16)
    return high, low


def dot_split(left, right, dims):
    out = None
    for a, b in ((left[0], right[0]), (left[0], right[1]), (left[1], right[0])):
        term = lax.dot_general(a, b, (dims, ((), ())), preferred_element_type=jnp.float32)
        out = term if out is None else out + term
    return out


def unpack(packed):
    return jnp.concatenate([packed[:, B * i : B * i + B] for i in range(4)], axis=0)


def permute(value, move):
    pairs = []
    for r in range(N):
        for c in range(N):
            nr, nc = move(r, c)
            pairs.append((r * N + c, nr * N + nc))
    return lax.ppermute(value, ALL, pairs)


def swap(value):
    return permute(value, lambda r, c: (r, c ^ 1))


def ring(value):
    return permute(value, lambda r, c: (r, (c + (2 if c % 2 == 0 else -2)) % N))


def spread_mask(col):
    mask = 10 if col % 2 else 0
    for bit, part in enumerate(SPREAD):
        if ((col // 2) >> bit) & 1:
            mask ^= part
    return mask


def prep_kernel(pat_one, pat_two, fac_one, fac_two, par, own, pat, fac, par_in, sems):
    row, col = lax.axis_index("prow"), lax.axis_index("pcol")
    copies = [
        pltpu.make_async_copy(pat_one, pat.at[0], sems.at[0]),
        pltpu.make_async_copy(fac_one, fac.at[0], sems.at[1]),
        pltpu.make_async_copy(par, par_in, sems.at[2]),
        pltpu.make_async_copy(pat_two, pat.at[1], sems.at[3]),
        pltpu.make_async_copy(fac_two, fac.at[1], sems.at[4]),
    ]
    for copy in copies:
        copy.start()
    lanes = lax.broadcasted_iota(jnp.int32, (1, 64), 1)

    def turn(level, top):
        for i in range(4):
            cut = pl.ds(B * i, B)
            flags = jnp.where(lanes == 4 * row + i, pat[level, pl.ds(col, 1), :], 0)
            weight = jnp.sum(flags.astype(jnp.float32), axis=1, keepdims=True)
            own[top : top + 128, cut] = fac[level, cut, :].T * weight

    copies[0].wait()
    copies[1].wait()
    turn(0, 0)
    copies[2].wait()
    turned = par_in[...].T
    for i in range(4):
        own[128:160, B * i : B * i + B] = turned[32 * i : 32 * i + 32, :]
    copies[3].wait()
    copies[4].wait()
    turn(1, 160)


def prepare(pat_one, pat_two, fac_one, fac_two, par):
    return pl.pallas_call(
        prep_kernel,
        out_shape=f32(288, KA),
        in_specs=[HBM] * 5,
        out_specs=VMEM,
        scratch_shapes=[
            pltpu.VMEM((2, N, 64), jnp.int32),
            pltpu.VMEM((2, KA, B), jnp.float32),
            pltpu.VMEM((B, B), jnp.float32),
            pltpu.SemaphoreType.DMA((5,)),
        ],
        compiler_params=pltpu.CompilerParams(vmem_limit_bytes=56 * MIB),
    )(pat_one, pat_two, fac_one, fac_two, par)


def gather(block, steps):
    blocks = [block]
    for _ in range(steps):
        block = ring(block)
        blocks += [block, swap(block)]
    return blocks


def stage(own):
    def body(source, out, sem):
        copy = pltpu.make_async_copy(source, out, sem)
        copy.start()
        copy.wait()

    return pl.pallas_call(
        body,
        out_shape=f32(288, KA),
        in_specs=[ANY],
        out_specs=VMEM,
        scratch_shapes=[pltpu.SemaphoreType.DMA],
        compiler_params=pltpu.CompilerParams(vmem_limit_bytes=4 * MIB),
        cost_estimate=pl.CostEstimate(flops=1000, bytes_accessed=1000, transcendentals=0),
    )(own)


def place():
    row, col = lax.axis_index("prow"), lax.axis_index("pcol")
    core = lax.rem(col, 2)
    z = lax.div(col, 2)
    target = row ^ (core * 10)
    for bit, mask in enumerate(SPREAD):
        target = target ^ (lax.rem(lax.shift_right_logical(z, bit), 2) * mask)
    return row, col, core, target


def sources(own, other, start, rows):
    col = lax.axis_index("pcol")
    z, core = lax.div(col, 2), lax.rem(col, 2)
    found = []
    for sibling, refs in enumerate((own, other)):
        for at, ref in enumerate(refs):
            step = (at + 1) // 2
            swapped = at > 0 and at % 2 == 0
            side = (1 - core) if swapped else core
            away = jnp.where(side == 0, 8 - step, step)
            plane = lax.rem(z + away, 8)
            parity = (1 - side) if sibling else side
            found.append((ref.at[pl.ds(start, rows)], plane * 2 + parity))
    return found


def fetch(own, other, start, rows, target, sems, first):
    return [
        pltpu.make_async_copy(source, target.at[m], sems.at[first + k])
        for k, (source, m) in enumerate(sources(own, other, start, rows))
    ]


def turn_kernel(parent, *refs):
    own, other, turn, sems = refs[:9], refs[9:16], refs[16], refs[17]
    row, col, core, target = place()
    for k, (start_row, which) in enumerate(((0, parent[target]), (0, target), (160, target))):
        for source, m in sources(own, other, start_row, B):

            @pl.when(m == which)
            def start():
                pltpu.make_async_copy(source, turn.at[pl.ds(B * k, B)], sems.at[k]).start()

    for k in range(3):
        part = turn.at[pl.ds(B * k, B)]
        pltpu.make_async_copy(part, part, sems.at[k]).wait()


def pick_turn(parent, own, other):
    return pl.pallas_call(
        turn_kernel,
        out_shape=f32(384, KA),
        in_specs=[SMEM] + [ANY] * 16,
        out_specs=VMEM,
        scratch_shapes=[pltpu.SemaphoreType.DMA((3,))],
        compiler_params=pltpu.CompilerParams(vmem_limit_bytes=4 * MIB),
        cost_estimate=pl.CostEstimate(flops=1000, bytes_accessed=1000, transcendentals=0),
    )(parent, *own, *other)


def products(ginv, level, at, row, core, half, left, outs):
    for variant in range(2):
        rows = pl.ds(64 * variant, 64)
        for slot in range(8):
            dest = destination(row, core, variant, slot + 8 * half)
            left[64 * slot : 64 * slot + 64, :] = level[dest, rows, :]
        value = dot_split(split(left[...]), ginv, ((1,), (0,)))
        outs[variant][:, 64 * at : 64 * at + 64, :] = -value.reshape(8, 64, KA)


def send_kernel(parent, ginv, turn, *refs):
    own, other, refs = refs[:9], refs[9:16], refs[16:]
    sends, one, two, left, block, sems = refs[0:2], *refs[2:]
    row, col, core, target = place()
    load = pltpu.make_async_copy(ginv, block, sems.at[32])
    low = fetch(own, other, 0, 160, one, sems, 0)
    high = fetch(own, other, 160, B, two, sems, 16)
    for copy in [load] + low + high:
        copy.start()
    load.wait()
    ginv = split(block[...])
    for copy in low:
        copy.wait()
    products(ginv, one, 0, row, core, 1, left, sends)
    for copy in high:
        copy.wait()
    for m in range(16):
        high_par, low_par = split(unpack(one[m, 128:160, :]))
        high_one, low_one = split(one[parent[m], 0:128, :])
        two[m] = two[m] - jnp.dot(
            jnp.concatenate([high_par, low_par, high_par], axis=1),
            jnp.concatenate([high_one, high_one, low_one], axis=0),
            preferred_element_type=jnp.float32,
        )
    products(ginv, two, 1, row, core, 1, left, sends)


def send_half(parent, ginv, turn, first, second):
    return pl.pallas_call(
        send_kernel,
        out_shape=[f32(8, B, KA)] * 2 + [f32(16, 160, KA), f32(16, B, KA)],
        in_specs=[SMEM, HBM] + [ANY] * 17,
        out_specs=[VMEM] * 4,
        scratch_shapes=[
            pltpu.VMEM((512, KA), jnp.float32),
            pltpu.VMEM((512, KA), jnp.float32),
            pltpu.SemaphoreType.DMA((33,)),
        ],
        compiler_params=pltpu.CompilerParams(vmem_limit_bytes=8 * MIB),
        cost_estimate=pl.CostEstimate(
            flops=20_000_000_000, bytes_accessed=1_000_000, transcendentals=0
        ),
    )(parent, ginv, turn, *first, *second)


def keep_half(parent, ginv, one, two, dinv_one, dinv_two, order):
    def body(parent, ginv, one, two, dinv_one, dinv_two, *refs):
        outs, refs = refs[len(order) : len(order) + 2], refs[len(order) + 2 :]
        par_out, base, left, dinv, sems = refs
        row, col, core, target = place()
        base_parts(parent, one, dinv_one, dinv_two, par_out, base, dinv, sems, row, core)
        ginv = split(ginv[...])
        products(ginv, one, 0, row, core, 0, left, outs)
        products(ginv, two, 1, row, core, 0, left, outs)

    return pl.pallas_call(
        body,
        out_shape=[f32(8, B, KA)] * 2 + [f32(B, B), f32(384, B)],
        in_specs=[SMEM] + [VMEM] * 3 + [HBM] * 2 + [ANY] * len(order),
        out_specs=[VMEM] * 4,
        scratch_shapes=[
            pltpu.VMEM((512, KA), jnp.float32),
            pltpu.VMEM((3, B, B), jnp.float32),
            pltpu.SemaphoreType.DMA((3,)),
        ],
        compiler_params=pltpu.CompilerParams(vmem_limit_bytes=8 * MIB),
        cost_estimate=pl.CostEstimate(
            flops=60_000_000_000, bytes_accessed=1_000_000, transcendentals=0
        ),
    )(parent, ginv, one, two, dinv_one, dinv_two, *order)


def base_parts(parent, one, dinv_one, dinv_two, par_out, base, dinv, sems, row, core):
    sources = (
        dinv_one.at[pl.ds(pl.multiple_of(row * B, B), B)],
        dinv_one.at[pl.ds(pl.multiple_of(parent[row] * B, B), B)],
        dinv_two,
    )
    copies = [
        pltpu.make_async_copy(source, dinv.at[i], sems.at[i]) for i, source in enumerate(sources)
    ]
    for copy in copies:
        copy.start()
    par_out[...] = unpack(one[row, 128:160, :])
    for copy in copies:
        copy.wait()
    base[0:128, :] = dinv[0]
    side = -jnp.dot(
        par_out[...],
        dinv[1],
        precision=lax.Precision.HIGHEST,
        preferred_element_type=jnp.float32,
    )
    base[128:256, :] = side
    base[256:384, :] = dinv[2] - lax.dot_general(
        side,
        par_out[...],
        (((1,), (1,)), ((), ())),
        precision=lax.Precision.HIGHEST,
        preferred_element_type=jnp.float32,
    )


def row_step(value, variant, step):
    return permute(value, lambda r, c: (r ^ MASKS[c % 2][variant][step], c))


def block_kernel(a_ref, b_ref, turn, par, one_out, two_out, send_out, keep_out, sums):
    core = lax.rem(lax.axis_index("pcol"), 2)
    for variant, ref in enumerate((a_ref, b_ref)):
        one_out[64 * variant : 64 * variant + 64, :] = ref[0:64, :]
        two_out[64 * variant : 64 * variant + 64, :] = ref[64:128, :]
    one = split(one_out[...])
    two = split(two_out[...])
    nt = ((1,), (1,))
    upper = dot_split(one, split(turn[128:256, :]), nt)
    side = dot_split(two, split(turn[0:128, :]), nt)
    lower = dot_split(two, split(turn[256:384, :]), nt)
    lower = lower - dot_split(split(side), split(par[...]), nt)
    i = lax.broadcasted_iota(jnp.int32, (B, B), 0)
    j = lax.broadcasted_iota(jnp.int32, (B, B), 1)
    both = jnp.where(i >= j, upper, lower)
    middle = jnp.sum(jnp.where(i == j, lower, 0.0), axis=0, keepdims=True)
    for half in range(2):
        sums[half, 0:64, :] = both[64 * half : 64 * half + 64]
        sums[half, 64:128, :] = side[64 * half : 64 * half + 64]
        sums[half, 128:136, :] = jnp.broadcast_to(middle, (8, B))
    keep_out[...] = sums[core]
    send_out[...] = sums[1 - core]


def blocks_of(parts, turn, par):
    return pl.pallas_call(
        block_kernel,
        out_shape=[f32(B, KA), f32(B, KA), f32(136, B), f32(136, B)],
        in_specs=[VMEM] * 4,
        out_specs=[VMEM] * 4,
        scratch_shapes=[pltpu.VMEM((2, 136, B), jnp.float32)],
        compiler_params=pltpu.CompilerParams(vmem_limit_bytes=8 * MIB),
    )(*parts, turn, par)


def add(part, kept, got, order=()):
    half = kept.shape[0] // 2

    def body(a, b, *refs):
        out = refs[-1]
        if half == 0:
            out[...] = a[0] + b[0]
        else:
            at = pl.ds(half * part, half)
            out[...] = a[at] + b[at]

    return pl.pallas_call(
        body,
        out_shape=f32(half, B, KA) if half else f32(B, KA),
        in_specs=[VMEM] * 2 + [ANY] * len(order),
        out_specs=VMEM,
        compiler_params=pltpu.CompilerParams(vmem_limit_bytes=8 * MIB),
        cost_estimate=pl.CostEstimate(flops=300_000, bytes_accessed=1_000_000, transcendentals=0),
    )(kept, got, *order)


def join_kernel(base, own, other, a_out, b_out, c_out, full):
    core = lax.rem(lax.axis_index("pcol"), 2)
    for at, ref in ((core, own), (1 - core, other)):
        rows = pl.ds(pl.multiple_of(at * 64, 64), 64)
        full[rows, :] = ref[0:64, :]
        b_out[rows, :] = base[pl.ds(pl.multiple_of(B + at * 64, 64), 64), :] - ref[64:128, :]
    i = lax.broadcasted_iota(jnp.int32, (B, B), 0)
    j = lax.broadcasted_iota(jnp.int32, (B, B), 1)
    both = full[...]
    turned = both.T
    middle = jnp.broadcast_to(own[128:129, :], (B, B))
    a_out[...] = base[0:128, :] - jnp.where(i >= j, both, turned)
    lower = jnp.where(i == j, middle, jnp.where(i < j, both, turned))
    c_out[...] = base[256:384, :] - lower


def join(base, own, other):
    return pl.pallas_call(
        join_kernel,
        out_shape=[f32(B, B)] * 3,
        in_specs=[VMEM] * 3,
        out_specs=[VMEM] * 3,
        scratch_shapes=[pltpu.VMEM((B, B), jnp.float32)],
        compiler_params=pltpu.CompilerParams(vmem_limit_bytes=4 * MIB),
    )(base, own, other)


def local(
    ginv_anc,
    factor_one,
    pattern_one,
    dinv_one,
    factor_two,
    factor_parent,
    pattern_two,
    parent,
    dinv_two,
):
    own = prepare(pattern_one.T, pattern_two.T, factor_one, factor_two, factor_parent)
    near = stage(own)
    blocks_own = [near] + gather(own, 4)[1:]
    blocks_other = gather(swap(near), 3)
    turn = pick_turn(parent, blocks_own, blocks_other)
    send_a, send_b, one, two = send_half(parent, ginv_anc, turn, blocks_own, blocks_other)
    turn = permute(turn, lambda r, c: (r ^ spread_mask(c), c))
    got = [row_step(send_a, 0, 0), row_step(send_b, 1, 0)]
    keep_a, keep_b, par, base = keep_half(
        parent, ginv_anc, one, two, dinv_one, dinv_two, [turn]
    )
    kept = [keep_a, keep_b]
    turn = permute(turn, lambda r, c: (r, r ^ spread_mask(c)))
    for step in range(1, 4):
        order = [turn] if step == 3 else []
        going = [add(1, kept[0], got[0]), add(1, kept[1], got[1], order)]
        kept = [add(0, kept[v], got[v]) for v in range(2)]
        got = [row_step(going[v], v, step) for v in range(2)]
    kept = [add(0, kept[v], got[v]) for v in range(2)]
    anc_one, anc_two, send, keep = blocks_of(kept, turn, par)
    sums = keep + swap(send)
    for mask in (2, 6, 14):
        sums = sums + permute(sums, lambda r, c: (r, c ^ mask))
    diag_one, cross, diag_two = join(base, sums, swap(sums))
    return anc_one, diag_one, anc_two, cross, diag_two


def solution(mesh):
    return jax.shard_map(
        local,
        mesh=mesh,
        in_specs=(
            P("prow", "pcol"),
            P("prow", "pcol"),
            P(),
            P(),
            P("prow", "pcol"),
            P(None, "pcol"),
            P(),
            P(),
            P("prow", None),
        ),
        out_specs=(
            P("prow", "pcol"),
            P("prow", None),
            P("prow", "pcol"),
            P("prow", None),
            P("prow", None),
        ),
        check_vma=False,
    )
```
